32 devices in a mesh: row: 16 (over z, y, core), head: 2 (over x).
Axes of the slice: x: 2, y: 2, z: 4, core: 2. Of those that a mesh axis runs over, the one named last changes fastest.
Arguments:
- tokens: bfloat16 [8192, 1024], P(('row', 'head')), may hold values from -6 to 6
- segments: int32 [8192], P('row'), may hold values from 0 to 4, as said below
- routes: int32 [8192, 8], P(('row', 'head')), may hold values from 0 to 15, all different within a row
- norm_gain: float32 [1024], replicated, may hold values from 0.25 to 1.75
- w_query: bfloat16 [1024, 1024], P(None, 'head'), may hold values from -0.1875 to 0.1875
- key_weight: bfloat16 [1024, 512], P(None, 'head'), may hold values from -0.1875 to 0.1875
- value_weight: bfloat16 [1024, 512], P(None, 'head'), may hold values from -0.1875 to 0.1875
- w_output: bfloat16 [1024, 1024], P('head'), may hold values from -1.5 to 1.5
- moe_gain: float32 [1024], replicated, may hold values from 0.25 to 1.75
- w_router: bfloat16 [1024, 16], replicated, may hold values from -0.08984375 to 0.08984375
- w_gate: bfloat16 [16, 1024, 512], P('row'), may hold values from -0.1875 to 0.1875
- w_up: bfloat16 [16, 1024, 512], P('row'), may hold values from -0.1875 to 0.1875
- w_down: bfloat16 [16, 512, 1024], P('row'), may hold values from -1 to 1
- cotangent: bfloat16 [8192, 1024], P(('row', 'head')), may hold values from -6 to 6
Outputs:
- mixed_out: bfloat16 [8192, 1024], P(('row', 'head'))
- grad_tokens: float32 [8192, 1024], P(('row', 'head'))
- grad_norm_gain: float32 [1024], replicated
- grad_query: float32 [1024, 1024], P('row', 'head')
- grad_key: float32 [1024, 512], P('row', 'head')
- grad_value: float32 [1024, 512], P('row', 'head')
- grad_output: float32 [1024, 1024], P('head', 'row')
- grad_moe_gain: float32 [1024], replicated
- grad_router: float32 [1024, 16], replicated
- grad_gate: float32 [16, 1024, 512], P('row', 'head')
- grad_up: float32 [16, 1024, 512], P('row', 'head')
- grad_down: float32 [16, 512, 1024], P('row', None, 'head')
The draws below stay inside these ranges and needn't reach their ends.
Inputs may be any that keep to these rules, and one draw needn't show every extreme that they name: `segments`: in each packed row of 512 tokens the numbers never fall and all five values occur; document 2 starts within the row's first 256 positions and ends within its last 256.
All inputs are finite; a program needn't handle non-finite values.
Results may differ from the reference program's by a relative error of at most 0.014.
The reference program's roundings to bfloat16 on the way count: a program that leaves them out, or rounds other values in their place, can miss the bound.
Values may be sent and summed in bfloat16 or wider, within the bound.
No kernel may reach another device: no remote copies, remote signals or barrier semaphores. Data moves between devices by JAX's collectives and lax.ppermute only.
A program may use at most 192 MiB of HBM per device.

```python
import jax
import jax.numpy as jnp
from jax import lax

MODEL_WIDTH = 1024
QUERY_HEADS = 16
KEY_VALUE_HEADS = 8
HEAD_SIZE = 64
F = 512
TOPK = 8
TOK_DEV = 256
E = 16
PACKED_TOKENS = 512
TOKENS = 8192
CAP = 160


def draw_segments(key, part):
    key = jax.random.fold_in(key, 11)
    n_rows = TOKENS // PACKED_TOKENS
    key_one, key_two, key_three, key_four = jax.random.split(key, 4)
    opening = jax.random.randint(key_one, (n_rows, 1), 2, TOK_DEV)
    closing = jax.random.randint(key_two, (n_rows, 1), PACKED_TOKENS - TOK_DEV + 1, PACKED_TOKENS - 1)
    early_cut = jax.random.randint(key_three, (n_rows, 1), 1, opening)
    late_cut = jax.random.randint(key_four, (n_rows, 1), closing + 1, PACKED_TOKENS)
    positions = jnp.arange(PACKED_TOKENS, dtype=jnp.int32)[None, :]
    numbers = (positions >= early_cut).astype(jnp.int32) + (positions >= opening).astype(jnp.int32)
    numbers = numbers + (positions >= closing).astype(jnp.int32) + (positions >= late_cut).astype(jnp.int32)
    return numbers.reshape(TOKENS).astype(jnp.int32)


def level_of(stream_key, dims, pieces, smallest, largest):
    def one(dim, shards_of):
        draws = jax.random.uniform(jax.random.fold_in(jax.random.fold_in(stream_key, 6), dim), (shards_of,), jnp.float32, smallest / len(pieces), largest / len(pieces))
        return jnp.repeat(jnp.exp(draws), dims[dim] // shards_of).reshape((-1,) + (1,) * (len(dims) - dim - 1))

    factor_of = one(*pieces[0])
    for cut in pieces[1:]:
        factor_of = factor_of * one(*cut)
    return factor_of


def choose_distinct(stream_key, rows, number_of, top, lift):
    order = jax.random.permutation(jax.random.fold_in(stream_key, 1), number_of)
    favour = order
    for power in range(3):
        favour = favour * favour // number_of
    favour = favour * lift // number_of
    chance = jax.random.randint(jax.random.fold_in(stream_key, 2), (rows, number_of), 0, 4096) + favour
    sure = jax.random.permutation(jax.random.fold_in(stream_key, 3), rows)[jnp.arange(number_of) % rows]
    chance = jnp.where(jnp.arange(rows)[:, None] == sure[None, :], 1 << 14, chance)
    score = chance * number_of + jnp.arange(number_of)
    return lax.top_k(score.astype(jnp.int32), top)[1].astype(jnp.int32)


def gaussian(stream_key, dims, scale, most, pieces=(), kind=jnp.bfloat16):
    loudness = level_of(stream_key, dims, pieces, -0.22, 0.18) if pieces else 1.0
    drawn = jax.random.normal(stream_key, dims, jnp.float32) * scale * loudness
    return jnp.minimum(jnp.maximum(drawn, -most), most).astype(kind)


def setup_inputs(seed: int = 0) -> dict:
    key_list = jax.random.split(jax.random.key(seed), 15)
    return {
        "tokens": gaussian(key_list[0], (TOKENS, MODEL_WIDTH), 1.0, 6.0, ((0, 32),)),
        "segments": draw_segments(jax.random.fold_in(key_list[14], 71), 0),
        "routes": choose_distinct(key_list[2], TOKENS, E, TOPK, 8192),
        "norm_gain": jnp.clip(1.0 + 0.15 * jax.random.normal(key_list[3], (MODEL_WIDTH,), jnp.float32), 0.25, 1.75),
        "w_query": gaussian(key_list[4], (MODEL_WIDTH, QUERY_HEADS * HEAD_SIZE), MODEL_WIDTH ** -0.5, 0.1875, ((1, 2),)),
        "key_weight": gaussian(key_list[5], (MODEL_WIDTH, KEY_VALUE_HEADS * HEAD_SIZE), MODEL_WIDTH ** -0.5, 0.1875, ((1, 2),)),
        "value_weight": gaussian(key_list[6], (MODEL_WIDTH, KEY_VALUE_HEADS * HEAD_SIZE), MODEL_WIDTH ** -0.5, 0.1875, ((1, 2),)),
        "w_output": gaussian(key_list[7], (QUERY_HEADS * HEAD_SIZE, MODEL_WIDTH), 16 ** -0.5, 1.5, ((0, 2),)),
        "moe_gain": jnp.clip(1.0 + 0.15 * jax.random.normal(key_list[8], (MODEL_WIDTH,), jnp.float32), 0.25, 1.75),
        "w_router": gaussian(key_list[9], (MODEL_WIDTH, E), 0.0156, 0.08984375),
        "w_gate": gaussian(key_list[10], (E, MODEL_WIDTH, F), MODEL_WIDTH ** -0.5, 0.1875, ((0, 16),)),
        "w_up": gaussian(key_list[11], (E, MODEL_WIDTH, F), MODEL_WIDTH ** -0.5, 0.1875, ((0, 16),)),
        "w_down": gaussian(key_list[12], (E, F, MODEL_WIDTH), (F // 16) ** -0.5, 1.0, ((0, 16),)),
        "cotangent": gaussian(key_list[13], (TOKENS, MODEL_WIDTH), 1.0, 6.0, ((0, 32),)),
    }


@jax.custom_vjp
def low(v):
    return lax.optimization_barrier(v.astype(jnp.bfloat16)).astype(jnp.float32)

@jax.custom_vjp
def low_back(v):
    return v

def low_keep(v):
    return (low(v), None)

def low_pass(kept, grad):
    return (grad,)

def back_keep(v):
    return (v, None)

def back_low(kept, grad):
    return (low(grad),)
low.defvjp(low_keep, low_pass)
low_back.defvjp(back_keep, back_low)
EPSILON = 1e-06
ROPE_BASE = 10000.0
TOP_PRECISION = lax.Precision.HIGHEST

def rms_norm(values, gain):
    factor = lax.rsqrt(lax.optimization_barrier(jnp.mean(values * values, axis=-1, keepdims=True)) + EPSILON)
    return values * factor * gain

def rotate(values, positions):
    halfway = values.shape[-1] // 2
    frequency = ROPE_BASE ** (-2.0 * jnp.arange(halfway, dtype=jnp.float32) / values.shape[-1])
    angles = positions.astype(jnp.float32)[:, None] * frequency[None, :]
    cosine = jnp.cos(angles)[:, None, :]
    sine_part = jnp.sin(angles)[:, None, :]
    first_half = values[..., :halfway]
    second = values[..., halfway:]
    return jnp.concatenate([first_half * cosine - second * sine_part, second * cosine + first_half * sine_part], axis=-1)

def slot_table(routes, n_experts, block_rows, capacity):
    one_hot = (routes[:, :, None] == jnp.arange(n_experts, dtype=jnp.int32)[None, None, :]).astype(jnp.int32)
    counted = lax.optimization_barrier(jnp.sum(one_hot, axis=1)).astype(jnp.int32)
    grouped = counted.reshape(-1, block_rows, n_experts)
    earlier = (jnp.cumsum(grouped, axis=1).astype(jnp.int32) - grouped).reshape(-1, n_experts)
    ranking = lax.optimization_barrier(jnp.sum(one_hot * earlier[:, None, :], axis=2)).astype(jnp.int32)
    kept_mask = ranking < capacity
    slot_index = jnp.where(kept_mask, routes * capacity + ranking, n_experts * capacity)
    return (slot_index.astype(jnp.int32), kept_mask)

def layer_row(x_row, seg_row, slot_row, kept_row, route_row, norm_g, query_w, key_matrix, value_matrix, output_w, moe_g, router_w, gate_w, up_w, down_w):
    positions = jnp.arange(PACKED_TOKENS, dtype=jnp.int32)
    normed_input = low(rms_norm(x_row, norm_g))
    queries = jnp.dot(normed_input, query_w, precision=TOP_PRECISION).reshape(PACKED_TOKENS, QUERY_HEADS, HEAD_SIZE)
    keys_linear = jnp.dot(normed_input, key_matrix, precision=TOP_PRECISION).reshape(PACKED_TOKENS, KEY_VALUE_HEADS, HEAD_SIZE)
    values_linear = jnp.dot(normed_input, value_matrix, precision=TOP_PRECISION).reshape(PACKED_TOKENS, KEY_VALUE_HEADS, HEAD_SIZE)
    queries = low(rotate(low_back(queries), positions))
    keys_rot = low(rotate(low_back(keys_linear), positions))
    values_low = low(low_back(values_linear))
    heads_per_group = QUERY_HEADS // KEY_VALUE_HEADS
    keys_wide = jnp.repeat(keys_rot, heads_per_group, axis=1)
    values_wide = jnp.repeat(values_low, heads_per_group, axis=1)
    scores = low_back(jnp.einsum('qhd,khd->hqk', queries, keys_wide, precision=TOP_PRECISION) * HEAD_SIZE ** (-0.5))
    allowed = (seg_row[:, None] == seg_row[None, :]) & (positions[None, :] <= positions[:, None])
    scores = jnp.where(allowed[None], scores, -1e+30)
    probabilities = low(jax.nn.softmax(scores, axis=-1))
    mixed_heads = jnp.einsum('hqk,khd->qhd', probabilities, values_wide, precision=TOP_PRECISION).reshape(PACKED_TOKENS, QUERY_HEADS * HEAD_SIZE)
    mixed_heads = low_back(low(mixed_heads))
    hidden = x_row + low_back(jnp.dot(mixed_heads, output_w, precision=TOP_PRECISION))
    normed_moe = low(rms_norm(hidden, moe_g))
    logits = jnp.dot(normed_moe, router_w, precision=TOP_PRECISION)
    gate_values = jax.nn.softmax(jnp.take_along_axis(logits, route_row, axis=1), axis=-1)
    blocks = PACKED_TOKENS // TOK_DEV
    slot_rows = slot_row.reshape(blocks, TOK_DEV * TOPK)
    which_block = jnp.broadcast_to(jnp.arange(blocks, dtype=jnp.int32)[:, None], slot_rows.shape)
    spread = jnp.broadcast_to(normed_moe.reshape(blocks, TOK_DEV, 1, MODEL_WIDTH), (blocks, TOK_DEV, TOPK, MODEL_WIDTH)).reshape(blocks, TOK_DEV * TOPK, MODEL_WIDTH)
    sent_rows = jnp.zeros((blocks, E * CAP, MODEL_WIDTH), jnp.float32).at[which_block, slot_rows].add(spread, mode='drop')
    sent_rows = low_back(sent_rows).reshape(blocks, E, CAP, MODEL_WIDTH)
    gate_pre = low_back(jnp.einsum('becd,edf->becf', sent_rows, gate_w, precision=TOP_PRECISION))
    up_pre = low_back(jnp.einsum('becd,edf->becf', sent_rows, up_w, precision=TOP_PRECISION))
    inner_act = low(jax.nn.silu(gate_pre) * up_pre)
    produced = low(low_back(jnp.einsum('becf,efd->becd', inner_act, down_w, precision=TOP_PRECISION)))
    produced = produced.reshape(blocks, E * CAP, MODEL_WIDTH)
    clipped = jnp.minimum(slot_rows, E * CAP - 1)
    fetched = jax.vmap(lambda source_table, indices: jnp.take(source_table, indices, axis=0))(produced, clipped)
    fetched = fetched.reshape(PACKED_TOKENS, TOPK, MODEL_WIDTH)
    weighting = gate_values * kept_row.astype(jnp.float32)
    return hidden + jnp.einsum('tk,tkd->td', weighting, fetched, precision=TOP_PRECISION)

def reference(tokens, segments, routes, norm_gain, w_query, key_weight, value_weight, w_output, moe_gain, w_router, w_gate, w_up, w_down, cotangent):
    slot_index, kept_mask = slot_table(routes, E, TOK_DEV, CAP)
    n_rows = TOKENS // PACKED_TOKENS
    seg_rows = segments.reshape(n_rows, PACKED_TOKENS)
    slot_rows = slot_index.reshape(n_rows, PACKED_TOKENS, TOPK)
    kept_rows = kept_mask.reshape(n_rows, PACKED_TOKENS, TOPK)
    route_rows = routes.reshape(n_rows, PACKED_TOKENS, TOPK)

    def forward(x_all, norm_g, query_w, key_matrix, value_matrix, output_w, moe_g, router_w, gate_w, up_w, down_w):

        def one_row(item):
            return layer_row(item[0], item[1], item[2], item[3], item[4], norm_g, query_w, key_matrix, value_matrix, output_w, moe_g, router_w, gate_w, up_w, down_w)
        rows_out = lax.map(jax.checkpoint(one_row), (x_all.reshape(n_rows, PACKED_TOKENS, MODEL_WIDTH), seg_rows, slot_rows, kept_rows, route_rows))
        return rows_out.reshape(TOKENS, MODEL_WIDTH)
    outputs, pull_back = jax.vjp(forward, tokens.astype(jnp.float32), norm_gain.astype(jnp.float32), w_query.astype(jnp.float32), key_weight.astype(jnp.float32), value_weight.astype(jnp.float32), w_output.astype(jnp.float32), moe_gain.astype(jnp.float32), w_router.astype(jnp.float32), w_gate.astype(jnp.float32), w_up.astype(jnp.float32), w_down.astype(jnp.float32))
    grads_all = pull_back(cotangent.astype(jnp.float32))
    return (outputs.astype(jnp.bfloat16), grads_all[0], grads_all[1], grads_all[2], grads_all[3], grads_all[4], grads_all[5], grads_all[6], grads_all[7], grads_all[8], grads_all[9], grads_all[10])
```

```python
import functools

import jax
import jax.numpy as jnp
from jax import lax
from jax.experimental import pallas as pl
from jax.experimental.pallas import tpu as pltpu
from jax.sharding import PartitionSpec as P

MODEL_WIDTH = 1024
HEAD_SIZE = 64
TOPK = 8
TABLE_ROWS = 16

EPSILON = 1e-06
ROPE_BASE = 10000.0
TOP_PRECISION = lax.Precision.HIGHEST
F32 = jnp.float32
BF16 = jnp.bfloat16


def row_swap(value, offset):
    size = lax.axis_size("row")
    return lax.ppermute(value, "row", [(i, i ^ offset) for i in range(size)])


def head_swap(value, offset):
    size = lax.axis_size("head")
    return lax.ppermute(value, "head", [(i, i ^ offset) for i in range(size)])


def dot(a, b, ca, cb, **kw):
    return lax.dot_general(a, b, (((ca,), (cb,)), ((), ())), preferred_element_type=F32, **kw)


def rotate(values, cosine, sine_part):
    halfway = values.shape[-1] // 2
    first_half = values[..., :halfway]
    second = values[..., halfway:]
    return jnp.concatenate(
        [first_half * cosine - second * sine_part, second * cosine + first_half * sine_part],
        axis=-1,
    )


def norm_back(values, factor, gain, upstream):
    weighted = upstream * gain
    middle = jnp.mean(weighted * values, axis=-1, keepdims=True)
    grad_in = factor * (weighted - values * factor * factor * middle)
    return (grad_in, jnp.sum(upstream * values * factor, axis=0))


def split_table(table, extra):
    coarse = table.astype(BF16)
    fine = (table - coarse.astype(F32)).astype(BF16)
    rows = jnp.concatenate(
        [coarse.reshape(-1, MODEL_WIDTH), fine.reshape(-1, MODEL_WIDTH)], axis=0
    )
    return jnp.concatenate([rows, jnp.zeros((extra - rows.shape[0], MODEL_WIDTH), BF16)], axis=0)


def join_table(rows, n_experts):
    per = n_experts * (MODEL_WIDTH // 4) // MODEL_WIDTH
    rows = rows.astype(F32)
    return (rows[:per] + rows[per : 2 * per]).reshape(n_experts, -1)


def experts_kernel(tokens_here, capacity, per, expert_ref, *refs):
    x_refs, g_refs = refs[:4], refs[4:8]
    gate_w, up_w, down_w = refs[8:11]
    out_refs, grad_refs = refs[11:13], refs[13:15]
    rows_ref, gprod_ref, inner_ref, dgate_ref, dup_ref = refs[15:20]
    pick_ref, g_rows_ref = refs[20:22]
    expert = expert_ref[0]
    groups = MODEL_WIDTH // tokens_here
    table_row = expert // groups
    group = expert % groups

    def take(table, first):
        index = lax.broadcasted_iota(jnp.int32, table.shape, 0)
        line = jnp.sum(jnp.where(index == table_row + first, table, 0.0), axis=0, keepdims=True)
        picked = jnp.zeros((1, tokens_here), F32)
        for q in range(groups):
            part = line[:, q * tokens_here : (q + 1) * tokens_here]
            picked = picked + jnp.where(group == q, part, 0.0)
        return picked

    slot_index = lax.broadcasted_iota(jnp.int32, (capacity, tokens_here), 0).astype(F32)
    gate_slots = []
    for b in range(4):
        rank = take(g_refs[b][tokens_here:, :].astype(F32), 0)
        table = x_refs[b][tokens_here:, :].astype(F32)
        gate = take(table, 0) + take(table, per)
        pick = (slot_index == rank).astype(F32)
        gate_slots.append(jnp.sum(pick * gate, axis=1, keepdims=True))
        pick = pick.astype(BF16)
        pick_ref[b] = pick
        at = slice(b * capacity, (b + 1) * capacity)
        rows_ref[at, :] = dot(pick, x_refs[b][:tokens_here, :], 1, 0).astype(BF16)
        g_rows_ref[at, :] = dot(pick, g_refs[b][:tokens_here, :], 1, 0).astype(BF16)
    gate_slot = jnp.concatenate(gate_slots, axis=0)
    gate_pre = dot(rows_ref[...], gate_w[0], 1, 0)
    up_pre = dot(rows_ref[...], up_w[0], 1, 0)
    sigmoid = jax.nn.sigmoid(gate_pre)
    silu = gate_pre * sigmoid
    inner = (silu * up_pre).astype(BF16)
    inner_ref[...] = inner
    produced = dot(inner, down_w[0], 1, 0).astype(BF16).astype(F32)
    g_rows = g_rows_ref[...].astype(F32)
    grad_gate = jnp.sum(g_rows * produced, axis=1, keepdims=True)
    scaled = (gate_slot * produced).astype(BF16)
    gprod = (gate_slot * g_rows).astype(BF16)
    gprod_ref[...] = gprod
    grad_inner = dot(gprod, down_w[0], 1, 1)
    dgate = (grad_inner * up_pre * sigmoid * (1.0 + gate_pre * (1.0 - sigmoid))).astype(BF16)
    dup = (grad_inner * silu).astype(BF16)
    dgate_ref[...] = dgate
    dup_ref[...] = dup
    grad_rows = (dot(dgate, gate_w[0], 1, 1) + dot(dup, up_w[0], 1, 1)).astype(BF16)
    shape = (TABLE_ROWS, MODEL_WIDTH)
    row_index = lax.broadcasted_iota(jnp.int32, shape, 0)
    in_group = lax.broadcasted_iota(jnp.int32, shape, 1) // tokens_here == group
    for b in range(4):
        at = slice(b * capacity, (b + 1) * capacity)
        out_ref, grad_ref = out_refs[b // 2], grad_refs[b // 2]
        pick = pick_ref[b]
        out_ref[b % 2] = dot(pick, scaled[at], 0, 0).astype(BF16)
        grad_ref[b % 2, :tokens_here, :] = dot(pick, grad_rows[at], 0, 0).astype(BF16)
        line = jnp.sum(pick.astype(F32) * grad_gate[at], axis=0, keepdims=True)
        coarse = line.astype(BF16).astype(F32)
        coarse, fine = (
            jnp.concatenate([v] * groups, axis=1) for v in (coarse, line - coarse)
        )
        table = jnp.where(in_group & (row_index == table_row), coarse, 0.0)
        table = table + jnp.where(in_group & (row_index == table_row + per), fine, 0.0)
        grad_ref[b % 2, tokens_here:, :] = table.astype(BF16)


def run_experts(expert, x_blocks, g_blocks, w_gate, w_up, w_down, capacity, n_experts):
    tokens_here = x_blocks[0].shape[0] - TABLE_ROWS
    width = w_gate.shape[2]
    rows = 4 * capacity
    per = n_experts * tokens_here // MODEL_WIDTH
    vmem = pl.BlockSpec(memory_space=pltpu.VMEM)
    out_shape = (
        [jax.ShapeDtypeStruct((2, tokens_here, MODEL_WIDTH), BF16)] * 2
        + [jax.ShapeDtypeStruct((2, tokens_here + TABLE_ROWS, MODEL_WIDTH), BF16)] * 2
        + [jax.ShapeDtypeStruct((rows, MODEL_WIDTH), BF16)] * 2
        + [jax.ShapeDtypeStruct((rows, width), BF16)] * 3
    )
    products = rows * MODEL_WIDTH * (6 * width + 4 * tokens_here)
    return pl.pallas_call(
        functools.partial(experts_kernel, tokens_here, capacity, per),
        out_shape=out_shape,
        in_specs=[pl.BlockSpec(memory_space=pltpu.SMEM)] + [vmem] * 11,
        out_specs=[vmem] * 9,
        scratch_shapes=[
            pltpu.VMEM((4, capacity, tokens_here), BF16),
            pltpu.VMEM((rows, MODEL_WIDTH), BF16),
        ],
        compiler_params=pltpu.CompilerParams(vmem_limit_bytes=48 * 1024 * 1024),
        cost_estimate=pl.CostEstimate(
            flops=2 * products, bytes_accessed=20 * 1024 * 1024, transcendentals=rows * width
        ),
        name="experts",
    )(expert, *x_blocks, *g_blocks, w_gate, w_up, w_down)


def local(
    tokens,
    segments,
    routes,
    norm_gain,
    w_query,
    key_weight,
    value_weight,
    w_output,
    moe_gain,
    w_router,
    w_gate,
    w_up,
    w_down,
    cotangent,
):
    local_rows = tokens.shape[0]
    length = segments.shape[0]
    n_experts = w_router.shape[1]
    capacity = local_rows * TOPK * 5 // (4 * n_experts)
    heads_here = w_query.shape[1] // HEAD_SIZE
    kv_here = key_weight.shape[1] // HEAD_SIZE
    heads_per_group = heads_here // kv_here
    width_query = w_query.shape[1]
    width_key = key_weight.shape[1]
    score_scale = HEAD_SIZE ** (-0.5)
    n_row = lax.axis_size("row")
    n_head = lax.axis_size("head")
    n_outer = n_row // 4
    row_at = lax.axis_index("row")
    head_at = lax.axis_index("head")
    expert = row_at.astype(jnp.int32).reshape(1)

    routes_t = routes.T
    expert_index = jnp.arange(n_experts, dtype=jnp.int32)[:, None]
    chosen = jnp.any(routes_t[:, None, :] == expert_index[None], axis=0)
    t_index = jnp.arange(local_rows, dtype=jnp.int32)
    before = (t_index[:, None] < t_index[None, :]).astype(BF16)
    rank = dot(chosen.astype(BF16), before, 1, 0)
    slots = jnp.where(chosen & (rank < capacity), rank, -1.0)
    slot_rows = slots.astype(BF16).reshape(-1, MODEL_WIDTH)
    g_block = jnp.concatenate(
        [
            cotangent,
            slot_rows,
            jnp.zeros((TABLE_ROWS - slot_rows.shape[0], MODEL_WIDTH), BF16),
        ],
        axis=0,
    )

    def spread(block):
        chunks = []
        for o in range(n_outer):
            first = block if o == 0 else row_swap(block, 4 * o)
            second = row_swap(first, 2)
            chunks.append((first, second, row_swap(first, 1), row_swap(second, 1)))
        return chunks

    def gather_sum(own, other):
        arrived = row_swap(other, 1)
        near = (own[0].astype(F32) + arrived[0].astype(F32)).astype(BF16)
        far = (own[1].astype(F32) + arrived[1].astype(F32)).astype(BF16)
        return near, row_swap(far, 2)

    tokens_full = [tokens] + [head_swap(tokens, k) for k in range(1, n_head)]
    g_chunks = spread(g_block)

    base = [(head_at ^ k) * local_rows for k in range(n_head)]
    positions = jnp.concatenate([b + t_index for b in base])
    seg_order = jnp.concatenate(
        [lax.dynamic_slice_in_dim(segments, b, local_rows, 0) for b in base]
    )
    frequency = ROPE_BASE ** (-2.0 * jnp.arange(HEAD_SIZE // 2, dtype=F32) / HEAD_SIZE)
    angles = positions.astype(F32)[:, None] * frequency[None, :]
    cosine, sine_part = jnp.cos(angles)[:, None, :], jnp.sin(angles)[:, None, :]

    x_full = jnp.concatenate(tokens_full, axis=0).astype(F32)
    norm_factor_full = lax.rsqrt(jnp.mean(x_full * x_full, axis=-1, keepdims=True) + EPSILON)
    normed_full = (x_full * norm_factor_full * norm_gain).astype(BF16)
    x_in = x_full[:local_rows]
    norm_factor = norm_factor_full[:local_rows]
    w_in = jnp.concatenate([w_query, key_weight, value_weight], axis=1)
    projected = dot(normed_full, w_in, 1, 0)
    queries = rotate(
        projected[:, :width_query].reshape(length, heads_here, HEAD_SIZE), cosine, sine_part
    ).astype(BF16)
    keys_rot = rotate(
        projected[:, width_query : width_query + width_key].reshape(length, kv_here, HEAD_SIZE),
        cosine,
        sine_part,
    ).astype(BF16)
    values_low = (
        projected[:, width_query + width_key :].reshape(length, kv_here, HEAD_SIZE).astype(BF16)
    )
    keys_wide = jnp.repeat(keys_rot, heads_per_group, axis=1)
    values_wide = jnp.repeat(values_low, heads_per_group, axis=1)
    allowed = (seg_order[:, None] == seg_order[None, :]) & (
        positions[None, :] <= positions[:, None]
    )

    def make_scores():
        scores = jnp.einsum("qhd,khd->hqk", queries, keys_wide, preferred_element_type=F32)
        return jnp.where(allowed[None], scores * score_scale, -1e30)

    scores = make_scores()
    highest = jnp.max(scores, axis=-1, keepdims=True)
    exponent = jnp.exp(scores - highest)
    totals = jnp.sum(exponent, axis=-1, keepdims=True)
    probs_low = (exponent / totals).astype(BF16)
    mixed = jnp.einsum("hqk,khd->qhd", probs_low, values_wide, preferred_element_type=F32)
    mixed_heads = mixed.astype(BF16).reshape(length, heads_here * HEAD_SIZE)
    log_totals = highest + jnp.log(totals)

    def head_sum(lhs, rhs, contract):
        parts = [
            dot(lhs[k * local_rows : (k + 1) * local_rows], rhs, 1, contract)
            for k in range(n_head)
        ]
        total = parts[0]
        for k in range(1, n_head):
            total = total + head_swap(parts[k].astype(BF16), k).astype(F32)
        return total

    attention = head_sum(mixed_heads, w_output, 0)
    hidden = x_in + attention
    moe_factor = lax.rsqrt(jnp.mean(hidden * hidden, axis=-1, keepdims=True) + EPSILON)
    normed_moe = (hidden * moe_factor * moe_gain).astype(BF16)
    logits = dot(w_router, normed_moe, 0, 1)
    logits = jnp.where(chosen, logits, -1e30)
    gate_exp = jnp.where(chosen, jnp.exp(logits - jnp.max(logits, axis=0, keepdims=True)), 0.0)
    gates = gate_exp / jnp.sum(gate_exp, axis=0, keepdims=True)
    x_block = jnp.concatenate([normed_moe, split_table(gates, TABLE_ROWS)], axis=0)
    x_chunks = spread(x_block)

    out_parts, grad_parts, saved = [], [], []
    for o in range(n_outer):
        made = run_experts(
            expert, x_chunks[o], g_chunks[o], w_gate, w_up, w_down, capacity, n_experts
        )
        out_parts.append(made[0:2])
        grad_parts.append(made[2:4])
        saved.append(made[4:])

    def collect(parts):
        total = None
        for o in range(n_outer):
            near, far = gather_sum(*parts[o])
            term = near.astype(F32) + far.astype(F32)
            if o:
                term = row_swap(term.astype(BF16), 4 * o).astype(F32)
            total = term if total is None else total + term
        return total

    grad_sum = collect(grad_parts)
    moe_out = collect(out_parts)
    mixed_out = (hidden + moe_out).astype(BF16)

    rows_in, gprod, inner, dgate, dup = (
        jnp.concatenate([s[i] for s in saved], axis=0) for i in range(5)
    )
    grad_gate_w = dot(rows_in, dgate, 0, 0)
    grad_up_w = dot(rows_in, dup, 0, 0)
    grad_down = dot(inner, gprod, 0, 0)

    def head_split(value, axis):
        size = value.shape[axis] // n_head
        total = lax.dynamic_slice_in_dim(value, head_at * size, size, axis)
        for k in range(1, n_head):
            part = lax.dynamic_slice_in_dim(value, (head_at ^ k) * size, size, axis)
            total = total + head_swap(part.astype(BF16), k).astype(F32)
        return total[None]

    expert_sums = (head_split(grad_gate_w, 0), head_split(grad_up_w, 0), head_split(grad_down, 1))

    upstream = cotangent.astype(F32)
    grad_gates = join_table(grad_sum[local_rows:], n_experts)
    grad_logits = gates * (grad_gates - jnp.sum(gates * grad_gates, axis=0, keepdims=True))
    grad_router = dot(grad_logits, normed_moe.astype(F32), 1, 0, precision=TOP_PRECISION)
    grad_normed_moe = grad_sum[:local_rows] + dot(
        grad_logits, w_router.astype(F32), 0, 1, precision=TOP_PRECISION
    )
    grad_hidden_norm, grad_moe_gain = norm_back(hidden, moe_factor, moe_gain, grad_normed_moe)
    grad_hidden = upstream + grad_hidden_norm
    grad_attention = grad_hidden.astype(BF16)
    grad_full = jnp.concatenate(
        [grad_attention] + [head_swap(grad_attention, k) for k in range(1, n_head)], axis=0
    )
    grad_mixed = dot(grad_full, w_output, 1, 1).astype(BF16)
    grad_mixed = grad_mixed.reshape(length, heads_here, HEAD_SIZE)
    grad_output_t = dot(grad_full, mixed_heads, 0, 0)

    probs_full = jnp.exp(make_scores() - log_totals)
    grad_probs = jnp.einsum("qhd,khd->hqk", grad_mixed, values_wide, preferred_element_type=F32)
    inner_prod = jnp.sum(probs_full * grad_probs, axis=-1, keepdims=True)
    grad_scores = (probs_full * (grad_probs - inner_prod)).astype(BF16)
    grad_queries = (
        jnp.einsum("hqk,khd->qhd", grad_scores, keys_wide, preferred_element_type=F32)
        * score_scale
    )
    grad_keys = (
        jnp.einsum("hqk,qhd->khd", grad_scores, queries, preferred_element_type=F32) * score_scale
    )
    grad_values = jnp.einsum(
        "hqk,qhd->khd", probs_full.astype(BF16), grad_mixed, preferred_element_type=F32
    )
    grad_keys = grad_keys.reshape(length, kv_here, heads_per_group, HEAD_SIZE).sum(axis=2)
    grad_values = grad_values.reshape(length, kv_here, heads_per_group, HEAD_SIZE).sum(axis=2)
    grad_queries = rotate(grad_queries, cosine, -sine_part)
    grad_keys = rotate(grad_keys, cosine, -sine_part)
    grad_proj = jnp.concatenate(
        [
            grad_queries.reshape(length, width_query),
            grad_keys.reshape(length, width_key),
            grad_values.reshape(length, width_key),
        ],
        axis=1,
    ).astype(BF16)
    grad_in_w = dot(normed_full, grad_proj, 0, 0)
    grad_normed = head_sum(grad_proj, w_in, 1)
    grad_x_norm, grad_norm_gain = norm_back(x_in, norm_factor, norm_gain, grad_normed)
    grad_tokens = grad_hidden + grad_x_norm

    def row_sum(value):
        share = value.shape[0] // n_row
        value = value.reshape(n_outer, 2, 2, share, -1)
        for axis, offset in ((2, 1), (1, 2)):
            bit = (row_at // offset) % 2
            own = lax.dynamic_index_in_dim(value, bit, axis, keepdims=False)
            other = lax.dynamic_index_in_dim(value, 1 - bit, axis, keepdims=False)
            value = own + row_swap(other.astype(BF16), offset).astype(F32)
        at = row_at // 4
        total = lax.dynamic_index_in_dim(value, at, 0, keepdims=False)
        for o in range(1, n_outer):
            part = lax.dynamic_index_in_dim(value, at ^ o, 0, keepdims=False)
            total = total + row_swap(part.astype(BF16), 4 * o).astype(F32)
        return total

    def sum_all(value):
        offset = 1
        while offset < n_row:
            value = value + row_swap(value, offset)
            offset *= 2
        offset = 1
        while offset < n_head:
            value = value + head_swap(value, offset)
            offset *= 2
        return value

    output_share = row_sum(grad_output_t).T
    in_share = row_sum(grad_in_w)
    early = sum_all(jnp.concatenate([grad_router, grad_moe_gain[None]], axis=0))
    grad_norm_gain = sum_all(grad_norm_gain)
    return (
        mixed_out,
        grad_tokens,
        grad_norm_gain,
        in_share[:, :width_query],
        in_share[:, width_query : width_query + width_key],
        in_share[:, width_query + width_key :],
        output_share,
        early[n_experts],
        early[:n_experts].T,
        *expert_sums,
    )


def solution(mesh):
    in_specs = (
        P(("row", "head"), None),
        P("row"),
        P(("row", "head"), None),
        P(),
        P(None, "head"),
        P(None, "head"),
        P(None, "head"),
        P("head", None),
        P(),
        P(),
        P("row", None, None),
        P("row", None, None),
        P("row", None, None),
        P(("row", "head"), None),
    )
    out_specs = (
        P(("row", "head"), None),
        P(("row", "head"), None),
        P(),
        P("row", "head"),
        P("row", "head"),
        P("row", "head"),
        P("head", "row"),
        P(),
        P(),
        P("row", "head", None),
        P("row", "head", None),
        P("row", None, "head"),
    )
    return jax.shard_map(local, mesh=mesh, in_specs=in_specs, out_specs=out_specs, check_vma=False)
```

```python
import functools

import jax
import jax.numpy as jnp
from jax import lax
from jax.experimental import pallas as pl
from jax.experimental.pallas import tpu as pltpu
from jax.sharding import PartitionSpec as P

MODEL_WIDTH = 1024
HEAD_SIZE = 64
TOPK = 8

EPSILON = 1e-06
ROPE_BASE = 10000.0
F32 = jnp.float32
BF16 = jnp.bfloat16


def row_swap(value, offset):
    size = lax.axis_size("row")
    return lax.ppermute(value, "row", [(i, i ^ offset) for i in range(size)])


def head_swap(value, offset):
    size = lax.axis_size("head")
    return lax.ppermute(value, "head", [(i, i ^ offset) for i in range(size)])


def dot(a, b, ca, cb, **kw):
    return lax.dot_general(a, b, (((ca,), (cb,)), ((), ())), preferred_element_type=F32, **kw)


def after(value, *others):
    return lax.optimization_barrier((value, *others))[0]


def experts_kernel(tokens_here, capacity, per, rows_before, first_call, number_ref, *refs):
    n_in = 13 if first_call else 18
    x_hbm, g_hbm, w_hbm = refs[0:2], refs[2:4], refs[4:13]
    made_hbm, saved_hbm = refs[n_in : n_in + 2], refs[n_in + 2 : n_in + 7]
    scratch = refs[n_in + 7 :]
    x_refs, g_refs, w_refs = scratch[0:2], scratch[2:4], scratch[4:10]
    made_refs = scratch[10:12]
    rows_ref, gprod_ref, inner_ref, dgate_ref, dup_ref = scratch[12:17]
    pick_ref, g_rows_ref, in_sem, out_sem, saved_sem = scratch[17:22]
    expert, bit = number_ref[0], number_ref[1]

    def half(which, index):
        size = w_refs[which].shape[1] // 2
        return w_refs[which].at[0, pl.ds(pl.multiple_of(index * size, size), size)]

    places = [x_refs[0], g_refs[0], x_refs[1], g_refs[1], *w_refs[:3]]
    places += [half(3, bit), half(3, 1 - bit), half(4, 0), half(4, 1), half(5, bit), half(5, 1 - bit)]
    sources = [x_hbm[0], g_hbm[0], x_hbm[1], g_hbm[1], *w_hbm]
    loads = [
        pltpu.make_async_copy(src, dst, in_sem.at[i])
        for i, (src, dst) in enumerate(zip(sources, places))
    ]
    for load in loads:
        load.start()
    arrivals = [[[4], [5], [6]], [[7, 8], [9, 10], [11, 12]]]

    def arrive(numbers):
        for i in numbers:
            loads[i].wait()

    saves = []

    def save(which, expert):
        buffer = (rows_ref, gprod_ref, inner_ref, dgate_ref, dup_ref)[which]
        copy = pltpu.make_async_copy(
            buffer.at[expert],
            saved_hbm[which].at[expert, pl.ds(rows_before, 2 * capacity)],
            saved_sem.at[which, expert],
        )
        copy.start()
        saves.append(copy)

    groups = MODEL_WIDTH // tokens_here

    def place(number):
        return number % per, number // per

    def take(table, first, number):
        table_row, group = place(number)
        index = lax.broadcasted_iota(jnp.int32, table.shape, 0)
        line = jnp.sum(jnp.where(index == table_row + first, table, 0.0), axis=0, keepdims=True)
        picked = jnp.zeros((1, tokens_here), F32)
        for q in range(groups):
            part = line[:, q * tokens_here : (q + 1) * tokens_here]
            picked = picked + jnp.where(group == q, part, 0.0)
        return picked

    numbers = (expert, expert ^ 2)
    slot_index = lax.broadcasted_iota(jnp.int32, (capacity, tokens_here), 0).astype(F32)
    gate_slots = [[], []]
    for b in range(2):
        arrive([2 * b, 2 * b + 1])
        table = x_refs[b][tokens_here:, :].astype(F32)
        for e in range(2):
            rank = take(table, 2 * per, numbers[e])
            gate = take(table, 0, numbers[e]) + take(table, per, numbers[e])
            pick = (slot_index == rank).astype(F32)
            gate_slots[e].append(jnp.sum(pick * gate, axis=1, keepdims=True))
            pick_ref[b, e * capacity : (e + 1) * capacity, :] = pick.astype(BF16)
        at = slice(b * capacity, (b + 1) * capacity)
        rows = dot(pick_ref[b], x_refs[b][:tokens_here, :], 1, 0).astype(BF16)
        g_rows = dot(pick_ref[b], g_refs[b][...], 1, 0).astype(BF16)
        for e in range(2):
            rows_ref[e, at, :] = rows[e * capacity : (e + 1) * capacity]
            g_rows_ref[e, at, :] = g_rows[e * capacity : (e + 1) * capacity]
    scaled, grad_rows, grad_gate = [], [], []
    for e in range(2):
        save(0, e)
        gate_slot = jnp.concatenate(gate_slots[e], axis=0)
        g_rows = g_rows_ref[e].astype(F32)
        gprod_ref[e] = (gate_slot * g_rows).astype(BF16)
        save(1, e)
        gate_w, up_w, down_w = w_refs[3 * e : 3 * e + 3]
        arrive(arrivals[e][0])
        gate_pre = dot(rows_ref[e], gate_w[0], 1, 0)
        arrive(arrivals[e][1])
        up_pre = dot(rows_ref[e], up_w[0], 1, 0)
        sigmoid = jax.nn.sigmoid(gate_pre)
        silu = gate_pre * sigmoid
        inner_ref[e] = (silu * up_pre).astype(BF16)
        save(2, e)
        arrive(arrivals[e][2])
        produced = dot(inner_ref[e], down_w[0], 1, 0).astype(BF16).astype(F32)
        grad_gate.append(jnp.sum(g_rows * produced, axis=1, keepdims=True))
        scaled.append((gate_slot * produced).astype(BF16))
        grad_inner = dot(gprod_ref[e], down_w[0], 1, 1)
        dgate_ref[e] = (
            grad_inner * up_pre * sigmoid * (1.0 + gate_pre * (1.0 - sigmoid))
        ).astype(BF16)
        save(3, e)
        dup_ref[e] = (grad_inner * silu).astype(BF16)
        save(4, e)
        grad_rows.append(
            (dot(dgate_ref[e], gate_w[0], 1, 1) + dot(dup_ref[e], up_w[0], 1, 1)).astype(BF16)
        )
    table_rows = x_refs[0].shape[0] - tokens_here
    shape = (table_rows, MODEL_WIDTH)
    row_index = lax.broadcasted_iota(jnp.int32, shape, 0)
    lane_group = lax.broadcasted_iota(jnp.int32, shape, 1) // tokens_here
    stores = []

    def store(i, src, dst):
        copy = pltpu.make_async_copy(src, dst, out_sem.at[i])
        copy.start()
        stores.append(copy)

    for b in (1, 0):
        at = slice(b * capacity, (b + 1) * capacity)
        pick = pick_ref[b]
        made = jnp.concatenate([grad_rows[0][at], grad_rows[1][at]], axis=0)
        made_refs[b][:tokens_here, :] = dot(pick, made, 0, 0).astype(BF16)
        table = jnp.zeros(shape, F32)
        for e in range(2):
            table_row, group = place(numbers[e])
            picked = pick[e * capacity : (e + 1) * capacity].astype(F32)
            line = jnp.sum(picked * grad_gate[e][at], axis=0, keepdims=True)
            coarse = line.astype(BF16).astype(F32)
            here = lane_group == group
            for first, part in ((0, coarse), (per, line - coarse)):
                wide = jnp.concatenate([part] * groups, axis=1)
                table = table + jnp.where(here & (row_index == table_row + first), wide, 0.0)
        tall = tokens_here + table_rows
        made_refs[b][tokens_here:tall, :] = table.astype(BF16)
        made = jnp.concatenate([scaled[0][at], scaled[1][at]], axis=0)
        made_refs[b][tall:, :] = dot(pick, made, 0, 0).astype(BF16)
        store(b, made_refs[b], made_hbm[b])
    for copy in saves + stores:
        copy.wait()


def run_experts(numbers, x_blocks, g_blocks, weights, saved, chunk, n_chunks, capacity):
    tokens_here = g_blocks[0].shape[0]
    block_rows = x_blocks[0].shape[0]
    width = weights[0].shape[2]
    n_experts = lax.axis_size("row")
    rows = 2 * capacity
    per = n_experts * tokens_here // MODEL_WIDTH
    first_call = saved is None
    anywhere = pl.BlockSpec(memory_space=pl.ANY)
    block = jax.ShapeDtypeStruct((tokens_here + block_rows, MODEL_WIDTH), BF16)
    kept = [jax.ShapeDtypeStruct((2, n_chunks * rows, MODEL_WIDTH), BF16)] * 2
    kept += [jax.ShapeDtypeStruct((2, n_chunks * rows, width), BF16)] * 3
    operands = [*x_blocks, *g_blocks, *weights] + ([] if first_call else list(saved))
    made = pl.pallas_call(
        functools.partial(
            experts_kernel, tokens_here, capacity, per, chunk * rows, first_call
        ),
        out_shape=[block] * 2 + kept,
        in_specs=[pl.BlockSpec(memory_space=pltpu.SMEM)] + [anywhere] * len(operands),
        out_specs=[anywhere] * 7,
        scratch_shapes=[pltpu.VMEM(v.shape, BF16) for v in (*x_blocks, *g_blocks, *weights[:3], *weights[:3])]
        + [pltpu.VMEM(block.shape, BF16)] * 2
        + [pltpu.VMEM((2, rows, MODEL_WIDTH), BF16)] * 2
        + [pltpu.VMEM((2, rows, width), BF16)] * 3
        + [
            pltpu.VMEM((2, 2 * capacity, tokens_here), BF16),
            pltpu.VMEM((2, rows, MODEL_WIDTH), BF16),
            pltpu.SemaphoreType.DMA((13,)),
            pltpu.SemaphoreType.DMA((2,)),
            pltpu.SemaphoreType.DMA((5, 2)),
        ],
        input_output_aliases={} if first_call else {14 + i: 2 + i for i in range(5)},
        compiler_params=pltpu.CompilerParams(vmem_limit_bytes=48 * 1024 * 1024),
        cost_estimate=pl.CostEstimate(flops=1000, bytes_accessed=1000, transcendentals=0),
        name="experts",
    )(numbers, *operands)
    return made[0:2], made[2:7]


def swap_halves(values):
    width = values.shape[1]
    half = HEAD_SIZE // 2
    lane = lax.broadcasted_iota(jnp.int32, values.shape, 1)
    return jnp.where(
        lane % HEAD_SIZE < half,
        pltpu.roll(values, width - half, 1),
        pltpu.roll(values, half, 1),
    )


def turn(values, cosine, sine_part):
    times = values.shape[1] // cosine.shape[1]
    wide = [jnp.concatenate([v] * times, axis=1) for v in (cosine, sine_part)]
    return values * wide[0] + swap_halves(values) * wide[1]


def rms_factor(values):
    return lax.rsqrt(jnp.mean(values * values, axis=-1, keepdims=True) + EPSILON)


def block_bias(seg_col_ref, seg_row_ref, first, rows, keys):
    queries = lax.broadcasted_iota(jnp.int32, (rows, keys), 0) + first
    at = lax.broadcasted_iota(jnp.int32, (rows, keys), 1)
    same = seg_col_ref[first : first + rows, :] == seg_row_ref[:, :keys]
    return jnp.where(same & (at <= queries), 0.0, -1e30)


def head_lanes(number):
    return slice(number * HEAD_SIZE, (number + 1) * HEAD_SIZE)


def attend_kernel(n_head, head_ref, *refs):
    token_refs = refs[:n_head]
    seg_col, seg_row, gain, w_q, w_k, w_v, w_o, cos_ref, sin_ref = refs[n_head : n_head + 9]
    normed_ref, q_ref, k_ref, v_ref, mixed_ref, lse_ref, own_ref, other_ref = refs[n_head + 9 : n_head + 17]
    part_ref = refs[n_head + 17]
    rows = token_refs[0].shape[0]
    head_at = head_ref[0]
    scale = HEAD_SIZE ** (-0.5)
    for k in range(n_head):
        x = token_refs[k][...].astype(F32)
        at = pl.ds(pl.multiple_of((head_at ^ k) * rows, rows), rows)
        normed_ref[at, :] = (x * rms_factor(x) * gain[...]).astype(BF16)
    normed = normed_ref[...]
    cosine, sine_part = cos_ref[...], sin_ref[...]
    q_ref[...] = (turn(dot(normed, w_q[...], 1, 0), cosine, sine_part).astype(BF16) * scale).astype(BF16)
    k_ref[...] = turn(dot(normed, w_k[...], 1, 0), cosine, sine_part).astype(BF16)
    v_ref[...] = dot(normed, w_v[...], 1, 0).astype(BF16)
    kv = k_ref.shape[1] // HEAD_SIZE
    per_group = q_ref.shape[1] // k_ref.shape[1]
    lane = lax.broadcasted_iota(jnp.int32, (rows, lse_ref.shape[1]), 1)
    for i in range(n_head):
        first, keys = i * rows, (i + 1) * rows
        bias = block_bias(seg_col, seg_row, first, rows, keys)
        log_totals = jnp.zeros((rows, lse_ref.shape[1]), F32)
        for j in range(kv):
            key = k_ref[:keys, head_lanes(j)]
            value = v_ref[:keys, head_lanes(j)]
            made = []
            for h in range(j * per_group, (j + 1) * per_group):
                scores = dot(q_ref[first:keys, head_lanes(h)], key, 1, 1) + bias
                highest = jnp.max(scores, axis=1, keepdims=True)
                exponent = jnp.exp(scores - highest)
                total = jnp.sum(exponent, axis=1, keepdims=True)
                log_totals = jnp.where(lane == h, highest + jnp.log(total), log_totals)
                probs = (exponent * (1.0 / total)).astype(BF16)
                made.append(dot(probs, value, 1, 0).astype(BF16))
            lanes = slice(j * per_group * HEAD_SIZE, (j + 1) * per_group * HEAD_SIZE)
            mixed_ref[first:keys, lanes] = jnp.concatenate(made, axis=1)
        lse_ref[first:keys, :] = log_totals
    part_ref[...] = dot(mixed_ref[...], w_o[...], 1, 0)
    own_ref[...] = part_ref[pl.ds(pl.multiple_of(head_at * rows, rows), rows), :]
    for k in range(1, n_head):
        at = pl.ds(pl.multiple_of((head_at ^ k) * rows, rows), rows)
        other_ref[k - 1] = part_ref[at, :].astype(BF16)


def attend_back_kernel(n_head, head_ref, *refs):
    token_refs, refs = refs[:n_head], refs[n_head:]
    grad_refs = refs[:n_head]
    seg_col, seg_row, w_q, w_k, w_v, w_o, cos_ref, sin_ref = refs[n_head : n_head + 8]
    q_ref, k_ref, v_ref, lse_ref = refs[n_head + 8 : n_head + 12]
    full_ref, proj_ref, own_ref, other_ref, gain_ref = refs[n_head + 12 : n_head + 17]
    gm_ref, dq_ref, dk_ref, dv_ref, part_ref = refs[n_head + 17 :]
    rows = grad_refs[0].shape[0]
    head_at = head_ref[0]
    scale = HEAD_SIZE ** (-0.5)
    for k in range(n_head):
        at = pl.ds(pl.multiple_of((head_at ^ k) * rows, rows), rows)
        full_ref[at, :] = grad_refs[k][...]
    gm_ref[...] = dot(full_ref[...], w_o[...], 1, 1).astype(BF16)
    cosine, sine_part = cos_ref[...], -sin_ref[...]
    kv = k_ref.shape[1] // HEAD_SIZE
    per_group = q_ref.shape[1] // k_ref.shape[1]
    dk_ref[...] = jnp.zeros(dk_ref.shape, F32)
    dv_ref[...] = jnp.zeros(dv_ref.shape, F32)
    for i in range(n_head):
        first, keys = i * rows, (i + 1) * rows
        bias = block_bias(seg_col, seg_row, first, rows, keys)
        for j in range(kv):
            key = k_ref[:keys, head_lanes(j)]
            value = v_ref[:keys, head_lanes(j)]
            made, dk, dv = [], 0.0, 0.0
            for h in range(j * per_group, (j + 1) * per_group):
                query = q_ref[first:keys, head_lanes(h)]
                grad = gm_ref[first:keys, head_lanes(h)]
                probs = jnp.exp(dot(query, key, 1, 1) + bias - lse_ref[first:keys, h : h + 1])
                grad_probs = dot(grad, value, 1, 1)
                middle = jnp.sum(probs * grad_probs, axis=1, keepdims=True)
                ds = (probs * (grad_probs - middle)).astype(BF16)
                made.append(dot(ds, key, 1, 0) * scale)
                dk = dk + dot(query, ds, 0, 0)
                dv = dv + dot(grad, probs.astype(BF16), 0, 0)
            lanes = slice(j * per_group * HEAD_SIZE, (j + 1) * per_group * HEAD_SIZE)
            dq_ref[first:keys, lanes] = jnp.concatenate(made, axis=1)
            dk_ref[head_lanes(j), :keys] += dk
            dv_ref[head_lanes(j), :keys] += dv
    width_q, width_k = q_ref.shape[1], k_ref.shape[1]
    proj_ref[:, :width_q] = turn(dq_ref[...], cosine, sine_part).astype(BF16)
    proj_ref[:, width_q : width_q + width_k] = turn(dk_ref[...].T, cosine, sine_part).astype(BF16)
    proj_ref[:, width_q + width_k :] = dv_ref[...].T.astype(BF16)
    part_ref[...] = (
        dot(proj_ref[:, :width_q], w_q[...], 1, 1)
        + dot(proj_ref[:, width_q : width_q + width_k], w_k[...], 1, 1)
        + dot(proj_ref[:, width_q + width_k :], w_v[...], 1, 1)
    )
    gain = jnp.zeros(gain_ref.shape, F32)
    for k in range(n_head):
        part = part_ref[pl.ds(pl.multiple_of((head_at ^ k) * rows, rows), rows), :]
        x = token_refs[k][...].astype(F32)
        gain = gain + jnp.sum(part * (x * rms_factor(x)), axis=0, keepdims=True)
        if k:
            other_ref[k - 1] = part.astype(BF16)
        else:
            own_ref[...] = part
    gain_ref[...] = gain


def weight_grads_kernel(share, core_ref, normed_ref, proj_ref, full_ref, mixed_ref, own_ref, other_ref, all_ref):
    core = core_ref[0]
    width = proj_ref.shape[1]
    all_ref[:, :width] = dot(normed_ref[...], proj_ref[...], 0, 0)
    all_ref[:, width:] = dot(full_ref[...], mixed_ref[...], 0, 0)
    for m in range(own_ref.shape[0] // share):
        at = slice(m * share, (m + 1) * share)
        own = pl.ds(pl.multiple_of((2 * m + core) * share, share), share)
        other = pl.ds(pl.multiple_of((2 * m + 1 - core) * share, share), share)
        own_ref[at, :] = all_ref[own, :]
        other_ref[at, :] = all_ref[other, :].astype(BF16)


def expert_grads_kernel(n_head, axis, head_ref, lhs_ref, rhs_ref, own_ref, other_ref, all_ref):
    head_at = head_ref[0]
    size = own_ref.shape[1 + axis]
    for e in range(2):
        all_ref[...] = dot(lhs_ref[e], rhs_ref[e], 0, 0)
        for k in range(n_head):
            at = pl.ds(pl.multiple_of((head_at ^ k) * size, size), size)
            part = all_ref[at, :] if axis == 0 else all_ref[:, at]
            if k:
                other_ref[k - 1, e] = part.astype(BF16)
            else:
                own_ref[e] = part


def final_kernel(n_head, tokens_ref, grad_hidden_ref, gain, own_ref, *refs):
    total = own_ref[...]
    for part in refs[: n_head - 1]:
        total = total + part[...].astype(F32)
    x = tokens_ref[...].astype(F32)
    factor = rms_factor(x)
    weighted = total * gain[...]
    middle = jnp.mean(weighted * x, axis=-1, keepdims=True)
    refs[-1][...] = grad_hidden_ref[...] + factor * (weighted - x * factor * factor * middle)


def hidden_kernel(n_head, tokens_ref, own_ref, *refs):
    arrived = refs[: n_head - 1]
    gain, router_t, slots_ref, chosen_ref = refs[n_head - 1 : n_head + 3]
    block_ref, hidden_ref, gates_ref = refs[n_head + 3 :]
    rows = tokens_ref.shape[0]
    attention = own_ref[...]
    for part in arrived:
        attention = attention + part[...].astype(F32)
    hidden = tokens_ref[...].astype(F32) + attention
    hidden_ref[...] = hidden
    normed = (hidden * rms_factor(hidden) * gain[...]).astype(BF16)
    block_ref[:rows, :] = normed
    chosen = chosen_ref[...] > 0.0
    logits = jnp.where(chosen, dot(router_t[...], normed, 1, 1), -1e30)
    gates = jnp.where(chosen, jnp.exp(logits - jnp.max(logits, axis=0, keepdims=True)), 0.0)
    gates = gates / jnp.sum(gates, axis=0, keepdims=True)
    gates_ref[...] = gates
    coarse = gates.astype(BF16).astype(F32)
    groups = MODEL_WIDTH // rows
    per = gates.shape[0] // groups
    lines = [
        jnp.concatenate([v[q * per : (q + 1) * per] for q in range(groups)], axis=1)
        for v in (coarse, gates - coarse, slots_ref[...])
    ]
    spare = block_ref.shape[0] - rows - 3 * per
    if spare:
        lines.append(jnp.zeros((spare, MODEL_WIDTH), F32))
    block_ref[rows:, :] = jnp.concatenate(lines, axis=0).astype(BF16)


def grad_hidden_kernel(n_parts, *refs):
    parts = refs[:n_parts]
    hidden_ref, gain, router_t, gates_ref, block_ref, cotangent_ref = refs[n_parts : n_parts + 6]
    grad_ref, low_ref, small_ref = refs[n_parts + 6 :]
    rows = hidden_ref.shape[0]
    tall = block_ref.shape[0]
    total = parts[0][:tall, :].astype(F32)
    for part in parts[1:]:
        total = total + part[:tall, :].astype(F32)
    gates = gates_ref[...]
    groups = MODEL_WIDTH // rows
    per = gates.shape[0] // groups
    lines = total[rows : rows + per] + total[rows + per : rows + 2 * per]
    grad_gates = jnp.concatenate(
        [lines[:, q * rows : (q + 1) * rows] for q in range(groups)], axis=0
    )
    grad_logits = gates * (grad_gates - jnp.sum(gates * grad_gates, axis=0, keepdims=True))
    coarse = grad_logits.astype(BF16)
    fine = (grad_logits - coarse.astype(F32)).astype(BF16)
    normed = block_ref[:rows, :]
    n_experts = gates.shape[0]
    small_ref[:n_experts, :] = dot(coarse, normed, 1, 0) + dot(fine, normed, 1, 0)
    upstream = total[:rows] + dot(coarse, router_t[...], 0, 0) + dot(fine, router_t[...], 0, 0)
    hidden = hidden_ref[...]
    factor = rms_factor(hidden)
    weighted = upstream * gain[...]
    middle = jnp.mean(weighted * hidden, axis=-1, keepdims=True)
    grad = cotangent_ref[...].astype(F32) + factor * (weighted - hidden * factor * factor * middle)
    grad_ref[...] = grad
    low_ref[...] = grad.astype(BF16)
    small_ref[n_experts:, :] = jnp.sum(upstream * hidden * factor, axis=0, keepdims=True)


def call(kernel, name, operands, out_shape, scratch_shapes=(), scalars=0):
    vmem = pl.BlockSpec(memory_space=pltpu.VMEM)
    smem = pl.BlockSpec(memory_space=pltpu.SMEM)
    return pl.pallas_call(
        kernel,
        out_shape=out_shape,
        in_specs=[smem] * scalars + [vmem] * (len(operands) - scalars),
        out_specs=[vmem] * len(out_shape),
        scratch_shapes=list(scratch_shapes),
        compiler_params=pltpu.CompilerParams(vmem_limit_bytes=48 * 1024 * 1024),
        cost_estimate=pl.CostEstimate(flops=1000, bytes_accessed=1000, transcendentals=0),
        name=name,
    )(*operands)


def local(
    tokens,
    segments,
    routes,
    norm_gain,
    w_query,
    key_weight,
    value_weight,
    w_output,
    moe_gain,
    w_router,
    w_gate,
    w_up,
    w_down,
    cotangent,
):
    local_rows = tokens.shape[0]
    length = segments.shape[0]
    n_experts = w_router.shape[1]
    capacity = local_rows * TOPK * 5 // (4 * n_experts)
    width_query = w_query.shape[1]
    width_key = key_weight.shape[1]
    n_row = lax.axis_size("row")
    n_head = lax.axis_size("head")
    n_outer = n_row // 4
    row_at = lax.axis_index("row")
    head_at = lax.axis_index("head")
    numbers = jnp.stack([row_at, head_at & 1]).astype(jnp.int32)

    routes_t = routes.T
    expert_index = jnp.arange(n_experts, dtype=jnp.int32)[:, None]
    chosen = jnp.any(routes_t[:, None, :] == expert_index[None], axis=0)
    t_index = jnp.arange(local_rows, dtype=jnp.int32)
    before = (t_index[:, None] < t_index[None, :]).astype(BF16)
    rank = dot(chosen.astype(BF16), before, 1, 0)
    slots = jnp.where(chosen & (rank < capacity), rank, -1.0)
    chosen = chosen.astype(F32)
    router_t = w_router.T
    head_number = head_at.astype(jnp.int32).reshape(1)

    line = n_outer == 4
    inner = [(i, i ^ 12) for i in range(4, 12)]
    outward = [(i, i ^ 4) for i in range(4, 12)]
    inward = [(i ^ 4, i) for i in range(4, 12)]

    def send(value, pairs):
        return lax.ppermute(value, "row", pairs)

    def share_of(weight):
        size = weight.shape[1] // 2
        return lax.dynamic_slice_in_dim(weight[0], (head_at & 1) * size, size, 0)

    tokens_full = [tokens] + [head_swap(tokens, k) for k in range(1, n_head)]

    gate_here, down_here = row_swap(share_of(w_gate), 2), row_swap(share_of(w_down), 2)
    gate_there = head_swap(gate_here, 1)
    up_size = w_up.shape[1] // 2
    up_low, up_high = row_swap(w_up[0, :up_size], 2), row_swap(w_up[0, up_size:], 2)

    if line:
        g_near, g_mid = row_swap(cotangent, 4), send(cotangent, inner)
    frequency = ROPE_BASE ** (-2.0 * jnp.arange(HEAD_SIZE // 2, dtype=F32) / HEAD_SIZE)
    angles = jnp.arange(length, dtype=F32)[:, None] * frequency[None, :]
    cosine, sine_part = jnp.cos(angles), jnp.sin(angles)
    cosine = jnp.concatenate([cosine] * 4, axis=1)
    sine_part = jnp.concatenate([-sine_part, sine_part] * 2, axis=1)
    seg_col, seg_row = segments[:, None], segments[None, :]
    gain_row, moe_gain_row = norm_gain[None], moe_gain[None]

    def shape(rows, columns, dtype=BF16):
        return jax.ShapeDtypeStruct((rows, columns), dtype)

    head_parts = [
        shape(local_rows, MODEL_WIDTH, F32),
        jax.ShapeDtypeStruct((n_head - 1, local_rows, MODEL_WIDTH), BF16),
    ]
    normed_full, queries, keys, values, mixed_heads, log_totals, part_own, part_other = call(
        functools.partial(attend_kernel, n_head),
        "attend",
        [head_number, *tokens_full, seg_col, seg_row, gain_row, w_query, key_weight, value_weight]
        + [w_output, cosine, sine_part],
        [shape(length, MODEL_WIDTH), shape(length, width_query)]
        + [shape(length, width_key)] * 2
        + [shape(length, width_query), shape(length, 128, F32), *head_parts],
        [pltpu.VMEM((length, MODEL_WIDTH), F32)],
        scalars=1,
    )

    def head_arrivals(other):
        return [head_swap(other[k - 1], k) for k in range(1, n_head)]

    if line:
        g_two, g_one = lax.optimization_barrier((g_mid, g_near, part_own))[:2]
        g_far, g_out = send(g_one, inner), send(g_two, outward)
        g_first = [row_swap(v, 1) for v in (cotangent, g_one)]
        part_other = after(part_other, g_near, g_mid, gate_there, down_here)
    arrived = head_arrivals(part_other)
    down_there = head_swap(after(down_here, arrived[0]), 1)
    if line:
        arrived[0] = after(arrived[0], g_far, g_out, up_low, *g_first)
    table_rows = -(-3 * n_experts * local_rows // MODEL_WIDTH // 16) * 16
    x_block, hidden, gates = call(
        functools.partial(hidden_kernel, n_head),
        "hidden",
        [tokens, part_own, *arrived, moe_gain_row, router_t, slots, chosen],
        [
            shape(local_rows + table_rows, MODEL_WIDTH),
            shape(local_rows, MODEL_WIDTH, F32),
            shape(n_experts, local_rows, F32),
        ],
    )
    weights = [w_gate, w_up, w_down, gate_here, gate_there, up_low, up_high, down_here, down_there]
    saved = None
    made = []

    def experts(chunk, block):
        nonlocal saved
        pair = (block, row_swap(block, 1))
        parts, saved = run_experts(
            numbers, pair, g_chunks[chunk], weights, saved, chunk, n_outer, capacity
        )
        made.append((parts[0], row_swap(parts[1], 1)))
        return parts[0]

    tall = x_block.shape[0]

    def near_parts(which, chunk):
        return [v[:tall] if which else v[tall:] for v in made[chunk]]

    def near(which, chunk):
        own, other = near_parts(which, chunk)
        return own.astype(F32) + other.astype(F32)

    if line:
        x_near, x_mid = row_swap(x_block, 4), send(x_block, inner)
        g_last = send(after(g_far, x_block), outward)
        g_slabs = [g_mid + g_out, g_far + g_last]
        g_chunks = [(cotangent, g_first[0]), (g_near, g_first[1])]
        g_chunks += [(v, row_swap(v, 1)) for v in g_slabs]
        mark = experts(0, x_block)
        x_near, x_mid = lax.optimization_barrier((x_near, x_mid, mark, g_last))[:2]
        x_far, x_out = send(x_near, inner), send(x_mid, outward)
        mark = experts(1, x_near)
        x_far, x_out = lax.optimization_barrier((x_far, x_out, mark))[:2]
        x_last = send(x_far, outward)
        mark = experts(2, x_mid + x_out)
        two = near(1, 2)
        out_two = send(two.astype(BF16), inward)
        experts(3, x_far + after(x_last, mark, two))
        three = near(1, 3)
        out_three = send(three.astype(BF16), inward)
        saved = lax.optimization_barrier((*saved, three))[:5]
        mid_two = send((two + out_two.astype(F32)).astype(BF16), inner)
        mid_three = send((three + out_three.astype(F32)).astype(BF16), inner)
        one = (near(1, 1) + mid_three.astype(F32)).astype(BF16)
        grad_sum = [*made[0], mid_two, row_swap(one, 4)]
        marks = [mid_three, grad_sum[-1], grad_sum[-1]]
    else:
        g_slabs = [cotangent] + [row_swap(cotangent, 4 * o) for o in range(1, n_outer)]
        g_chunks = [(v, row_swap(v, 1)) for v in g_slabs]
        for o in range(n_outer):
            experts(o, row_swap(x_block, 4 * o) if o else x_block)
        grad_sum = list(made[0])
        for o in range(1, n_outer):
            grad_sum.append(row_swap(near(1, o).astype(BF16), 4 * o))
        marks = [grad_sum[-1]] * 3

    rows_in, gprod, inner_act, dgate, dup = saved

    def expert_grads(lhs, rhs, axis):
        sizes = [lhs.shape[2], rhs.shape[2]]
        part = list(sizes)
        part[axis] //= n_head
        return call(
            functools.partial(expert_grads_kernel, n_head, axis),
            "expert_grads",
            [head_number, lhs, rhs],
            [
                jax.ShapeDtypeStruct((2, *part), F32),
                jax.ShapeDtypeStruct((n_head - 1, 2, *part), BF16),
            ],
            [pltpu.VMEM(tuple(sizes), F32)],
            scalars=1,
        )

    expert_parts = [
        expert_grads(inner_act, gprod, 1),
        expert_grads(rows_in, dup, 0),
        expert_grads(rows_in, dgate, 0),
    ]
    expert_first = [
        [head_swap(expert_parts[i][1][k - 1], k) for k in range(1, n_head)] if i != 1 else
        [row_swap(expert_parts[i][0][1].astype(BF16), 2), row_swap(expert_parts[i][1][:, 1], 2)]
        for i in range(3)
    ]

    grad_hidden, grad_attention, early = call(
        functools.partial(grad_hidden_kernel, len(grad_sum)),
        "grad_hidden",
        [*grad_sum, hidden, moe_gain_row, router_t, gates, x_block, cotangent],
        [
            shape(local_rows, MODEL_WIDTH, F32),
            shape(local_rows, MODEL_WIDTH),
            shape(n_experts + 1, MODEL_WIDTH, F32),
        ],
    )
    def expert_sum(i):
        own, other = expert_parts[i]
        first = [after(v, marks[i]) for v in expert_first[i]]
        if i != 1:
            both = own
            for part in first:
                both = both + part.astype(F32)
            return both[0], [row_swap(both[1].astype(BF16), 2)]
        mine = own[0] + first[0].astype(F32)
        rest = other[:, 0].astype(F32) + first[1].astype(F32)
        rest = after(rest, grad_arrived[0])
        return mine, [head_swap(rest[k - 1].astype(BF16), k) for k in range(1, n_head)]

    grad_arrived = [head_swap(grad_attention, k) for k in range(1, n_head)]
    expert_last = [expert_sum(i) for i in range(3)]
    if line:
        two_out, three_out = near(0, 2), near(0, 3)
        low = [v.astype(BF16) for v in (two_out, three_out)]
        low = lax.optimization_barrier((*low, grad_attention))[:2]
        out_two, out_three = send(low[0], inward), send(low[1], inward)
    grad_arrived[0] = after(grad_arrived[0], *expert_last[0][1], *expert_last[2][1])
    grad_full, grad_proj, grad_own, grad_other, gain_part = call(
        functools.partial(attend_back_kernel, n_head),
        "attend_back",
        [head_number, *tokens_full, grad_attention]
        + grad_arrived
        + [seg_col, seg_row, w_query, key_weight, value_weight, w_output, cosine, sine_part]
        + [queries, keys, values, log_totals],
        [
            shape(length, MODEL_WIDTH),
            shape(length, width_query + 2 * width_key),
            *head_parts,
            shape(1, MODEL_WIDTH, F32),
        ],
        [
            pltpu.VMEM((length, width_query), BF16),
            pltpu.VMEM((length, width_query), F32),
            pltpu.VMEM((width_key, length), F32),
            pltpu.VMEM((width_key, length), F32),
            pltpu.VMEM((length, MODEL_WIDTH), F32),
        ],
        scalars=1,
    )
    grad_other = after(grad_other, *expert_last[1][1])
    if line:
        out_two, out_three = lax.optimization_barrier((out_two, out_three, grad_proj))[:2]
        mid_two = send((two_out + out_two.astype(F32)).astype(BF16), inner)
        mid_three = send((three_out + out_three.astype(F32)).astype(BF16), inner)

    share = MODEL_WIDTH // n_row
    width_all = width_query + 2 * width_key
    weights_own, weights_other = call(
        functools.partial(weight_grads_kernel, share),
        "weight_grads",
        [(row_at % 2).astype(jnp.int32).reshape(1), normed_full, grad_proj, grad_full, mixed_heads],
        [
            shape(MODEL_WIDTH // 2, width_all + width_query, F32),
            shape(MODEL_WIDTH // 2, width_all + width_query),
        ],
        [pltpu.VMEM((MODEL_WIDTH, width_all + width_query), F32)],
        scalars=1,
    )
    (grad_tokens,) = call(
        functools.partial(final_kernel, n_head),
        "final",
        [tokens, grad_hidden, gain_row, grad_own, *head_arrivals(grad_other)],
        [shape(local_rows, MODEL_WIDTH, F32)],
    )

    def row_half(own, other):
        value = own + row_swap(other, 1).astype(F32)
        value = value.reshape(n_outer, 2, share, -1)
        bit = (row_at // 2) % 2
        other = lax.dynamic_index_in_dim(value, 1 - bit, 1, keepdims=False).astype(BF16)
        value = lax.dynamic_index_in_dim(value, bit, 1, keepdims=False)
        return value, other

    def row_rest(value, arrived):
        value = value + arrived.astype(F32)
        at = row_at // 4
        total = lax.dynamic_index_in_dim(value, at, 0, keepdims=False)
        for o in range(1, n_outer):
            part = lax.dynamic_index_in_dim(value, at ^ o, 0, keepdims=False)
            total = total + row_swap(part.astype(BF16), 4 * o).astype(F32)
        return total

    small = jnp.concatenate([early, gain_part], axis=0)
    small = small + row_swap(small, 1)
    weights_half, weights_other = row_half(weights_own, weights_other)
    small = after(small, weights_other)
    weights_arrived = row_swap(weights_other, 2)
    small = small + row_swap(small, 2)
    weights_sum = row_rest(weights_half, weights_arrived)
    offset = 4
    while offset < n_row:
        small = small + row_swap(small, offset)
        offset *= 2
    offset = 1
    while offset < n_head:
        small = small + head_swap(small, offset)
        offset *= 2

    if line:
        one = near(0, 1) + after(mid_three, weights_other).astype(F32)
        out_sum = near_parts(0, 0) + [mid_two, row_swap(one.astype(BF16), 4)]
    else:
        out_sum = near_parts(0, 0)
        for o in range(1, n_outer):
            out_sum.append(row_swap(near(0, o).astype(BF16), 4 * o))
    mixed_out = hidden
    for part in out_sum:
        mixed_out = mixed_out + part.astype(F32)
    mixed_out = mixed_out.astype(BF16)
    down_sum, up_sum, gate_sum = (
        mine + sum(v.astype(F32) for v in rest) for mine, rest in expert_last
    )
    return (
        mixed_out,
        grad_tokens,
        small[n_experts + 1],
        weights_sum[:, :width_query],
        weights_sum[:, width_query : width_query + width_key],
        weights_sum[:, width_query + width_key : width_all],
        weights_sum[:, width_all:].T,
        small[n_experts],
        small[:n_experts].T,
        gate_sum[None],
        up_sum[None],
        down_sum[None],
    )


def solution(mesh):
    in_specs = (
        P(("row", "head"), None),
        P("row"),
        P(("row", "head"), None),
        P(),
        P(None, "head"),
        P(None, "head"),
        P(None, "head"),
        P("head", None),
        P(),
        P(),
        P("row", None, None),
        P("row", None, None),
        P("row", None, None),
        P(("row", "head"), None),
    )
    out_specs = (
        P(("row", "head"), None),
        P(("row", "head"), None),
        P(),
        P("row", "head"),
        P("row", "head"),
        P("row", "head"),
        P("head", "row"),
        P(),
        P(),
        P("row", "head", None),
        P("row", "head", None),
        P("row", None, "head"),
    )
    return jax.shard_map(local, mesh=mesh, in_specs=in_specs, out_specs=out_specs, check_vma=False)
```

```python
import functools

import jax
import jax.numpy as jnp
from jax import lax
from jax.experimental import pallas as pl
from jax.experimental.pallas import tpu as pltpu
from jax.sharding import PartitionSpec as P

MODEL_WIDTH = 1024
HEAD_SIZE = 64
VMEM_BYTES = 36 * 1024 * 1024
VMEM_ALL = 63 * 1024 * 1024
TOPK = 8

EPSILON = 1e-06
ROPE_BASE = 10000.0
F32 = jnp.float32
BF16 = jnp.bfloat16


def row_swap(value, offset):
    size = lax.axis_size("row")
    return lax.ppermute(value, "row", [(i, i ^ offset) for i in range(size)])


def head_swap(value, offset):
    size = lax.axis_size("head")
    return lax.ppermute(value, "head", [(i, i ^ offset) for i in range(size)])


def dot(a, b, ca, cb, **kw):
    return lax.dot_general(a, b, (((ca,), (cb,)), ((), ())), preferred_element_type=F32, **kw)


def tie(*values):
    return lax.optimization_barrier(values)


def experts_kernel(tokens_here, capacity, per, plan, number_ref, *refs):
    sources, experts, rows_before, prior, handed_on = plan
    n_blocks, n_experts = len(sources), len(experts)
    emit = prior or n_experts == 2
    refs = list(refs)

    def pop(number):
        taken, refs[:] = refs[:number], refs[number:]
        return taken

    x_hbm = [pop(k) for k in sources]
    g_hbm = [pop(k) for k in sources]
    w_hbm = {e: pop(5 if e else 3) for e in experts}
    prior_hbm = pop(3) if prior else []
    if handed_on:
        pop(5)
    made_hbm = pop(n_blocks) if emit else pop(3)
    saved_hbm = pop(5)
    x_refs, g_refs = pop(n_blocks), pop(n_blocks)
    w_refs = {e: pop(3) for e in experts}
    made_refs = pop(n_blocks) if emit else pop(3)
    prior_refs = pop(3) if prior else []
    rows_ref, gprod_ref, inner_ref, dgate_ref, dup_ref = pop(5)
    pick_ref, g_rows_ref, in_sem, out_sem, saved_sem = pop(5)
    ids = (number_ref[0], number_ref[0] ^ 2)
    bit, flag = number_ref[1], number_ref[2]
    arrivals = []

    def load(source, target):
        i = len(arrivals)
        if len(source) == 2:
            for k in range(2):
                copy = pltpu.make_async_copy(source[k], target, in_sem.at[i])
                pl.when(flag == k)(copy.start)
        else:
            copy = pltpu.make_async_copy(source[0], target, in_sem.at[i])
            copy.start()
        arrivals.append(copy)
        return i

    def arrive(numbers):
        for i in numbers:
            arrivals[i].wait()

    def halves(gate, down, index):
        gate_w, _, down_w = w_refs[1]
        rows, depth = gate_w.shape[1] // 2, down_w.shape[1] // 2
        width = gate_w.shape[2]
        first = pl.ds(pl.multiple_of(index * rows, rows), rows)
        second = pl.ds(pl.multiple_of(index * depth, depth), depth)
        return (gate, gate_w.at[0, first, :]), [
            (down.at[k * depth : (k + 1) * depth, :], down_w.at[0, second, k * width : (k + 1) * width])
            for k in range(down_w.shape[2] // width)
        ]

    tokens_in = [[load(x_hbm[b], x_refs[b]), load(g_hbm[b], g_refs[b])] for b in range(n_blocks)]
    weights_in = {}
    for e in experts:
        gate_w, up_w, down_w = w_refs[e]
        if e == 0:
            weights_in[e] = [[load([h], v)] for h, v in zip(w_hbm[e], w_refs[e])]
        else:
            gate_near, gate_far, down_near, down_far, up_h = w_hbm[e]
            gate_here, down_here = halves(gate_near, down_near, bit)
            gate_there, down_there = halves(gate_far, down_far, 1 - bit)
            weights_in[e] = [
                [load([a], b) for a, b in pieces]
                for pieces in ([gate_here, gate_there], [(up_h, up_w)], down_here + down_there)
            ]
    prior_in = [load([h], v) for h, v in zip(prior_hbm, prior_refs)]
    saves = []

    def save(which, i):
        buffer = (rows_ref, gprod_ref, inner_ref, dgate_ref, dup_ref)[which]
        copy = pltpu.make_async_copy(
            buffer.at[i],
            saved_hbm[which].at[experts[i], pl.ds(rows_before, n_blocks * capacity)],
            saved_sem.at[which, i],
        )
        copy.start()
        saves.append(copy)

    groups = MODEL_WIDTH // tokens_here

    def place(number):
        return number % per, number // per

    def take(table, first, number):
        table_row, group = place(number)
        index = lax.broadcasted_iota(jnp.int32, table.shape, 0)
        line = jnp.sum(jnp.where(index == table_row + first, table, 0.0), axis=0, keepdims=True)
        picked = jnp.zeros((1, tokens_here), F32)
        for q in range(groups):
            part = line[:, q * tokens_here : (q + 1) * tokens_here]
            picked = picked + jnp.where(group == q, part, 0.0)
        return picked

    held = (0, 1) if emit else experts
    slot_index = lax.broadcasted_iota(jnp.int32, (capacity, tokens_here), 0).astype(F32)
    gate_slots = [[] for _ in experts]
    for b in range(n_blocks):
        arrive(tokens_in[b])
        table = x_refs[b][tokens_here:, :].astype(F32)
        for h, e in enumerate(held):
            pick = (slot_index == take(table, 2 * per, ids[e])).astype(F32)
            if e in experts:
                gate = take(table, 0, ids[e]) + take(table, per, ids[e])
                gate_slots[experts.index(e)].append(jnp.sum(pick * gate, axis=1, keepdims=True))
            pick_ref[b, h * capacity : (h + 1) * capacity, :] = pick.astype(BF16)
        first = held.index(experts[0]) * capacity
        pick = pick_ref[b, first : first + n_experts * capacity, :]
        at = slice(b * capacity, (b + 1) * capacity)
        rows = dot(pick, x_refs[b][:tokens_here, :], 1, 0).astype(BF16)
        g_rows = dot(pick, g_refs[b][...], 1, 0).astype(BF16)
        for i in range(n_experts):
            rows_ref[i, at, :] = rows[i * capacity : (i + 1) * capacity]
            g_rows_ref[i, at, :] = g_rows[i * capacity : (i + 1) * capacity]
    scaled, grad_rows, grad_gate = [], [], []
    if prior:
        arrive(prior_in)
        scaled.append(prior_refs[0][...])
        grad_rows.append(prior_refs[1][...])
        grad_gate.append(prior_refs[2][:, :1])
    for i, e in enumerate(experts):
        save(0, i)
        gate_slot = jnp.concatenate(gate_slots[i], axis=0)
        g_rows = g_rows_ref[i].astype(F32)
        gprod_ref[i] = (gate_slot * g_rows).astype(BF16)
        save(1, i)
        gate_w, up_w, down_w = w_refs[e]
        arrive(weights_in[e][0])
        gate_pre = dot(rows_ref[i], gate_w[0], 1, 0)
        arrive(weights_in[e][1])
        up_pre = dot(rows_ref[i], up_w[0], 1, 0)
        sigmoid = jax.nn.sigmoid(gate_pre)
        silu = gate_pre * sigmoid
        inner_ref[i] = (silu * up_pre).astype(BF16)
        save(2, i)
        arrive(weights_in[e][2])
        produced = dot(inner_ref[i], down_w[0], 1, 0).astype(BF16).astype(F32)
        grad_gate.append(jnp.sum(g_rows * produced, axis=1, keepdims=True))
        scaled.append((gate_slot * produced).astype(BF16))
        grad_inner = dot(gprod_ref[i], down_w[0], 1, 1)
        dgate_ref[i] = (
            grad_inner * up_pre * sigmoid * (1.0 + gate_pre * (1.0 - sigmoid))
        ).astype(BF16)
        save(3, i)
        dup_ref[i] = (grad_inner * silu).astype(BF16)
        save(4, i)
        grad_rows.append(
            (dot(dgate_ref[i], gate_w[0], 1, 1) + dot(dup_ref[i], up_w[0], 1, 1)).astype(BF16)
        )
    stores = []

    def store(i):
        copy = pltpu.make_async_copy(made_refs[i], made_hbm[i], out_sem.at[i])
        copy.start()
        stores.append(copy)

    if not emit:
        made_refs[0][...] = scaled[0]
        made_refs[1][...] = grad_rows[0]
        made_refs[2][...] = jnp.broadcast_to(grad_gate[0], made_refs[2].shape)
        for i in range(3):
            store(i)
    else:
        table_rows = x_refs[0].shape[0] - tokens_here
        tall = tokens_here + table_rows
        shape = (table_rows, MODEL_WIDTH)
        row_index = lax.broadcasted_iota(jnp.int32, shape, 0)
        lane_group = lax.broadcasted_iota(jnp.int32, shape, 1) // tokens_here
        for b in reversed(range(n_blocks)):
            at = slice(b * capacity, (b + 1) * capacity)
            pick = pick_ref[b]
            made = jnp.concatenate([grad_rows[0][at], grad_rows[1][at]], axis=0)
            made_refs[b][:tokens_here, :] = dot(pick, made, 0, 0).astype(BF16)
            table = jnp.zeros(shape, F32)
            for e in range(2):
                table_row, group = place(ids[e])
                picked = pick[e * capacity : (e + 1) * capacity].astype(F32)
                line = jnp.sum(picked * grad_gate[e][at], axis=0, keepdims=True)
                coarse = line.astype(BF16).astype(F32)
                here = lane_group == group
                for first, part in ((0, coarse), (per, line - coarse)):
                    wide = jnp.concatenate([part] * groups, axis=1)
                    table = table + jnp.where(here & (row_index == table_row + first), wide, 0.0)
            made_refs[b][tokens_here:tall, :] = table.astype(BF16)
            made = jnp.concatenate([scaled[0][at], scaled[1][at]], axis=0)
            made_refs[b][tall:, :] = dot(pick, made, 0, 0).astype(BF16)
            store(b)
    for copy in saves + stores:
        copy.wait()


def run_experts(numbers, x_blocks, g_blocks, weights, experts, saved, first, total, capacity, prior=()):
    tokens_here = g_blocks[0][0].shape[0]
    block_rows = x_blocks[0][0].shape[0]
    width = weights[0].shape[2]
    n_blocks, n_here = len(x_blocks), len(experts)
    rows = n_blocks * capacity
    per = lax.axis_size("row") * tokens_here // MODEL_WIDTH
    emit = bool(prior) or n_here == 2
    sources = tuple(len(v) for v in x_blocks)
    plan = (sources, tuple(experts), first, bool(prior), saved is not None)
    hbm = pl.BlockSpec(memory_space=pltpu.HBM)
    if emit:
        made = [jax.ShapeDtypeStruct((tokens_here + block_rows, MODEL_WIDTH), BF16)] * n_blocks
    else:
        made = [jax.ShapeDtypeStruct((rows, MODEL_WIDTH), BF16)] * 2
        made.append(jax.ShapeDtypeStruct((rows, 128), F32))
    kept = [jax.ShapeDtypeStruct((2, total, MODEL_WIDTH), BF16)] * 2
    kept += [jax.ShapeDtypeStruct((2, total, width), BF16)] * 3
    operands = [w for v in (*x_blocks, *g_blocks) for w in v]
    for e in experts:
        operands += weights[3:] if e else weights[:3]
    operands += prior
    handed = 1 + len(operands)
    aliases = {}
    if saved is not None:
        operands += saved
        aliases = {handed + i: len(made) + i for i in range(5)}
    results = pl.pallas_call(
        functools.partial(experts_kernel, tokens_here, capacity, per, plan),
        out_shape=made + kept,
        in_specs=[pl.BlockSpec(memory_space=pltpu.SMEM)] + [hbm] * len(operands),
        out_specs=[hbm] * (len(made) + 5),
        scratch_shapes=[pltpu.VMEM(v[0].shape, BF16) for v in (*x_blocks, *g_blocks)]
        + [pltpu.VMEM(v.shape, BF16) for _ in experts for v in weights[:3]]
        + [pltpu.VMEM(v.shape, v.dtype) for v in made]
        + [pltpu.VMEM(v.shape, v.dtype) for v in prior]
        + [pltpu.VMEM((n_here, rows, MODEL_WIDTH), BF16)] * 2
        + [pltpu.VMEM((n_here, rows, width), BF16)] * 3
        + [
            pltpu.VMEM((n_blocks, (2 if emit else 1) * capacity, tokens_here), BF16),
            pltpu.VMEM((n_here, rows, MODEL_WIDTH), BF16),
            pltpu.SemaphoreType.DMA((2 * n_blocks + 14,)),
            pltpu.SemaphoreType.DMA((len(made),)),
            pltpu.SemaphoreType.DMA((5, n_here)),
        ],
        input_output_aliases=aliases,
        compiler_params=pltpu.CompilerParams(vmem_limit_bytes=VMEM_ALL),
        cost_estimate=pl.CostEstimate(flops=1000, bytes_accessed=1000, transcendentals=0),
        name="experts",
    )(numbers, *operands)
    return list(results[: len(made)]), list(results[len(made) :])


def swap_halves(values):
    width = values.shape[1]
    half = HEAD_SIZE // 2
    lane = lax.broadcasted_iota(jnp.int32, values.shape, 1)
    return jnp.where(
        lane % HEAD_SIZE < half,
        pltpu.roll(values, width - half, 1),
        pltpu.roll(values, half, 1),
    )


def turn(values, cosine, sine_part):
    times = values.shape[1] // cosine.shape[1]
    wide = [jnp.concatenate([v] * times, axis=1) for v in (cosine, sine_part)]
    return values * wide[0] + swap_halves(values) * wide[1]


def rms_factor(values):
    return lax.rsqrt(jnp.mean(values * values, axis=-1, keepdims=True) + EPSILON)


def block_bias(seg_col_ref, seg_row_ref, first, rows, keys):
    queries = lax.broadcasted_iota(jnp.int32, (rows, keys), 0) + first
    at = lax.broadcasted_iota(jnp.int32, (rows, keys), 1)
    same = seg_col_ref[first : first + rows, :] == seg_row_ref[:, :keys]
    return jnp.where(same & (at <= queries), 0.0, -1e30)


def head_lanes(number):
    return slice(number * HEAD_SIZE, (number + 1) * HEAD_SIZE)


def attend_kernel(n_head, head_ref, *refs):
    token_refs = refs[:n_head]
    seg_col, seg_row, gain, w_q, w_k, w_v, w_o, cos_ref, sin_ref = refs[n_head : n_head + 9]
    normed_ref, q_ref, k_ref, v_ref, mixed_ref, lse_ref, own_ref, other_ref = refs[n_head + 9 : n_head + 17]
    part_ref = refs[n_head + 17]
    rows = token_refs[0].shape[0]
    head_at = head_ref[0]
    scale = HEAD_SIZE ** (-0.5)
    for k in range(n_head):
        x = token_refs[k][...].astype(F32)
        at = pl.ds(pl.multiple_of((head_at ^ k) * rows, rows), rows)
        normed_ref[at, :] = (x * rms_factor(x) * gain[...]).astype(BF16)
    normed = normed_ref[...]
    cosine, sine_part = cos_ref[...], sin_ref[...]
    q_ref[...] = (turn(dot(normed, w_q[...], 1, 0), cosine, sine_part).astype(BF16) * scale).astype(BF16)
    k_ref[...] = turn(dot(normed, w_k[...], 1, 0), cosine, sine_part).astype(BF16)
    v_ref[...] = dot(normed, w_v[...], 1, 0).astype(BF16)
    kv = k_ref.shape[1] // HEAD_SIZE
    per_group = q_ref.shape[1] // k_ref.shape[1]
    lane = lax.broadcasted_iota(jnp.int32, (rows, lse_ref.shape[1]), 1)
    for i in range(n_head):
        first, keys = i * rows, (i + 1) * rows
        bias = block_bias(seg_col, seg_row, first, rows, keys)
        log_totals = jnp.zeros((rows, lse_ref.shape[1]), F32)
        for j in range(kv):
            key = k_ref[:keys, head_lanes(j)]
            value = v_ref[:keys, head_lanes(j)]
            made = []
            for h in range(j * per_group, (j + 1) * per_group):
                scores = dot(q_ref[first:keys, head_lanes(h)], key, 1, 1) + bias
                highest = jnp.max(scores, axis=1, keepdims=True)
                exponent = jnp.exp(scores - highest)
                total = jnp.sum(exponent, axis=1, keepdims=True)
                log_totals = jnp.where(lane == h, highest + jnp.log(total), log_totals)
                probs = (exponent * (1.0 / total)).astype(BF16)
                made.append(dot(probs, value, 1, 0).astype(BF16))
            lanes = slice(j * per_group * HEAD_SIZE, (j + 1) * per_group * HEAD_SIZE)
            mixed_ref[first:keys, lanes] = jnp.concatenate(made, axis=1)
        lse_ref[first:keys, :] = log_totals
    part_ref[...] = dot(mixed_ref[...], w_o[...], 1, 0)
    own_ref[...] = part_ref[pl.ds(pl.multiple_of(head_at * rows, rows), rows), :]
    for k in range(1, n_head):
        at = pl.ds(pl.multiple_of((head_at ^ k) * rows, rows), rows)
        other_ref[k - 1] = part_ref[at, :].astype(BF16)


def attend_back_kernel(n_head, head_ref, *refs):
    token_refs, refs = refs[:n_head], refs[n_head:]
    grad_refs = refs[:n_head]
    seg_col, seg_row, w_q, w_k, w_v, w_o, cos_ref, sin_ref = refs[n_head : n_head + 8]
    q_ref, k_ref, v_ref, lse_ref = refs[n_head + 8 : n_head + 12]
    full_ref, proj_ref, own_ref, other_ref, gain_ref = refs[n_head + 12 : n_head + 17]
    gm_ref, dq_ref, dk_ref, dv_ref, part_ref = refs[n_head + 17 :]
    rows = grad_refs[0].shape[0]
    head_at = head_ref[0]
    scale = HEAD_SIZE ** (-0.5)
    for k in range(n_head):
        at = pl.ds(pl.multiple_of((head_at ^ k) * rows, rows), rows)
        full_ref[at, :] = grad_refs[k][...]
    gm_ref[...] = dot(full_ref[...], w_o[...], 1, 1).astype(BF16)
    cosine, sine_part = cos_ref[...], -sin_ref[...]
    kv = k_ref.shape[1] // HEAD_SIZE
    per_group = q_ref.shape[1] // k_ref.shape[1]
    dk_ref[...] = jnp.zeros(dk_ref.shape, F32)
    dv_ref[...] = jnp.zeros(dv_ref.shape, F32)
    for i in range(n_head):
        first, keys = i * rows, (i + 1) * rows
        bias = block_bias(seg_col, seg_row, first, rows, keys)
        for j in range(kv):
            key = k_ref[:keys, head_lanes(j)]
            value = v_ref[:keys, head_lanes(j)]
            made, dk, dv = [], 0.0, 0.0
            for h in range(j * per_group, (j + 1) * per_group):
                query = q_ref[first:keys, head_lanes(h)]
                grad = gm_ref[first:keys, head_lanes(h)]
                probs = jnp.exp(dot(query, key, 1, 1) + bias - lse_ref[first:keys, h : h + 1])
                grad_probs = dot(grad, value, 1, 1)
                middle = jnp.sum(probs * grad_probs, axis=1, keepdims=True)
                ds = (probs * (grad_probs - middle)).astype(BF16)
                made.append(dot(ds, key, 1, 0) * scale)
                dk = dk + dot(query, ds, 0, 0)
                dv = dv + dot(grad, probs.astype(BF16), 0, 0)
            lanes = slice(j * per_group * HEAD_SIZE, (j + 1) * per_group * HEAD_SIZE)
            dq_ref[first:keys, lanes] = jnp.concatenate(made, axis=1)
            dk_ref[head_lanes(j), :keys] += dk
            dv_ref[head_lanes(j), :keys] += dv
    width_q, width_k = q_ref.shape[1], k_ref.shape[1]
    proj_ref[:, :width_q] = turn(dq_ref[...], cosine, sine_part).astype(BF16)
    proj_ref[:, width_q : width_q + width_k] = turn(dk_ref[...].T, cosine, sine_part).astype(BF16)
    proj_ref[:, width_q + width_k :] = dv_ref[...].T.astype(BF16)
    part_ref[...] = (
        dot(proj_ref[:, :width_q], w_q[...], 1, 1)
        + dot(proj_ref[:, width_q : width_q + width_k], w_k[...], 1, 1)
        + dot(proj_ref[:, width_q + width_k :], w_v[...], 1, 1)
    )
    gain = jnp.zeros(gain_ref.shape, F32)
    for k in range(n_head):
        part = part_ref[pl.ds(pl.multiple_of((head_at ^ k) * rows, rows), rows), :]
        x = token_refs[k][...].astype(F32)
        gain = gain + jnp.sum(part * (x * rms_factor(x)), axis=0, keepdims=True)
        if k:
            other_ref[k - 1] = part.astype(BF16)
        else:
            own_ref[...] = part
    gain_ref[...] = gain


def weight_grads_kernel(share, core_ref, normed_ref, proj_ref, full_ref, mixed_ref, own_ref, other_ref, all_ref):
    core = core_ref[0]
    width = proj_ref.shape[1]
    all_ref[:, :width] = dot(normed_ref[...], proj_ref[...], 0, 0)
    all_ref[:, width:] = dot(full_ref[...], mixed_ref[...], 0, 0)
    for m in range(own_ref.shape[0] // share):
        at = slice(m * share, (m + 1) * share)
        own = pl.ds(pl.multiple_of((2 * m + core) * share, share), share)
        other = pl.ds(pl.multiple_of((2 * m + 1 - core) * share, share), share)
        own_ref[at, :] = all_ref[own, :]
        other_ref[at, :] = all_ref[other, :].astype(BF16)


def expert_grads_kernel(n_head, axis, heads_first, head_ref, lhs_ref, rhs_ref, *refs):
    head_at = head_ref[0]
    own_ref, rest_ref, first_ref, second_ref, all_ref = refs
    size = own_ref.shape[axis]
    for e in range(2):
        all_ref[...] = dot(lhs_ref[e], rhs_ref[e], 0, 0)
        for k in range(n_head):
            at = pl.ds(pl.multiple_of((head_at ^ k) * size, size), size)
            part = all_ref[at, :] if axis == 0 else all_ref[:, at]
            if e == 0 and k == 0:
                own_ref[...] = part
            elif heads_first:
                if k:
                    (second_ref if e else first_ref)[k - 1] = part.astype(BF16)
                else:
                    rest_ref[0] = part
            elif e:
                if k:
                    second_ref[k - 1] = part.astype(BF16)
                else:
                    first_ref[0] = part.astype(BF16)
            else:
                rest_ref[k - 1] = part


def final_kernel(n_head, tokens_ref, grad_hidden_ref, gain, own_ref, *refs):
    total = own_ref[...]
    for part in refs[: n_head - 1]:
        total = total + part[...].astype(F32)
    x = tokens_ref[...].astype(F32)
    factor = rms_factor(x)
    weighted = total * gain[...]
    middle = jnp.mean(weighted * x, axis=-1, keepdims=True)
    refs[-1][...] = grad_hidden_ref[...] + factor * (weighted - x * factor * factor * middle)


def hidden_kernel(n_head, tokens_ref, own_ref, *refs):
    arrived = refs[: n_head - 1]
    gain, router_t, slots_ref, chosen_ref = refs[n_head - 1 : n_head + 3]
    block_ref, hidden_ref, gates_ref = refs[n_head + 3 :]
    rows = tokens_ref.shape[0]
    attention = own_ref[...]
    for part in arrived:
        attention = attention + part[...].astype(F32)
    hidden = tokens_ref[...].astype(F32) + attention
    hidden_ref[...] = hidden
    normed = (hidden * rms_factor(hidden) * gain[...]).astype(BF16)
    block_ref[:rows, :] = normed
    chosen = chosen_ref[...] > 0.0
    logits = jnp.where(chosen, dot(router_t[...], normed, 1, 1), -1e30)
    gates = jnp.where(chosen, jnp.exp(logits - jnp.max(logits, axis=0, keepdims=True)), 0.0)
    gates = gates / jnp.sum(gates, axis=0, keepdims=True)
    gates_ref[...] = gates
    coarse = gates.astype(BF16).astype(F32)
    groups = MODEL_WIDTH // rows
    per = gates.shape[0] // groups
    lines = [
        jnp.concatenate([v[q * per : (q + 1) * per] for q in range(groups)], axis=1)
        for v in (coarse, gates - coarse, slots_ref[...])
    ]
    spare = block_ref.shape[0] - rows - 3 * per
    if spare:
        lines.append(jnp.zeros((spare, MODEL_WIDTH), F32))
    block_ref[rows:, :] = jnp.concatenate(lines, axis=0).astype(BF16)


def grad_hidden_kernel(n_parts, *refs):
    parts = refs[:n_parts]
    hidden_ref, gain, router_t, gates_ref, block_ref, cotangent_ref = refs[n_parts : n_parts + 6]
    grad_ref, low_ref, small_ref = refs[n_parts + 6 :]
    rows = hidden_ref.shape[0]
    tall = block_ref.shape[0]
    total = parts[0][:tall, :].astype(F32)
    for part in parts[1:]:
        total = total + part[:tall, :].astype(F32)
    gates = gates_ref[...]
    groups = MODEL_WIDTH // rows
    per = gates.shape[0] // groups
    lines = total[rows : rows + per] + total[rows + per : rows + 2 * per]
    grad_gates = jnp.concatenate(
        [lines[:, q * rows : (q + 1) * rows] for q in range(groups)], axis=0
    )
    grad_logits = gates * (grad_gates - jnp.sum(gates * grad_gates, axis=0, keepdims=True))
    coarse = grad_logits.astype(BF16)
    fine = (grad_logits - coarse.astype(F32)).astype(BF16)
    normed = block_ref[:rows, :]
    n_experts = gates.shape[0]
    small_ref[:n_experts, :] = dot(coarse, normed, 1, 0) + dot(fine, normed, 1, 0)
    upstream = total[:rows] + dot(coarse, router_t[...], 0, 0) + dot(fine, router_t[...], 0, 0)
    hidden = hidden_ref[...]
    factor = rms_factor(hidden)
    weighted = upstream * gain[...]
    middle = jnp.mean(weighted * hidden, axis=-1, keepdims=True)
    grad = cotangent_ref[...].astype(F32) + factor * (weighted - hidden * factor * factor * middle)
    grad_ref[...] = grad
    low_ref[...] = grad.astype(BF16)
    small_ref[n_experts:, :] = jnp.sum(upstream * hidden * factor, axis=0, keepdims=True)


def call(kernel, name, operands, out_shape, scratch_shapes=(), scalars=0, room=VMEM_BYTES):
    vmem = pl.BlockSpec(memory_space=pltpu.VMEM)
    smem = pl.BlockSpec(memory_space=pltpu.SMEM)
    made = pl.pallas_call(
        kernel,
        out_shape=out_shape,
        in_specs=[smem] * scalars + [vmem] * (len(operands) - scalars),
        out_specs=[vmem] * len(out_shape),
        scratch_shapes=list(scratch_shapes),
        compiler_params=pltpu.CompilerParams(vmem_limit_bytes=room),
        cost_estimate=pl.CostEstimate(flops=1000, bytes_accessed=1000, transcendentals=0),
        name=name,
    )(*operands)
    return list(made)


def local(
    tokens,
    segments,
    routes,
    norm_gain,
    w_query,
    key_weight,
    value_weight,
    w_output,
    moe_gain,
    w_router,
    w_gate,
    w_up,
    w_down,
    cotangent,
):
    local_rows = tokens.shape[0]
    length = segments.shape[0]
    n_experts = w_router.shape[1]
    capacity = local_rows * TOPK * 5 // (4 * n_experts)
    width_query = w_query.shape[1]
    width_key = key_weight.shape[1]
    n_row = lax.axis_size("row")
    n_head = lax.axis_size("head")
    n_outer = n_row // 4
    row_at = lax.axis_index("row")
    head_at = lax.axis_index("head")
    at_end = (row_at // 4 % 3 == 0).astype(jnp.int32)
    numbers = jnp.stack([row_at, head_at & 1, at_end]).astype(jnp.int32)

    routes_t = routes.T
    expert_index = jnp.arange(n_experts, dtype=jnp.int32)[:, None]
    chosen = jnp.any(routes_t[:, None, :] == expert_index[None], axis=0)
    t_index = jnp.arange(local_rows, dtype=jnp.int32)
    before = (t_index[:, None] < t_index[None, :]).astype(BF16)
    rank = dot(chosen.astype(BF16), before, 1, 0)
    slots = jnp.where(chosen & (rank < capacity), rank, -1.0)
    chosen = chosen.astype(F32)
    router_t = w_router.T
    head_number = head_at.astype(jnp.int32).reshape(1)

    line = n_outer == 4
    inner = [(i, i ^ 12) for i in range(4, 12)]
    outward = [(i, i ^ 4) for i in range(4, 12)]
    inward = [(i ^ 4, i) for i in range(4, 12)]

    def send(value, pairs):
        return lax.ppermute(value, "row", pairs)

    def share_of(weight):
        size = weight.shape[1] // 2
        return lax.dynamic_slice_in_dim(weight[0], (head_at & 1) * size, size, 0)

    def head_all(values):
        return [head_swap(values[k - 1], k) for k in range(1, n_head)]

    def low(value):
        return value.astype(BF16)

    def shape(rows, columns, dtype=BF16):
        return jax.ShapeDtypeStruct((rows, columns), dtype)

    seg_col, seg_row = segments[:, None], segments[None, :]
    gain_row, moe_gain_row = norm_gain[None], moe_gain[None]

    tokens_other = head_all([tokens] * (n_head - 1))
    frequency = ROPE_BASE ** (-2.0 * jnp.arange(HEAD_SIZE // 2, dtype=F32) / HEAD_SIZE)
    angles = jnp.arange(length, dtype=F32)[:, None] * frequency[None, :]
    cosine, sine_part = jnp.cos(angles), jnp.sin(angles)
    cosine = jnp.concatenate([cosine] * 4, axis=1)
    sine_part = jnp.concatenate([-sine_part, sine_part] * 2, axis=1)
    gate_share, down_share = share_of(w_gate), share_of(w_down)
    width = gate_share.shape[1]
    pieces = [down_share[:, k : k + width] for k in range(0, down_share.shape[1], width)]
    gate_here = row_swap(gate_share, 2)
    down_here = row_swap(jnp.concatenate(pieces, axis=0), 2)
    if line:
        g_far = [row_swap(cotangent, 4), send(cotangent, inner)]
    else:
        g_far = [row_swap(cotangent, 4 * o) for o in range(1, n_outer)]
    tokens_other, cosine, sine_part, seg_col, slots, chosen = tie(
        tokens_other, cosine, sine_part, seg_col, slots, chosen
    )
    g_far, w_up_later, _ = tie(g_far, w_up, seg_col)

    g_slabs = [cotangent, *g_far]
    if line:
        g_far += [send(g_far[1], outward), send(g_far[0], inner)]
    head_parts = [
        shape(local_rows, MODEL_WIDTH, F32),
        jax.ShapeDtypeStruct((n_head - 1, local_rows, MODEL_WIDTH), BF16),
    ]
    normed_full, queries, keys, values, mixed_heads, log_totals, part_own, part_other = call(
        functools.partial(attend_kernel, n_head),
        "attend",
        [head_number, tokens, *tokens_other, seg_col, seg_row, gain_row]
        + [w_query, key_weight, value_weight, w_output, cosine, sine_part],
        [shape(length, MODEL_WIDTH), shape(length, width_query)]
        + [shape(length, width_key)] * 2
        + [shape(length, width_query), shape(length, 128, F32), *head_parts],
        [pltpu.VMEM((length, MODEL_WIDTH), F32)],
        scalars=1,
        room=VMEM_ALL,
    )
    part_other, part_own, gate_here, down_here, g_far, w_up_later = tie(
        part_other, part_own, gate_here, down_here, g_far, w_up_later
    )

    arrived = head_all(part_other)
    up_here = row_swap(w_up_later, 2)
    g_last = send(g_far[3], outward) if line else cotangent
    arrived, part_own, g_last = tie(arrived, part_own, g_last)
    table_rows = -(-3 * n_experts * local_rows // MODEL_WIDTH // 16) * 16
    x_block, hidden, gates = call(
        functools.partial(hidden_kernel, n_head),
        "hidden",
        [tokens, part_own, *arrived, moe_gain_row, router_t, slots, chosen],
        [
            shape(local_rows + table_rows, MODEL_WIDTH),
            shape(local_rows, MODEL_WIDTH, F32),
            shape(n_experts, local_rows, F32),
        ],
    )
    tall = x_block.shape[0]
    saved = None
    made = []

    def cores(values):
        return [row_swap(v, 1) for v in values]

    def pass_on(chunk):
        made[chunk][1] = row_swap(made[chunk][1], 1)

    def near(which, chunk):
        own, other = (v[:tall] if which else v[tall:] for v in made[chunk])
        return own.astype(F32) + other.astype(F32)

    def experts(x_blocks, g_blocks, which, prior=()):
        nonlocal saved
        first = 2 * len(made) * capacity
        results, saved = run_experts(
            numbers, x_blocks, g_blocks, weights, which, saved, first, total_rows, capacity, prior
        )
        if which == (0,):
            return results
        made.extend(results[i : i + 2] for i in range(0, len(results), 2))

    total_rows = 2 * n_outer * capacity
    gate_there = head_swap(gate_here, 1)
    x_core = row_swap(x_block, 1)
    if line:
        x_far = [row_swap(x_block, 4), send(x_block, inner)]
    else:
        x_far = [row_swap(x_block, 4 * o) for o in range(1, n_outer)]
    x_block, x_core, x_far, up_here, gate_there, down_later, g_slabs, g_far, g_last, cotangent = tie(
        x_block, x_core, x_far, up_here, gate_there, down_here, g_slabs, g_far, g_last, cotangent
    )
    down_there = head_swap(down_later, 1)
    weights = [w_gate, w_up, w_down, gate_here, gate_there, down_here, down_there, up_here]

    if line:
        x_near, x_mid = x_far
        x_near_core = row_swap(x_near, 1)
        g_cores = cores(g_slabs[:2])
        x_near, x_mid, x_near_core, g_cores, g_far = tie(x_near, x_mid, x_near_core, g_cores, g_far)
        x_out, x_deep = send(x_mid, outward), send(x_near, inner)
        x_pairs = [[x_block], [x_core], [x_near], [x_near_core]]
        g_pairs = [[cotangent], [g_cores[0]], [g_slabs[1]], [g_cores[1]]]
        prior = experts(x_pairs, g_pairs, (0,))
        x_out, x_deep, prior, saved, down_there, g_far, x_mid, g_mid, g_last = tie(
            x_out, x_deep, prior, saved, down_there, g_far, x_mid, g_slabs[2], g_last
        )
        weights[6] = down_there
        x_last = send(x_deep, outward)
        x_mid_core, g_mid_core, g_out_core = cores([x_mid, g_mid, g_far[2]])
        experts(x_pairs, g_pairs, (1,), prior)
        x_last, x_mid_core, g_mid_core, g_out_core, made[0], made[1], saved, x_out = tie(
            x_last, x_mid_core, g_mid_core, g_out_core, made[0], made[1], saved, x_out
        )
        x_out_core = row_swap(x_out, 1)
        x_out_core, x_last, x_deep, g_deep, g_last = tie(x_out_core, x_last, x_deep, g_far[3], g_last)
        x_deep_core, x_last_core, g_deep_core, g_last_core = cores([x_deep, x_last, g_deep, g_last])
        g_two = [[g_mid, g_far[2]], [g_mid_core, g_out_core]]
        experts([[x_mid, x_out], [x_mid_core, x_out_core]], g_two, (0, 1))
        x_deep_core, x_last_core, g_deep_core, g_last_core, made[0], made[1], made[2], saved = tie(
            x_deep_core, x_last_core, g_deep_core, g_last_core, made[0], made[1], made[2], saved
        )
        pass_on(2)
        made[2], made[0], made[1] = tie(made[2], made[0], made[1])
        two = near(1, 2)
        pass_on(1)
        out_two = send(low(two), inward)
        g_three = [[g_deep, g_last], [g_deep_core, g_last_core]]
        experts([[x_deep, x_last], [x_deep_core, x_last_core]], g_three, (0, 1))
        made[1], made[3], saved, out_two = tie(made[1], made[3], saved, out_two)
        pass_on(3)
        made[3], saved, out_two = tie(made[3], saved, out_two)
        three = near(1, 3)
        out_three = send(low(three), inward)
        mid_two = send(low(two + out_two.astype(F32)), inner)
    else:
        for o, x in enumerate([x_block, *x_far]):
            experts([[x], [row_swap(x, 1)]], [[g_slabs[o]], [row_swap(g_slabs[o], 1)]], (0, 1))
        for o in range(n_outer):
            pass_on(o)
        one = [row_swap(low(near(1, o)), 4 * o) for o in range(1, n_outer)]

    rows_in, gprod, inner_act, dgate, dup = saved

    def expert_grads(lhs, rhs, axis, heads_first):
        sizes = [lhs.shape[2], rhs.shape[2]]
        part = list(sizes)
        part[axis] //= n_head
        others = (n_head - 1, *part)
        one = (1, *part)
        return call(
            functools.partial(expert_grads_kernel, n_head, axis, heads_first),
            "expert_grads",
            [head_number, lhs, rhs],
            [
                jax.ShapeDtypeStruct(tuple(part), F32),
                jax.ShapeDtypeStruct(one if heads_first else others, F32),
                jax.ShapeDtypeStruct(others if heads_first else one, BF16),
                jax.ShapeDtypeStruct(others, BF16),
            ],
            [pltpu.VMEM(tuple(sizes), F32)],
            scalars=1,
        )

    up_parts = expert_grads(rows_in, dup, 0, False)
    down_parts = expert_grads(inner_act, gprod, 1, True)
    up_first, up_second, down_first, down_second = (*up_parts[2:], *down_parts[2:])
    if line:
        out_three, mid_two, up_first, up_second, down_first, down_second, rows_in, dgate, made_now = tie(
            out_three, mid_two, up_first, up_second, down_first, down_second, rows_in, dgate, made
        )
        made = list(made_now)
        mid_three = send(low(three + out_three.astype(F32)), inner)
        two_out = near(0, 2)
        last_two = send(low(two_out), inward)
    up_first = row_swap(up_first, 2)
    down_first = head_all(down_first)
    gate_parts = expert_grads(rows_in, dgate, 0, False)
    gate_first, gate_second = gate_parts[2:]
    if line:
        mid_three, up_first, down_first, last_two, gate_first, made_now, up_second, down_second = tie(
            mid_three, up_first, down_first, last_two, gate_first, made, up_second, down_second
        )
        made = list(made_now)
        one = [mid_two, row_swap(low(near(1, 1) + mid_three.astype(F32)), 4)]
        pass_on(0)
        last_two = send(low(two_out + last_two.astype(F32)), inner)
    else:
        last_two = up_first
    up_second = row_swap(up_second, 2)
    down_second = head_all(down_second)
    one, up_second, down_second, made_now, last_two, gate_first, gate_second = tie(
        one, up_second, down_second, made, last_two, gate_first, gate_second
    )
    made = list(made_now)
    grad_sum = [*made[0], *one]
    grad_hidden, grad_attention, early = call(
        functools.partial(grad_hidden_kernel, len(grad_sum)),
        "grad_hidden",
        [*grad_sum, hidden, moe_gain_row, router_t, gates, x_block, cotangent],
        [
            shape(local_rows, MODEL_WIDTH, F32),
            shape(local_rows, MODEL_WIDTH),
            shape(n_experts + 1, MODEL_WIDTH, F32),
        ],
    )
    gate_first, made_now, up_first, up_second, down_first, down_second, grad_attention = tie(
        gate_first, made, up_first, up_second, down_first, down_second, grad_attention
    )
    made = list(made_now)
    grad_arrived = head_all([grad_attention] * (n_head - 1))
    gate_first = row_swap(gate_first, 2)
    last_three = low(near(0, 3)) if line else grad_attention
    up_rest = [low(v + w.astype(F32)) for v, w in zip(up_parts[1], up_second)]
    down_rest = low(down_parts[1][0] + sum(v.astype(F32) for v in down_second))
    grad_arrived, gate_first, last_three, up_rest, down_rest, gate_second, made_now = tie(
        grad_arrived, gate_first, last_three, up_rest, down_rest, gate_second, made
    )
    made = list(made_now)
    up_last = head_all(up_rest)
    gate_second = row_swap(gate_second, 2)
    if line:
        arrived_three = send(last_three, inward)
        three_later = near(0, 3)
    else:
        arrived_three = three_later = last_three
    grad_full, grad_proj, grad_own, grad_other, gain_part = call(
        functools.partial(attend_back_kernel, n_head),
        "attend_back",
        [head_number, tokens, *tokens_other, grad_attention, *grad_arrived, seg_col, seg_row]
        + [w_query, key_weight, value_weight, w_output, cosine, sine_part]
        + [queries, keys, values, log_totals],
        [
            shape(length, MODEL_WIDTH),
            shape(length, width_query + 2 * width_key),
            *head_parts,
            shape(1, MODEL_WIDTH, F32),
        ],
        [
            pltpu.VMEM((length, width_query), BF16),
            pltpu.VMEM((length, width_query), F32),
            pltpu.VMEM((width_key, length), F32),
            pltpu.VMEM((width_key, length), F32),
            pltpu.VMEM((length, MODEL_WIDTH), F32),
        ],
        scalars=1,
        room=VMEM_ALL,
    )
    grad_full, grad_proj, grad_other, gain_part, up_last, gate_second, arrived_three, down_rest = tie(
        grad_full, grad_proj, grad_other, gain_part, up_last, gate_second, arrived_three, down_rest
    )
    share = MODEL_WIDTH // n_row
    width_all = width_query + 2 * width_key
    small = jnp.concatenate([early, gain_part], axis=0)
    weights_own, weights_other = call(
        functools.partial(weight_grads_kernel, share),
        "weight_grads",
        [(row_at % 2).astype(jnp.int32).reshape(1), normed_full, grad_proj, grad_full, mixed_heads],
        [
            shape(MODEL_WIDTH // 2, width_all + width_query, F32),
            shape(MODEL_WIDTH // 2, width_all + width_query),
        ],
        [pltpu.VMEM((MODEL_WIDTH, width_all + width_query), F32)],
        scalars=1,
        room=VMEM_ALL,
    )
    small_core = row_swap(small, 1)
    small, small_core, weights_own, weights_other, made_now = tie(
        small, small_core, weights_own, weights_other, made
    )
    made = list(made_now)
    small = small + small_core
    small_far = row_swap(small, 2)
    weights_core = row_swap(weights_other, 1)
    if line:
        last_three = send(low(three_later + arrived_three.astype(F32)), inner)
    small, small_far, weights_own, weights_core, grad_other, made_now = tie(
        small, small_far, weights_own, weights_core, grad_other, made
    )
    made = list(made_now)
    value = (weights_own + weights_core.astype(F32)).reshape(n_outer, 2, share, -1)
    bit = (row_at // 2) % 2
    other = low(lax.dynamic_index_in_dim(value, 1 - bit, 1, keepdims=False))
    value = lax.dynamic_index_in_dim(value, bit, 1, keepdims=False)
    small, other, value, grad_other, down_rest, gate_second, made_now = tie(
        small + small_far, other, value, grad_other, down_rest, gate_second, made
    )
    made = list(made_now)
    other_arrived = row_swap(other, 2)
    offset = 4
    while offset < n_row:
        small = small + row_swap(small, offset)
        offset *= 2
    offset = 1
    while offset < n_head:
        small = small + head_swap(small, offset)
        offset *= 2
    grad_arrived = head_all(grad_other)
    gate_rest = [low(v + w.astype(F32)) for v, w in zip(gate_parts[1], gate_second)]
    mixed_out = hidden + near(0, 0)
    if line:
        mixed_out = mixed_out + last_two.astype(F32)
        last = [low(near(0, 1) + last_three.astype(F32))]
    else:
        last = [low(near(0, o)) for o in range(1, n_outer)]
    grad_arrived, value, other_arrived, small, gate_rest, last, mixed_out, down_rest = tie(
        grad_arrived, value, other_arrived, small, gate_rest, last, mixed_out, down_rest
    )
    last = [row_swap(v, 4 * o + 4) for o, v in enumerate(last)]
    gate_last = head_all(gate_rest)
    value = value + other_arrived.astype(F32)
    at = row_at // 4
    weights_sum = lax.dynamic_index_in_dim(value, at, 0, keepdims=False)
    for o in range(1, n_outer):
        part = low(lax.dynamic_index_in_dim(value, at ^ o, 0, keepdims=False))
        weights_sum = weights_sum + row_swap(part, 4 * o).astype(F32)
    down_last = row_swap(down_rest, 2)
    (grad_tokens,) = call(
        functools.partial(final_kernel, n_head),
        "final",
        [tokens, grad_hidden, gain_row, grad_own, *grad_arrived],
        [shape(local_rows, MODEL_WIDTH, F32)],
    )
    for part in last:
        mixed_out = mixed_out + part.astype(F32)
    mixed_out = mixed_out.astype(BF16)

    def add(own, *parts):
        for part in parts:
            own = own + part.astype(F32)
        return own

    down_sum = add(down_parts[0], *down_first, down_last)
    up_sum = add(up_parts[0], up_first[0], *up_last)
    gate_sum = add(gate_parts[0], gate_first[0], *gate_last)
    return (
        mixed_out,
        grad_tokens,
        small[n_experts + 1],
        weights_sum[:, :width_query],
        weights_sum[:, width_query : width_query + width_key],
        weights_sum[:, width_query + width_key : width_all],
        weights_sum[:, width_all:].T,
        small[n_experts],
        small[:n_experts].T,
        gate_sum[None],
        up_sum[None],
        down_sum[None],
    )


def solution(mesh):
    in_specs = (
        P(("row", "head"), None),
        P("row"),
        P(("row", "head"), None),
        P(),
        P(None, "head"),
        P(None, "head"),
        P(None, "head"),
        P("head", None),
        P(),
        P(),
        P("row", None, None),
        P("row", None, None),
        P("row", None, None),
        P(("row", "head"), None),
    )
    out_specs = (
        P(("row", "head"), None),
        P(("row", "head"), None),
        P(),
        P("row", "head"),
        P("row", "head"),
        P("row", "head"),
        P("head", "row"),
        P(),
        P(),
        P("row", "head", None),
        P("row", "head", None),
        P("row", None, "head"),
    )
    return jax.shard_map(local, mesh=mesh, in_specs=in_specs, out_specs=out_specs, check_vma=False)
```

```python
import functools

import jax
import jax.numpy as jnp
from jax import lax
from jax.experimental import pallas as pl
from jax.experimental.pallas import tpu as pltpu
from jax.sharding import PartitionSpec as P

MODEL_WIDTH = 1024
HEAD_SIZE = 64
VMEM_BYTES = 36 * 1024 * 1024
VMEM_ALL = 63 * 1024 * 1024
TOPK = 8

EPSILON = 1e-06
ROPE_BASE = 10000.0
F32 = jnp.float32
BF16 = jnp.bfloat16


def row_swap(value, offset):
    size = lax.axis_size("row")
    return lax.ppermute(value, "row", [(i, i ^ offset) for i in range(size)])


def head_swap(value, offset):
    size = lax.axis_size("head")
    return lax.ppermute(value, "head", [(i, i ^ offset) for i in range(size)])


def dot(a, b, ca, cb, **kw):
    return lax.dot_general(a, b, (((ca,), (cb,)), ((), ())), preferred_element_type=F32, **kw)


def tie(*values):
    return lax.optimization_barrier(values)


def each(count, body):
    lax.fori_loop(0, count, lambda i, carry: (body(i), carry)[1], 0)


def experts_kernel(tokens_here, capacity, per, plan, number_ref, *refs):
    sources, experts, rows_before, prior, handed_on = plan
    n_blocks, n_experts = len(sources), len(experts)
    emit = prior or n_experts == 2
    refs = list(refs)

    def pop(number):
        taken, refs[:] = refs[:number], refs[number:]
        return taken

    x_hbm = [pop(k) for k in sources]
    g_hbm = [pop(k) for k in sources]
    w_hbm = {e: pop(5 if e else 3) for e in experts}
    prior_hbm = pop(3) if prior else []
    if handed_on:
        pop(5)
    made_hbm = pop(n_blocks) if emit else pop(3)
    saved_hbm = pop(5)
    x_ref, g_ref, gate_ref, up_ref, down_ref, made_ref = pop(6)
    rows_ref, gprod_ref, inner_ref, dgate_ref, dup_ref = pop(5)
    pick_ref, g_rows_ref, gate_pre_ref, up_pre_ref, slot_ref = pop(5)
    scaled_ref, back_ref, gate_grad_ref, in_sem, out_sem, saved_sem = pop(6)
    ids = (number_ref[0], number_ref[0] ^ 2)
    bit, flag = number_ref[1], number_ref[2]
    arrivals = []

    def load(source, target):
        i = len(arrivals)

        def copy(k=0):
            return pltpu.make_async_copy(source[k](), target(), in_sem.at[i])

        if len(source) == 2:
            for k in range(2):
                pl.when(flag == k)(copy(k).start)
        else:
            copy().start()
        arrivals.append(copy)
        return i

    def whole(ref, *index):
        return lambda: ref.at[index] if index else ref

    def arrive(at, numbers):
        for turn, mine in enumerate(numbers):

            def wait(mine=mine):
                for i in mine:
                    arrivals[i]().wait()

            pl.when(at == turn)(wait)

    width = gate_ref.shape[2]
    depth = down_ref.shape[1] // 2
    rows_half = gate_ref.shape[1] // 2

    def halves(gate, down, index, i):
        def first():
            return gate_ref.at[i, pl.ds(pl.multiple_of(index * rows_half, rows_half), rows_half)]

        def second(k):
            at = pl.ds(pl.multiple_of(index * depth, depth), depth)
            return lambda: down_ref.at[i, at, k * width : (k + 1) * width]

        def part(k):
            return lambda: down.at[k * depth : (k + 1) * depth]

        return (whole(gate), first), [(part(k), second(k)) for k in range(down_ref.shape[2] // width)]

    tokens_in = [
        [
            load([whole(h) for h in x_hbm[b]], whole(x_ref, b)),
            load([whole(h) for h in g_hbm[b]], whole(g_ref, b)),
        ]
        for b in range(n_blocks)
    ]
    gate_in, up_in, down_in = [], [], []
    for i, e in enumerate(experts):
        if e == 0:
            gate_in.append([load([whole(w_hbm[e][0], 0)], whole(gate_ref, i))])
            up_in.append([load([whole(w_hbm[e][1], 0)], whole(up_ref, i))])
            down_in.append([load([whole(w_hbm[e][2], 0)], whole(down_ref, i))])
        else:
            gate_near, gate_far, down_near, down_far, up_h = w_hbm[e]
            gate_here, down_here = halves(gate_near, down_near, bit, i)
            gate_there, down_there = halves(gate_far, down_far, 1 - bit, i)
            gate_in.append([load([a], b) for a, b in (gate_here, gate_there)])
            up_in.append([load([whole(up_h, 0)], whole(up_ref, i))])
            down_in.append([load([a], b) for a, b in down_here + down_there])
    if prior:
        prior_in = [
            load([whole(prior_hbm[0])], whole(scaled_ref, 0)),
            load([whole(prior_hbm[1])], whole(back_ref, 0)),
            load([whole(prior_hbm[2])], whole(gate_grad_ref, 0)),
        ]

    def saving(which, turn):
        buffer = (rows_ref, gprod_ref, inner_ref, dgate_ref, dup_ref)[which]
        return pltpu.make_async_copy(
            buffer.at[turn],
            saved_hbm[which].at[experts[turn], pl.ds(rows_before, n_blocks * capacity)],
            saved_sem.at[which, turn],
        )

    def save(which, i):
        for turn in range(n_experts):
            pl.when(i == turn)(lambda turn=turn: saving(which, turn).start())

    groups = MODEL_WIDTH // tokens_here

    def place(number):
        return number % per, number // per

    def take(table, first, number):
        table_row, group = place(number)
        index = lax.broadcasted_iota(jnp.int32, table.shape, 0)
        line = jnp.sum(jnp.where(index == table_row + first, table, 0.0), axis=0, keepdims=True)
        picked = jnp.zeros((1, tokens_here), F32)
        for q in range(groups):
            part = line[:, q * tokens_here : (q + 1) * tokens_here]
            picked = picked + jnp.where(group == q, part, 0.0)
        return picked

    held = (0, 1) if emit else experts
    first_held = held.index(experts[0]) * capacity
    shift = 1 if prior else 0

    def gather(b):
        arrive(b, tokens_in)
        table = x_ref[b, tokens_here:, :].astype(F32)
        slot_index = lax.broadcasted_iota(jnp.int32, (capacity, tokens_here), 0).astype(F32)
        at = pl.ds(pl.multiple_of(b * capacity, capacity), capacity)
        for h, e in enumerate(held):
            pick = (slot_index == take(table, 2 * per, ids[e])).astype(F32)
            if e in experts:
                gate = take(table, 0, ids[e]) + take(table, per, ids[e])
                slot = jnp.sum(pick * gate, axis=1, keepdims=True)
                slot_ref[experts.index(e), at, :] = jnp.broadcast_to(slot, (capacity, 128))
            pick_ref[b, h * capacity : (h + 1) * capacity, :] = pick.astype(BF16)
        pick = pick_ref[b, first_held : first_held + n_experts * capacity, :]
        rows = dot(pick, x_ref[b, :tokens_here, :], 1, 0).astype(BF16)
        g_rows = dot(pick, g_ref[b], 1, 0).astype(BF16)
        for i in range(n_experts):
            rows_ref[i, at, :] = rows[i * capacity : (i + 1) * capacity]
            g_rows_ref[i, at, :] = g_rows[i * capacity : (i + 1) * capacity]

    each(n_blocks, gather)
    TF, TD = 512, 1024

    def tile_at(n):
        return slice(n * tile, (n + 1) * tile)

    def expert(i):
        save(0, i)
        arrive(i, gate_in)
        arrive(i, up_in)

        def forward(n):
            at = slice(n * TF, (n + 1) * TF)
            gate_pre = dot(rows_ref[i], gate_ref[i, :, at], 1, 0)
            up_pre = dot(rows_ref[i], up_ref[i, :, at], 1, 0)
            gate_pre_ref[:, at] = gate_pre
            up_pre_ref[:, at] = up_pre
            inner_ref[i, :, at] = (gate_pre * jax.nn.sigmoid(gate_pre) * up_pre).astype(BF16)

        for n in range(width // TF):
            forward(n)
        save(2, i)
        arrive(i, down_in)
        gate_grad_ref[i + shift] = jnp.zeros(gate_grad_ref.shape[1:], F32)

        def produce(n):
            at = slice(n * TD, (n + 1) * TD)
            slot = slot_ref[i, :, :1]
            produced = dot(inner_ref[i], down_ref[i, :, at], 1, 0).astype(BF16).astype(F32)
            g_rows = g_rows_ref[i, :, at].astype(F32)
            gate_grad_ref[i + shift] += jnp.sum(g_rows * produced, axis=1, keepdims=True)
            scaled_ref[i + shift, :, at] = (slot * produced).astype(BF16)
            gprod_ref[i, :, at] = (slot * g_rows).astype(BF16)

        for n in range(MODEL_WIDTH // TD):
            produce(n)
        save(1, i)

        def backward(n):
            at = slice(n * TF, (n + 1) * TF)
            grad_inner = dot(gprod_ref[i], down_ref[i, at, :], 1, 1)
            gate_pre, up_pre = gate_pre_ref[:, at], up_pre_ref[:, at]
            sigmoid = jax.nn.sigmoid(gate_pre)
            dgate = grad_inner * up_pre * sigmoid * (1.0 + gate_pre * (1.0 - sigmoid))
            dgate_ref[i, :, at] = dgate.astype(BF16)
            dup_ref[i, :, at] = (grad_inner * (gate_pre * sigmoid)).astype(BF16)

        for n in range(width // TF):
            backward(n)
        save(3, i)
        save(4, i)

        def to_rows(n):
            at = slice(n * TD, (n + 1) * TD)
            back = dot(dgate_ref[i], gate_ref[i, at, :], 1, 1)
            back = back + dot(dup_ref[i], up_ref[i, at, :], 1, 1)
            back_ref[i + shift, :, at] = back.astype(BF16)

        for n in range(MODEL_WIDTH // TD):
            to_rows(n)

    each(n_experts, expert)
    def storing(i):
        source = made_ref.at[i] if emit else (scaled_ref, back_ref, gate_grad_ref)[i].at[0]
        return pltpu.make_async_copy(source, made_hbm[i], out_sem.at[i])

    if not emit:
        for i in range(3):
            storing(i).start()
    else:
        if prior:
            for i in prior_in:
                arrivals[i]().wait()
        table_rows = x_ref.shape[1] - tokens_here
        tall = tokens_here + table_rows
        shape = (table_rows, MODEL_WIDTH)

        def scatter(b):
            row_index = lax.broadcasted_iota(jnp.int32, shape, 0)
            lane_group = lax.broadcasted_iota(jnp.int32, shape, 1) // tokens_here
            slots = pl.ds(pl.multiple_of(b * capacity, capacity), capacity)
            pick = pick_ref[b]

            def spread(n):
                at = slice(n * TD, (n + 1) * TD)
                made = jnp.concatenate([back_ref[0, slots, at], back_ref[1, slots, at]], axis=0)
                made_ref[b, :tokens_here, at] = dot(pick, made, 0, 0).astype(BF16)
                made = jnp.concatenate([scaled_ref[0, slots, at], scaled_ref[1, slots, at]], axis=0)
                made_ref[b, tall:, at] = dot(pick, made, 0, 0).astype(BF16)

            for n in range(MODEL_WIDTH // TD):
                spread(n)
            table = jnp.zeros(shape, F32)
            for e in range(2):
                table_row, group = place(ids[e])
                picked = pick[e * capacity : (e + 1) * capacity].astype(F32)
                line = jnp.sum(picked * gate_grad_ref[e, slots, :1], axis=0, keepdims=True)
                coarse = line.astype(BF16).astype(F32)
                here = lane_group == group
                for first, part in ((0, coarse), (per, line - coarse)):
                    wide = jnp.concatenate([part] * groups, axis=1)
                    table = table + jnp.where(here & (row_index == table_row + first), wide, 0.0)
            made_ref[b, tokens_here:tall, :] = table.astype(BF16)
            for turn in range(n_blocks):
                pl.when(b == turn)(lambda turn=turn: storing(turn).start())

        each(n_blocks, scatter)
    for turn in range(n_experts):
        for which in range(5):
            saving(which, turn).wait()
    for i in range(len(made_hbm)):
        storing(i).wait()


def run_experts(numbers, x_blocks, g_blocks, weights, experts, saved, first, total, capacity, prior=()):
    tokens_here = g_blocks[0][0].shape[0]
    block_rows = x_blocks[0][0].shape[0]
    width = weights[0].shape[2]
    n_blocks, n_here = len(x_blocks), len(experts)
    rows = n_blocks * capacity
    per = lax.axis_size("row") * tokens_here // MODEL_WIDTH
    emit = bool(prior) or n_here == 2
    sources = tuple(len(v) for v in x_blocks)
    plan = (sources, tuple(experts), first, bool(prior), saved is not None)
    hbm = pl.BlockSpec(memory_space=pltpu.HBM)
    if emit:
        made = [jax.ShapeDtypeStruct((tokens_here + block_rows, MODEL_WIDTH), BF16)] * n_blocks
    else:
        made = [jax.ShapeDtypeStruct((rows, MODEL_WIDTH), BF16)] * 2
        made.append(jax.ShapeDtypeStruct((rows, 128), F32))
    kept = [jax.ShapeDtypeStruct((2, total, MODEL_WIDTH), BF16)] * 2
    kept += [jax.ShapeDtypeStruct((2, total, width), BF16)] * 3
    operands = [w for v in (*x_blocks, *g_blocks) for w in v]
    for e in experts:
        operands += weights[3:] if e else weights[:3]
    operands += prior
    handed = 1 + len(operands)
    aliases = {}
    if saved is not None:
        operands += saved
        aliases = {handed + i: len(made) + i for i in range(5)}
    results = pl.pallas_call(
        functools.partial(experts_kernel, tokens_here, capacity, per, plan),
        out_shape=made + kept,
        in_specs=[pl.BlockSpec(memory_space=pltpu.SMEM)] + [hbm] * len(operands),
        out_specs=[hbm] * (len(made) + 5),
        scratch_shapes=[
            pltpu.VMEM((n_blocks, block_rows, MODEL_WIDTH), BF16),
            pltpu.VMEM((n_blocks, tokens_here, MODEL_WIDTH), BF16),
        ]
        + [pltpu.VMEM((n_here, *v.shape[1:]), BF16) for v in weights[:3]]
        + [pltpu.VMEM((n_blocks, *made[0].shape) if emit else (16, 128), BF16)]
        + [pltpu.VMEM((n_here, rows, MODEL_WIDTH), BF16)] * 2
        + [pltpu.VMEM((n_here, rows, width), BF16)] * 3
        + [
            pltpu.VMEM((n_blocks, (2 if emit else 1) * capacity, tokens_here), BF16),
            pltpu.VMEM((n_here, rows, MODEL_WIDTH), BF16),
            pltpu.VMEM((rows, width), F32),
            pltpu.VMEM((rows, width), F32),
            pltpu.VMEM((n_here, rows, 128), F32),
            pltpu.VMEM((2 if emit else 1, rows, MODEL_WIDTH), BF16),
            pltpu.VMEM((2 if emit else 1, rows, MODEL_WIDTH), BF16),
            pltpu.VMEM((2 if emit else 1, rows, 128), F32),
            pltpu.SemaphoreType.DMA((2 * n_blocks + 14,)),
            pltpu.SemaphoreType.DMA((len(made),)),
            pltpu.SemaphoreType.DMA((5, n_here)),
        ],
        input_output_aliases=aliases,
        compiler_params=pltpu.CompilerParams(vmem_limit_bytes=VMEM_ALL),
        cost_estimate=pl.CostEstimate(flops=1000, bytes_accessed=1000, transcendentals=0),
        name="experts",
    )(numbers, *operands)
    return list(results[: len(made)]), list(results[len(made) :])


def swap_halves(values):
    width = values.shape[1]
    half = HEAD_SIZE // 2
    lane = lax.broadcasted_iota(jnp.int32, values.shape, 1)
    return jnp.where(
        lane % HEAD_SIZE < half,
        pltpu.roll(values, width - half, 1),
        pltpu.roll(values, half, 1),
    )


def turn(values, cosine, sine_part):
    times = values.shape[1] // cosine.shape[1]
    wide = [jnp.concatenate([v] * times, axis=1) for v in (cosine, sine_part)]
    return values * wide[0] + swap_halves(values) * wide[1]


def rms_factor(values):
    return lax.rsqrt(jnp.mean(values * values, axis=-1, keepdims=True) + EPSILON)


def block_bias(seg_col_ref, seg_row_ref, first, rows, keys):
    queries = lax.broadcasted_iota(jnp.int32, (rows, keys), 0) + first
    at = lax.broadcasted_iota(jnp.int32, (rows, keys), 1)
    same = seg_col_ref[first : first + rows, :] == seg_row_ref[:, :keys]
    return jnp.where(same & (at <= queries), 0.0, -1e30)


def head_lanes(number):
    return slice(number * HEAD_SIZE, (number + 1) * HEAD_SIZE)


def attend_kernel(n_head, head_ref, *refs):
    token_refs = refs[:n_head]
    seg_col, seg_row, gain, w_q, w_k, w_v, w_o, cos_ref, sin_ref = refs[n_head : n_head + 9]
    normed_ref, q_ref, k_ref, v_ref, mixed_ref, lse_ref, own_ref, other_ref = refs[n_head + 9 : n_head + 17]
    part_ref, bias_ref = refs[n_head + 17 :]
    rows = token_refs[0].shape[0]
    head_at = head_ref[0]
    scale = HEAD_SIZE ** (-0.5)
    for k in range(n_head):
        x = token_refs[k][...].astype(F32)
        at = pl.ds(pl.multiple_of((head_at ^ k) * rows, rows), rows)
        normed_ref[at, :] = (x * rms_factor(x) * gain[...]).astype(BF16)
    normed = normed_ref[...]
    cosine, sine_part = cos_ref[...], sin_ref[...]
    q_ref[...] = (turn(dot(normed, w_q[...], 1, 0), cosine, sine_part).astype(BF16) * scale).astype(BF16)
    k_ref[...] = turn(dot(normed, w_k[...], 1, 0), cosine, sine_part).astype(BF16)
    v_ref[...] = dot(normed, w_v[...], 1, 0).astype(BF16)
    kv = k_ref.shape[1] // HEAD_SIZE
    per_group = q_ref.shape[1] // k_ref.shape[1]
    lane = lax.broadcasted_iota(jnp.int32, (rows, lse_ref.shape[1]), 1)
    wide_q, wide_k = 2 * per_group * HEAD_SIZE, 2 * HEAD_SIZE
    for i in range(n_head):
        first, keys = i * rows, (i + 1) * rows
        bias_ref[:, :keys] = block_bias(seg_col, seg_row, first, rows, keys)
        lse_ref[first:keys, :] = jnp.zeros((rows, lse_ref.shape[1]), F32)

        def pair(jj, first=first, keys=keys):
            q_at = pl.ds(pl.multiple_of(jj * wide_q, wide_q), wide_q)
            k_at = pl.ds(pl.multiple_of(jj * wide_k, wide_k), wide_k)
            query_all, key_all, value_all = q_ref[first:keys, q_at], k_ref[:keys, k_at], v_ref[:keys, k_at]
            made = []
            log_totals = lse_ref[first:keys, :]
            for h in range(2 * per_group):
                j = h // per_group
                key, value = key_all[:, head_lanes(j)], value_all[:, head_lanes(j)]
                scores = dot(query_all[:, head_lanes(h)], key, 1, 1) + bias_ref[:, :keys]
                highest = jnp.max(scores, axis=1, keepdims=True)
                exponent = jnp.exp(scores - highest)
                total = jnp.sum(exponent, axis=1, keepdims=True)
                log_totals = jnp.where(
                    lane == jj * (2 * per_group) + h, highest + jnp.log(total), log_totals
                )
                probs = (exponent * (1.0 / total)).astype(BF16)
                made.append(dot(probs, value, 1, 0).astype(BF16))
            mixed_ref[first:keys, q_at] = jnp.concatenate(made, axis=1)
            lse_ref[first:keys, :] = log_totals

        each(kv // 2, pair)
    part_ref[...] = dot(mixed_ref[...], w_o[...], 1, 0)
    own_ref[...] = part_ref[pl.ds(pl.multiple_of(head_at * rows, rows), rows), :]
    for k in range(1, n_head):
        at = pl.ds(pl.multiple_of((head_at ^ k) * rows, rows), rows)
        other_ref[k - 1] = part_ref[at, :].astype(BF16)


def attend_back_kernel(n_head, head_ref, *refs):
    token_refs, refs = refs[:n_head], refs[n_head:]
    grad_refs = refs[:n_head]
    seg_col, seg_row, w_q, w_k, w_v, w_o, cos_ref, sin_ref = refs[n_head : n_head + 8]
    q_ref, k_ref, v_ref, lse_ref = refs[n_head + 8 : n_head + 12]
    full_ref, proj_ref, own_ref, other_ref, gain_ref = refs[n_head + 12 : n_head + 17]
    gm_ref, dq_ref, dk_ref, dv_ref, part_ref, bias_ref = refs[n_head + 17 :]
    rows = grad_refs[0].shape[0]
    head_at = head_ref[0]
    scale = HEAD_SIZE ** (-0.5)
    for k in range(n_head):
        at = pl.ds(pl.multiple_of((head_at ^ k) * rows, rows), rows)
        full_ref[at, :] = grad_refs[k][...]
    gm_ref[...] = dot(full_ref[...], w_o[...], 1, 1).astype(BF16)
    cosine, sine_part = cos_ref[...], -sin_ref[...]
    kv = k_ref.shape[1] // HEAD_SIZE
    per_group = q_ref.shape[1] // k_ref.shape[1]
    dk_ref[...] = jnp.zeros(dk_ref.shape, F32)
    dv_ref[...] = jnp.zeros(dv_ref.shape, F32)
    lane = lax.broadcasted_iota(jnp.int32, (rows, lse_ref.shape[1]), 1)
    wide_q, wide_k = 2 * per_group * HEAD_SIZE, 2 * HEAD_SIZE
    for i in range(n_head):
        first, keys = i * rows, (i + 1) * rows
        bias_ref[:, :keys] = block_bias(seg_col, seg_row, first, rows, keys)

        def pair(jj, first=first, keys=keys):
            q_at = pl.ds(pl.multiple_of(jj * wide_q, wide_q), wide_q)
            k_at = pl.ds(pl.multiple_of(jj * wide_k, wide_k), wide_k)
            query_all, grad_all = q_ref[first:keys, q_at], gm_ref[first:keys, q_at]
            key_all, value_all = k_ref[:keys, k_at], v_ref[:keys, k_at]
            log_totals = lse_ref[first:keys, :]
            made, dk_all, dv_all = [], [], []
            for j in range(2):
                key, value = key_all[:, head_lanes(j)], value_all[:, head_lanes(j)]
                dk, dv = 0.0, 0.0
                for h in range(j * per_group, (j + 1) * per_group):
                    query, grad = query_all[:, head_lanes(h)], grad_all[:, head_lanes(h)]
                    mine = jnp.where(lane == jj * (2 * per_group) + h, log_totals, 0.0)
                    log_total = jnp.sum(mine, axis=1, keepdims=True)
                    probs = jnp.exp(dot(query, key, 1, 1) + bias_ref[:, :keys] - log_total)
                    grad_probs = dot(grad, value, 1, 1)
                    middle = jnp.sum(probs * grad_probs, axis=1, keepdims=True)
                    ds = (probs * (grad_probs - middle)).astype(BF16)
                    made.append(dot(ds, key, 1, 0) * scale)
                    dk = dk + dot(query, ds, 0, 0)
                    dv = dv + dot(grad, probs.astype(BF16), 0, 0)
                dk_all.append(dk)
                dv_all.append(dv)
            dq_ref[first:keys, q_at] = jnp.concatenate(made, axis=1)
            dk_ref[k_at, :keys] += jnp.concatenate(dk_all, axis=0)
            dv_ref[k_at, :keys] += jnp.concatenate(dv_all, axis=0)

        each(kv // 2, pair)
    width_q, width_k = q_ref.shape[1], k_ref.shape[1]
    proj_ref[:, :width_q] = turn(dq_ref[...], cosine, sine_part).astype(BF16)
    proj_ref[:, width_q : width_q + width_k] = turn(dk_ref[...].T, cosine, sine_part).astype(BF16)
    proj_ref[:, width_q + width_k :] = dv_ref[...].T.astype(BF16)
    part_ref[...] = (
        dot(proj_ref[:, :width_q], w_q[...], 1, 1)
        + dot(proj_ref[:, width_q : width_q + width_k], w_k[...], 1, 1)
        + dot(proj_ref[:, width_q + width_k :], w_v[...], 1, 1)
    )
    gain = jnp.zeros(gain_ref.shape, F32)
    for k in range(n_head):
        part = part_ref[pl.ds(pl.multiple_of((head_at ^ k) * rows, rows), rows), :]
        x = token_refs[k][...].astype(F32)
        gain = gain + jnp.sum(part * (x * rms_factor(x)), axis=0, keepdims=True)
        if k:
            other_ref[k - 1] = part.astype(BF16)
        else:
            own_ref[...] = part
    gain_ref[...] = gain


def weight_grads_kernel(share, core_ref, normed_ref, proj_ref, full_ref, mixed_ref, own_ref, other_ref, all_ref):
    core = core_ref[0]
    width = proj_ref.shape[1]
    all_ref[:, :width] = dot(normed_ref[...], proj_ref[...], 0, 0)
    all_ref[:, width:] = dot(full_ref[...], mixed_ref[...], 0, 0)
    for m in range(own_ref.shape[0] // share):
        at = slice(m * share, (m + 1) * share)
        own = pl.ds(pl.multiple_of((2 * m + core) * share, share), share)
        other = pl.ds(pl.multiple_of((2 * m + 1 - core) * share, share), share)
        own_ref[at, :] = all_ref[own, :]
        other_ref[at, :] = all_ref[other, :].astype(BF16)


def expert_grads_kernel(n_head, axis, heads_first, head_ref, lhs_ref, rhs_ref, *refs):
    head_at = head_ref[0]
    own_ref, rest_ref, away_ref, all_ref = refs
    size = own_ref.shape[axis]

    def part(k):
        at = pl.ds(pl.multiple_of((head_at ^ k) * size, size), size)
        return all_ref[at, :] if axis == 0 else all_ref[:, at]

    def first():
        own_ref[...] = part(0)
        for k in range(1, n_head):
            if heads_first:
                away_ref[k - 1, 0] = part(k).astype(BF16)
            else:
                rest_ref[k - 1] = part(k)

    def second():
        for k in range(n_head):
            if not heads_first:
                away_ref[k] = part(k).astype(BF16)
            elif k:
                away_ref[k - 1, 1] = part(k).astype(BF16)
            else:
                rest_ref[0] = part(0)

    def turn(e):
        all_ref[...] = dot(lhs_ref[e], rhs_ref[e], 0, 0)
        pl.when(e == 0)(first)
        pl.when(e == 1)(second)

    each(2, turn)


def final_kernel(n_head, tokens_ref, grad_hidden_ref, gain, own_ref, *refs):
    total = own_ref[...]
    for part in refs[: n_head - 1]:
        total = total + part[...].astype(F32)
    x = tokens_ref[...].astype(F32)
    factor = rms_factor(x)
    weighted = total * gain[...]
    middle = jnp.mean(weighted * x, axis=-1, keepdims=True)
    refs[-1][...] = grad_hidden_ref[...] + factor * (weighted - x * factor * factor * middle)


def hidden_kernel(n_head, tokens_ref, own_ref, *refs):
    arrived = refs[: n_head - 1]
    gain, router_t, slots_ref, chosen_ref = refs[n_head - 1 : n_head + 3]
    block_ref, hidden_ref, gates_ref = refs[n_head + 3 :]
    rows = tokens_ref.shape[0]
    attention = own_ref[...]
    for part in arrived:
        attention = attention + part[...].astype(F32)
    hidden = tokens_ref[...].astype(F32) + attention
    hidden_ref[...] = hidden
    normed = (hidden * rms_factor(hidden) * gain[...]).astype(BF16)
    block_ref[:rows, :] = normed
    chosen = chosen_ref[...] > 0.0
    logits = jnp.where(chosen, dot(router_t[...], normed, 1, 1), -1e30)
    gates = jnp.where(chosen, jnp.exp(logits - jnp.max(logits, axis=0, keepdims=True)), 0.0)
    gates = gates / jnp.sum(gates, axis=0, keepdims=True)
    gates_ref[...] = gates
    coarse = gates.astype(BF16).astype(F32)
    groups = MODEL_WIDTH // rows
    per = gates.shape[0] // groups
    lines = [
        jnp.concatenate([v[q * per : (q + 1) * per] for q in range(groups)], axis=1)
        for v in (coarse, gates - coarse, slots_ref[...])
    ]
    spare = block_ref.shape[0] - rows - 3 * per
    if spare:
        lines.append(jnp.zeros((spare, MODEL_WIDTH), F32))
    block_ref[rows:, :] = jnp.concatenate(lines, axis=0).astype(BF16)


def grad_hidden_kernel(n_parts, *refs):
    parts = refs[:n_parts]
    hidden_ref, gain, router_t, gates_ref, block_ref, cotangent_ref = refs[n_parts : n_parts + 6]
    grad_ref, low_ref, small_ref = refs[n_parts + 6 :]
    rows = hidden_ref.shape[0]
    tall = block_ref.shape[0]
    total = parts[0][:tall, :].astype(F32)
    for part in parts[1:]:
        total = total + part[:tall, :].astype(F32)
    gates = gates_ref[...]
    groups = MODEL_WIDTH // rows
    per = gates.shape[0] // groups
    lines = total[rows : rows + per] + total[rows + per : rows + 2 * per]
    grad_gates = jnp.concatenate(
        [lines[:, q * rows : (q + 1) * rows] for q in range(groups)], axis=0
    )
    grad_logits = gates * (grad_gates - jnp.sum(gates * grad_gates, axis=0, keepdims=True))
    coarse = grad_logits.astype(BF16)
    fine = (grad_logits - coarse.astype(F32)).astype(BF16)
    normed = block_ref[:rows, :]
    n_experts = gates.shape[0]
    small_ref[:n_experts, :] = dot(coarse, normed, 1, 0) + dot(fine, normed, 1, 0)
    upstream = total[:rows] + dot(coarse, router_t[...], 0, 0) + dot(fine, router_t[...], 0, 0)
    hidden = hidden_ref[...]
    factor = rms_factor(hidden)
    weighted = upstream * gain[...]
    middle = jnp.mean(weighted * hidden, axis=-1, keepdims=True)
    grad = cotangent_ref[...].astype(F32) + factor * (weighted - hidden * factor * factor * middle)
    grad_ref[...] = grad
    low_ref[...] = grad.astype(BF16)
    small_ref[n_experts:, :] = jnp.sum(upstream * hidden * factor, axis=0, keepdims=True)


def call(kernel, name, operands, out_shape, scratch_shapes=(), scalars=0, room=VMEM_BYTES):
    vmem = pl.BlockSpec(memory_space=pltpu.VMEM)
    smem = pl.BlockSpec(memory_space=pltpu.SMEM)
    made = pl.pallas_call(
        kernel,
        out_shape=out_shape,
        in_specs=[smem] * scalars + [vmem] * (len(operands) - scalars),
        out_specs=[vmem] * len(out_shape),
        scratch_shapes=list(scratch_shapes),
        compiler_params=pltpu.CompilerParams(vmem_limit_bytes=room),
        cost_estimate=pl.CostEstimate(flops=1000, bytes_accessed=1000, transcendentals=0),
        name=name,
    )(*operands)
    return list(made)


def local(
    tokens,
    segments,
    routes,
    norm_gain,
    w_query,
    key_weight,
    value_weight,
    w_output,
    moe_gain,
    w_router,
    w_gate,
    w_up,
    w_down,
    cotangent,
):
    local_rows = tokens.shape[0]
    length = segments.shape[0]
    n_experts = w_router.shape[1]
    capacity = local_rows * TOPK * 5 // (4 * n_experts)
    width_query = w_query.shape[1]
    width_key = key_weight.shape[1]
    n_row = lax.axis_size("row")
    n_head = lax.axis_size("head")
    n_outer = n_row // 4
    row_at = lax.axis_index("row")
    head_at = lax.axis_index("head")
    at_end = (row_at // 4 % 3 == 0).astype(jnp.int32)
    numbers = jnp.stack([row_at, head_at & 1, at_end]).astype(jnp.int32)

    routes_t = routes.T
    expert_index = jnp.arange(n_experts, dtype=jnp.int32)[:, None]
    chosen = jnp.any(routes_t[:, None, :] == expert_index[None], axis=0)
    t_index = jnp.arange(local_rows, dtype=jnp.int32)
    before = (t_index[:, None] < t_index[None, :]).astype(BF16)
    rank = dot(chosen.astype(BF16), before, 1, 0)
    slots = jnp.where(chosen & (rank < capacity), rank, -1.0)
    chosen = chosen.astype(F32)
    router_t = w_router.T
    head_number = head_at.astype(jnp.int32).reshape(1)

    line = n_outer == 4
    inner = [(i, i ^ 12) for i in range(4, 12)]
    outward = [(i, i ^ 4) for i in range(4, 12)]
    ends = [*range(4), *range(12, 16)]
    ends_in = [(i, i ^ 8) for i in ends]
    ends_over = [(i, i ^ 12) for i in ends]
    inner_out = [(i, i ^ 8) for i in range(4, 12)]

    def send(value, pairs):
        return lax.ppermute(value, "row", pairs)

    def share_of(weight):
        size = weight.shape[1] // 2
        return lax.dynamic_slice_in_dim(weight[0], (head_at & 1) * size, size, 0)

    def head_all(values):
        return [head_swap(values[k - 1], k) for k in range(1, n_head)]

    def low(value):
        return value.astype(BF16)

    def shape(rows, columns, dtype=BF16):
        return jax.ShapeDtypeStruct((rows, columns), dtype)

    seg_col, seg_row = segments[:, None], segments[None, :]
    gain_row, moe_gain_row = norm_gain[None], moe_gain[None]

    tokens_other = head_all([tokens] * (n_head - 1))
    frequency = ROPE_BASE ** (-2.0 * jnp.arange(HEAD_SIZE // 2, dtype=F32) / HEAD_SIZE)
    angles = jnp.arange(length, dtype=F32)[:, None] * frequency[None, :]
    cosine, sine_part = jnp.cos(angles), jnp.sin(angles)
    cosine = jnp.concatenate([cosine] * 4, axis=1)
    sine_part = jnp.concatenate([-sine_part, sine_part] * 2, axis=1)
    gate_share, down_share = share_of(w_gate), share_of(w_down)
    width = gate_share.shape[1]
    pieces = [down_share[:, k : k + width] for k in range(0, down_share.shape[1], width)]
    gate_here = row_swap(gate_share, 2)
    down_here = row_swap(jnp.concatenate(pieces, axis=0), 2)
    if line:
        g_far = [row_swap(cotangent, 4), send(cotangent, inner)]
    else:
        g_far = [row_swap(cotangent, 4 * o) for o in range(1, n_outer)]
    tokens_other, cosine, sine_part, seg_col, slots, chosen = tie(
        tokens_other, cosine, sine_part, seg_col, slots, chosen
    )
    g_far, w_up_later, _ = tie(g_far, w_up, seg_col)

    g_slabs = [cotangent, *g_far]
    if line:
        g_far += [send(g_far[1], outward), send(g_far[0], inner)]
    head_parts = [
        shape(local_rows, MODEL_WIDTH, F32),
        jax.ShapeDtypeStruct((n_head - 1, local_rows, MODEL_WIDTH), BF16),
    ]
    normed_full, queries, keys, values, mixed_heads, log_totals, part_own, part_other = call(
        functools.partial(attend_kernel, n_head),
        "attend",
        [head_number, tokens, *tokens_other, seg_col, seg_row, gain_row]
        + [w_query, key_weight, value_weight, w_output, cosine, sine_part],
        [shape(length, MODEL_WIDTH), shape(length, width_query)]
        + [shape(length, width_key)] * 2
        + [shape(length, width_query), shape(length, 128, F32), *head_parts],
        [pltpu.VMEM((length, MODEL_WIDTH), F32), pltpu.VMEM((local_rows, length), F32)],
        scalars=1,
        room=VMEM_ALL,
    )
    part_other, part_own, gate_here, down_here, g_far, w_up_later = tie(
        part_other, part_own, gate_here, down_here, g_far, w_up_later
    )

    arrived = head_all(part_other)
    up_here = row_swap(w_up_later, 2)
    g_last = send(g_far[3], outward) if line else cotangent
    arrived, part_own, g_last = tie(arrived, part_own, g_last)
    table_rows = -(-3 * n_experts * local_rows // MODEL_WIDTH // 16) * 16
    x_block, hidden, gates = call(
        functools.partial(hidden_kernel, n_head),
        "hidden",
        [tokens, part_own, *arrived, moe_gain_row, router_t, slots, chosen],
        [
            shape(local_rows + table_rows, MODEL_WIDTH),
            shape(local_rows, MODEL_WIDTH, F32),
            shape(n_experts, local_rows, F32),
        ],
    )
    tall = x_block.shape[0]
    saved = None
    made = []

    def cores(values):
        return [row_swap(v, 1) for v in values]

    def pass_on(chunk):
        made[chunk][1] = row_swap(made[chunk][1], 1)

    def near(which, chunk):
        own, other = (v[:tall] if which else v[tall:] for v in made[chunk])
        return own.astype(F32) + other.astype(F32)

    def experts(x_blocks, g_blocks, which, prior=()):
        nonlocal saved
        first = 2 * len(made) * capacity
        results, saved = run_experts(
            numbers, x_blocks, g_blocks, weights, which, saved, first, total_rows, capacity, prior
        )
        if which == (0,):
            return results
        made.extend(results[i : i + 2] for i in range(0, len(results), 2))

    total_rows = 2 * n_outer * capacity
    gate_there = head_swap(gate_here, 1)
    x_core = row_swap(x_block, 1)
    if line:
        x_far = [row_swap(x_block, 4), send(x_block, inner)]
    else:
        x_far = [row_swap(x_block, 4 * o) for o in range(1, n_outer)]
    x_block, x_core, x_far, up_here, gate_there, down_later, g_slabs, g_far, g_last, cotangent = tie(
        x_block, x_core, x_far, up_here, gate_there, down_here, g_slabs, g_far, g_last, cotangent
    )
    down_there = head_swap(down_later, 1)
    weights = [w_gate, w_up, w_down, gate_here, gate_there, down_here, down_there, up_here]

    if line:
        x_near, x_mid = x_far
        x_near_core = row_swap(x_near, 1)
        g_cores = cores(g_slabs[:2])
        x_near, x_mid, x_near_core, g_cores, g_far = tie(x_near, x_mid, x_near_core, g_cores, g_far)
        x_out, x_deep = send(x_mid, outward), send(x_near, inner)
        x_pairs = [[x_block], [x_core], [x_near], [x_near_core]]
        g_pairs = [[cotangent], [g_cores[0]], [g_slabs[1]], [g_cores[1]]]
        prior = experts(x_pairs, g_pairs, (0,))
        x_out, x_deep, prior, saved, down_there, g_far, x_mid, g_mid, g_last = tie(
            x_out, x_deep, prior, saved, down_there, g_far, x_mid, g_slabs[2], g_last
        )
        weights[6] = down_there
        x_last = send(x_deep, outward)
        x_mid_core, g_mid_core, g_out_core = cores([x_mid, g_mid, g_far[2]])
        experts(x_pairs, g_pairs, (1,), prior)
        x_last, x_mid_core, g_mid_core, g_out_core, made[0], made[1], saved, x_out = tie(
            x_last, x_mid_core, g_mid_core, g_out_core, made[0], made[1], saved, x_out
        )
        x_out_core = row_swap(x_out, 1)
        x_out_core, x_last, x_deep, g_deep, g_last, made[0] = tie(
            x_out_core, x_last, x_deep, g_far[3], g_last, made[0]
        )
        pass_on(1)
        x_deep_core, x_last_core, g_deep_core, g_last_core = cores([x_deep, x_last, g_deep, g_last])
        g_two = [[g_mid, g_far[2]], [g_mid_core, g_out_core]]
        experts([[x_mid, x_out], [x_mid_core, x_out_core]], g_two, (0, 1))
        x_deep_core, x_last_core, g_deep_core, g_last_core, made[0], made[1], made[2], saved = tie(
            x_deep_core, x_last_core, g_deep_core, g_last_core, made[0], made[1], made[2], saved
        )
        pass_on(2)
        made[0], made[1], made[2], x_deep, x_last = tie(made[0], made[1], made[2], x_deep, x_last)
        g_three = [[g_deep, g_last], [g_deep_core, g_last_core]]
        two, sum_one = low(near(1, 2)), low(near(1, 1))
        first_sums = [send(two, ends_in), send(two, inner), row_swap(sum_one, 4)]
        x_deep, x_last, _, _ = tie(x_deep, x_last, two, sum_one)
        experts([[x_deep, x_last], [x_deep_core, x_last_core]], g_three, (0, 1))
    else:
        for o, x in enumerate([x_block, *x_far]):
            experts([[x], [row_swap(x, 1)]], [[g_slabs[o]], [row_swap(g_slabs[o], 1)]], (0, 1))
        for o in range(n_outer):
            pass_on(o)
        one = [row_swap(low(near(1, o)), 4 * o) for o in range(1, n_outer)]

    rows_in, gprod, inner_act, dgate, dup = saved

    def expert_grads(lhs, rhs, axis, heads_first):
        sizes = [lhs.shape[2], rhs.shape[2]]
        part = list(sizes)
        part[axis] //= n_head
        rest = (1, *part) if heads_first else (n_head - 1, *part)
        away = (n_head - 1, 2, *part) if heads_first else (n_head, *part)
        return call(
            functools.partial(expert_grads_kernel, n_head, axis, heads_first),
            "expert_grads",
            [head_number, lhs, rhs],
            [
                jax.ShapeDtypeStruct(tuple(part), F32),
                jax.ShapeDtypeStruct(rest, F32),
                jax.ShapeDtypeStruct(away, BF16),
            ],
            [pltpu.VMEM(tuple(sizes), F32)],
            scalars=1,
        )

    if line:
        made[0], made[3], inner_act, gprod, rows_in, dgate, dup = tie(
            made[0], made[3], inner_act, gprod, rows_in, dgate, dup
        )
    up_parts = expert_grads(rows_in, dup, 0, False)
    down_parts = expert_grads(inner_act, gprod, 1, True)
    up_away, down_away = up_parts[2], down_parts[2]
    if line:
        first_sums, made[0], made[3], up_away, down_away, rows_in, dgate = tie(
            first_sums, made[0], made[3], up_away, down_away, rows_in, dgate
        )
        pass_on(0)
        pass_on(3)
        made[0], made[3], first_sums, up_away, down_away, rows_in, dgate = tie(
            made[0], made[3], first_sums, up_away, down_away, rows_in, dgate
        )
        three = low(near(1, 3))
        last_sums = [send(three, ends_over), send(three, inner_out)]
    up_away = row_swap(up_away, 2)
    down_away = head_all(down_away)
    gate_parts = expert_grads(rows_in, dgate, 0, False)
    gate_away = gate_parts[2]
    if line:
        total = near(1, 0) + sum(v.astype(F32) for v in first_sums)
        out_one, out_two, out_three = (low(near(0, o)) for o in range(1, 4))
        one = [total, *last_sums]
    else:
        one = [near(1, 0), *one]
        out_one = out_two = out_three = one[0]
    one, up_away, down_away, gate_away, made_now, out_one, out_two, out_three = tie(
        one, up_away, down_away, gate_away, made, out_one, out_two, out_three
    )
    made = list(made_now)
    grad_sum = one
    grad_hidden, grad_attention, early = call(
        functools.partial(grad_hidden_kernel, len(grad_sum)),
        "grad_hidden",
        [*grad_sum, hidden, moe_gain_row, router_t, gates, x_block, cotangent],
        [
            shape(local_rows, MODEL_WIDTH, F32),
            shape(local_rows, MODEL_WIDTH),
            shape(n_experts + 1, MODEL_WIDTH, F32),
        ],
    )
    made_now, up_away, down_away, gate_away, grad_attention = tie(
        made, up_away, down_away, gate_away, grad_attention
    )
    made = list(made_now)
    grad_arrived = head_all([grad_attention] * (n_head - 1))
    gate_away = row_swap(gate_away, 2)
    out_first = [send(out_two, ends_in)] if line else [out_two]
    up_rest = [low(v + w.astype(F32)) for v, w in zip(up_parts[1], up_away[1:])]
    down_rest = low(down_parts[1][0] + sum(v[1].astype(F32) for v in down_away))
    grad_arrived, up_rest, down_rest, made_now, out_two, out_three, out_first = tie(
        grad_arrived, up_rest, down_rest, made, out_two, out_three, out_first
    )
    made = list(made_now)
    up_last = head_all(up_rest)
    if line:
        out_first += [send(out_three, ends_over), send(out_three, inner_out)]
    else:
        out_first = grad_attention
    grad_full, grad_proj, grad_own, grad_other, gain_part = call(
        functools.partial(attend_back_kernel, n_head),
        "attend_back",
        [head_number, tokens, *tokens_other, grad_attention, *grad_arrived, seg_col, seg_row]
        + [w_query, key_weight, value_weight, w_output, cosine, sine_part]
        + [queries, keys, values, log_totals],
        [
            shape(length, MODEL_WIDTH),
            shape(length, width_query + 2 * width_key),
            *head_parts,
            shape(1, MODEL_WIDTH, F32),
        ],
        [
            pltpu.VMEM((length, width_query), BF16),
            pltpu.VMEM((length, width_query), F32),
            pltpu.VMEM((width_key, length), F32),
            pltpu.VMEM((width_key, length), F32),
            pltpu.VMEM((length, MODEL_WIDTH), F32),
            pltpu.VMEM((local_rows, length), F32),
        ],
        scalars=1,
        room=VMEM_ALL,
    )
    grad_full, grad_proj, grad_other, gain_part, up_last, gate_away, down_rest, *outs = tie(
        grad_full, grad_proj, grad_other, gain_part, up_last, gate_away, down_rest,
        out_one, out_two,
    )
    out_one, out_two = outs
    share = MODEL_WIDTH // n_row
    width_all = width_query + 2 * width_key
    small = jnp.concatenate([early, gain_part], axis=0)
    weights_own, weights_other = call(
        functools.partial(weight_grads_kernel, share),
        "weight_grads",
        [(row_at % 2).astype(jnp.int32).reshape(1), normed_full, grad_proj, grad_full, mixed_heads],
        [
            shape(MODEL_WIDTH // 2, width_all + width_query, F32),
            shape(MODEL_WIDTH // 2, width_all + width_query),
        ],
        [pltpu.VMEM((MODEL_WIDTH, width_all + width_query), F32)],
        scalars=1,
        room=VMEM_ALL,
    )
    small, weights_own, weights_other, made_now, out_first, out_one, out_two = tie(
        small, weights_own, weights_other, made, out_first, out_one, out_two
    )
    made = list(made_now)
    small_core = row_swap(small, 1)
    weights_core = row_swap(weights_other, 1)
    small, small_core, weights_own, weights_core = tie(small, small_core, weights_own, weights_core)
    small = small + small_core
    small_far = row_swap(small, 2)
    if line:
        out_first = [*out_first, send(out_two, inner), row_swap(out_one, 4)]
    else:
        out_first = small
    value = (weights_own + weights_core.astype(F32)).reshape(n_outer, 2, share, -1)
    bit = (row_at // 2) % 2
    other = low(lax.dynamic_index_in_dim(value, 1 - bit, 1, keepdims=False))
    value = lax.dynamic_index_in_dim(value, bit, 1, keepdims=False)
    small, other, value, grad_other, down_rest, gate_away, made_now, out_two = tie(
        small + small_far, other, value, grad_other, down_rest, gate_away, made, out_two
    )
    made = list(made_now)
    other_arrived = row_swap(other, 2)
    offset = 4
    while offset < n_row:
        small = small + row_swap(small, offset)
        offset *= 2
    offset = 1
    while offset < n_head:
        small = small + head_swap(small, offset)
        offset *= 2
    grad_arrived = head_all(grad_other)
    gate_rest = [low(v + w.astype(F32)) for v, w in zip(gate_parts[1], gate_away[1:])]
    mixed_out = hidden + near(0, 0)
    if line:
        mixed_out = mixed_out + sum(v.astype(F32) for v in out_first)
        last = []
    else:
        last = [row_swap(low(near(0, o)), 4 * o) for o in range(1, n_outer)]
    grad_arrived, value, other_arrived, small, gate_rest, last, mixed_out, down_rest = tie(
        grad_arrived, value, other_arrived, small, gate_rest, last, mixed_out, down_rest
    )
    gate_last = head_all(gate_rest)
    value = value + other_arrived.astype(F32)
    at = row_at // 4
    weights_sum = lax.dynamic_index_in_dim(value, at, 0, keepdims=False)
    for o in range(1, n_outer):
        part = low(lax.dynamic_index_in_dim(value, at ^ o, 0, keepdims=False))
        weights_sum = weights_sum + row_swap(part, 4 * o).astype(F32)
    down_last = row_swap(down_rest, 2)
    (grad_tokens,) = call(
        functools.partial(final_kernel, n_head),
        "final",
        [tokens, grad_hidden, gain_row, grad_own, *grad_arrived],
        [shape(local_rows, MODEL_WIDTH, F32)],
    )
    for part in last:
        mixed_out = mixed_out + part.astype(F32)
    mixed_out = mixed_out.astype(BF16)

    def add(own, *parts):
        for part in parts:
            own = own + part.astype(F32)
        return own

    down_sum = add(down_parts[0], *(v[0] for v in down_away), down_last)
    up_sum = add(up_parts[0], up_away[0], *up_last)
    gate_sum = add(gate_parts[0], gate_away[0], *gate_last)
    return (
        mixed_out,
        grad_tokens,
        small[n_experts + 1],
        weights_sum[:, :width_query],
        weights_sum[:, width_query : width_query + width_key],
        weights_sum[:, width_query + width_key : width_all],
        weights_sum[:, width_all:].T,
        small[n_experts],
        small[:n_experts].T,
        gate_sum[None],
        up_sum[None],
        down_sum[None],
    )


def solution(mesh):
    in_specs = (
        P(("row", "head"), None),
        P("row"),
        P(("row", "head"), None),
        P(),
        P(None, "head"),
        P(None, "head"),
        P(None, "head"),
        P("head", None),
        P(),
        P(),
        P("row", None, None),
        P("row", None, None),
        P("row", None, None),
        P(("row", "head"), None),
    )
    out_specs = (
        P(("row", "head"), None),
        P(("row", "head"), None),
        P(),
        P("row", "head"),
        P("row", "head"),
        P("row", "head"),
        P("head", "row"),
        P(),
        P(),
        P("row", "head", None),
        P("row", "head", None),
        P("row", None, "head"),
    )
    return jax.shard_map(local, mesh=mesh, in_specs=in_specs, out_specs=out_specs, check_vma=False)
```

```python
import functools

import jax
import jax.numpy as jnp
from jax import lax
from jax.experimental import pallas as pl
from jax.experimental.pallas import tpu as pltpu
from jax.sharding import PartitionSpec as P

MODEL_WIDTH = 1024
HEAD_SIZE = 64
VMEM_BYTES = 36 * 1024 * 1024
VMEM_ALL = 63 * 1024 * 1024
TOPK = 8

EPSILON = 1e-06
ROPE_BASE = 10000.0
F32 = jnp.float32
BF16 = jnp.bfloat16


def row_swap(value, offset):
    size = lax.axis_size("row")
    return lax.ppermute(value, "row", [(i, i ^ offset) for i in range(size)])


def head_swap(value, offset):
    size = lax.axis_size("head")
    return lax.ppermute(value, "head", [(i, i ^ offset) for i in range(size)])


def dot(a, b, ca, cb, **kw):
    return lax.dot_general(a, b, (((ca,), (cb,)), ((), ())), preferred_element_type=F32, **kw)


def tie(*values):
    return lax.optimization_barrier(values)


def each(count, body):
    lax.fori_loop(0, count, lambda i, carry: (body(i), carry)[1], 0)


def experts_kernel(tokens_here, capacity, per, plan, number_ref, *refs):
    sources, experts, rows_before, prior, handed_on = plan
    n_blocks, n_experts = len(sources), len(experts)
    emit = prior or n_experts == 2
    refs = list(refs)

    def pop(number):
        taken, refs[:] = refs[:number], refs[number:]
        return taken

    x_hbm = [pop(k) for k in sources]
    g_hbm = [pop(k) for k in sources]
    w_hbm = {e: pop(5 if e else 3) for e in experts}
    prior_hbm = pop(3) if prior else []
    if handed_on:
        pop(5)
    made_hbm = pop(n_blocks) if emit else pop(3)
    saved_hbm = pop(5)
    x_ref, g_ref, gate_ref, up_ref, down_ref, made_ref = pop(6)
    rows_ref, gprod_ref, inner_ref, dgate_ref, dup_ref = pop(5)
    pick_ref, g_rows_ref, gate_pre_ref, up_pre_ref, slot_ref = pop(5)
    scaled_ref, back_ref, gate_grad_ref, in_sem, out_sem, saved_sem = pop(6)
    ids = (number_ref[0], number_ref[0] ^ 2)
    bit, flag = number_ref[1], number_ref[2]
    arrivals = []

    def load(source, target):
        i = len(arrivals)

        def copy(k=0):
            return pltpu.make_async_copy(source[k](), target(), in_sem.at[i])

        if len(source) == 2:
            for k in range(2):
                pl.when(flag == k)(copy(k).start)
        else:
            copy().start()
        arrivals.append(copy)
        return i

    def whole(ref, *index):
        return lambda: ref.at[index] if index else ref

    def arrive(at, numbers):
        for turn, mine in enumerate(numbers):

            def wait(mine=mine):
                for i in mine:
                    arrivals[i]().wait()

            pl.when(at == turn)(wait)

    width = gate_ref.shape[2]
    depth = down_ref.shape[1] // 2
    rows_half = gate_ref.shape[1] // 2

    def halves(gate, down, index, i):
        def first():
            return gate_ref.at[i, pl.ds(pl.multiple_of(index * rows_half, rows_half), rows_half)]

        def second(k):
            at = pl.ds(pl.multiple_of(index * depth, depth), depth)
            return lambda: down_ref.at[i, at, k * width : (k + 1) * width]

        def part(k):
            return lambda: down.at[k * depth : (k + 1) * depth]

        return (whole(gate), first), [(part(k), second(k)) for k in range(down_ref.shape[2] // width)]

    tokens_in = [
        [
            load([whole(h) for h in x_hbm[b]], whole(x_ref, b)),
            load([whole(h) for h in g_hbm[b]], whole(g_ref, b)),
        ]
        for b in range(n_blocks)
    ]
    gate_in, up_in, down_in = [], [], []
    for i, e in enumerate(experts):
        if e == 0:
            gate_in.append([load([whole(w_hbm[e][0], 0)], whole(gate_ref, i))])
            up_in.append([load([whole(w_hbm[e][1], 0)], whole(up_ref, i))])
            down_in.append([load([whole(w_hbm[e][2], 0)], whole(down_ref, i))])
        else:
            gate_near, gate_far, down_near, down_far, up_h = w_hbm[e]
            gate_here, down_here = halves(gate_near, down_near, bit, i)
            gate_there, down_there = halves(gate_far, down_far, 1 - bit, i)
            gate_in.append([load([a], b) for a, b in (gate_here, gate_there)])
            up_in.append([load([whole(up_h, 0)], whole(up_ref, i))])
            down_in.append([load([a], b) for a, b in down_here + down_there])
    if prior:
        prior_in = [
            load([whole(prior_hbm[0])], whole(scaled_ref, 0)),
            load([whole(prior_hbm[1])], whole(back_ref, 0)),
            load([whole(prior_hbm[2])], whole(gate_grad_ref, 0)),
        ]

    def saving(which, turn):
        buffer = (rows_ref, gprod_ref, inner_ref, dgate_ref, dup_ref)[which]
        return pltpu.make_async_copy(
            buffer.at[turn],
            saved_hbm[which].at[experts[turn], pl.ds(rows_before, n_blocks * capacity)],
            saved_sem.at[which, turn],
        )

    def save(which, i):
        for turn in range(n_experts):
            pl.when(i == turn)(lambda turn=turn: saving(which, turn).start())

    groups = MODEL_WIDTH // tokens_here

    def place(number):
        return number % per, number // per

    def take(table, first, number):
        table_row, group = place(number)
        index = lax.broadcasted_iota(jnp.int32, table.shape, 0)
        line = jnp.sum(jnp.where(index == table_row + first, table, 0.0), axis=0, keepdims=True)
        picked = jnp.zeros((1, tokens_here), F32)
        for q in range(groups):
            part = line[:, q * tokens_here : (q + 1) * tokens_here]
            picked = picked + jnp.where(group == q, part, 0.0)
        return picked

    held = (0, 1) if emit else experts
    first_held = held.index(experts[0]) * capacity
    shift = 1 if prior else 0

    def gather(b):
        arrive(b, tokens_in)
        table = x_ref[b, tokens_here:, :].astype(F32)
        slot_index = lax.broadcasted_iota(jnp.int32, (capacity, tokens_here), 0).astype(F32)
        at = pl.ds(pl.multiple_of(b * capacity, capacity), capacity)
        for h, e in enumerate(held):
            pick = (slot_index == take(table, 2 * per, ids[e])).astype(F32)
            if e in experts:
                gate = take(table, 0, ids[e]) + take(table, per, ids[e])
                slot = jnp.sum(pick * gate, axis=1, keepdims=True)
                slot_ref[experts.index(e), at, :] = jnp.broadcast_to(slot, (capacity, 128))
            pick_ref[b, h * capacity : (h + 1) * capacity, :] = pick.astype(BF16)
        pick = pick_ref[b, first_held : first_held + n_experts * capacity, :]
        rows = dot(pick, x_ref[b, :tokens_here, :], 1, 0).astype(BF16)
        g_rows = dot(pick, g_ref[b], 1, 0).astype(BF16)
        for i in range(n_experts):
            rows_ref[i, at, :] = rows[i * capacity : (i + 1) * capacity]
            g_rows_ref[i, at, :] = g_rows[i * capacity : (i + 1) * capacity]

    each(n_blocks, gather)
    TF, TD = 512, 1024

    def tile_at(n):
        return slice(n * tile, (n + 1) * tile)

    def expert(i):
        save(0, i)
        arrive(i, gate_in)
        arrive(i, up_in)

        def forward(n):
            at = slice(n * TF, (n + 1) * TF)
            gate_pre = dot(rows_ref[i], gate_ref[i, :, at], 1, 0)
            up_pre = dot(rows_ref[i], up_ref[i, :, at], 1, 0)
            gate_pre_ref[:, at] = gate_pre
            up_pre_ref[:, at] = up_pre
            inner_ref[i, :, at] = (gate_pre * jax.nn.sigmoid(gate_pre) * up_pre).astype(BF16)

        for n in range(width // TF):
            forward(n)
        save(2, i)
        arrive(i, down_in)
        gate_grad_ref[i + shift] = jnp.zeros(gate_grad_ref.shape[1:], F32)

        def produce(n):
            at = slice(n * TD, (n + 1) * TD)
            slot = slot_ref[i, :, :1]
            produced = dot(inner_ref[i], down_ref[i, :, at], 1, 0).astype(BF16).astype(F32)
            g_rows = g_rows_ref[i, :, at].astype(F32)
            gate_grad_ref[i + shift] += jnp.sum(g_rows * produced, axis=1, keepdims=True)
            scaled_ref[i + shift, :, at] = (slot * produced).astype(BF16)
            gprod_ref[i, :, at] = (slot * g_rows).astype(BF16)

        for n in range(MODEL_WIDTH // TD):
            produce(n)
        save(1, i)

        def backward(n):
            at = slice(n * TF, (n + 1) * TF)
            grad_inner = dot(gprod_ref[i], down_ref[i, at, :], 1, 1)
            gate_pre, up_pre = gate_pre_ref[:, at], up_pre_ref[:, at]
            sigmoid = jax.nn.sigmoid(gate_pre)
            dgate = grad_inner * up_pre * sigmoid * (1.0 + gate_pre * (1.0 - sigmoid))
            dgate_ref[i, :, at] = dgate.astype(BF16)
            dup_ref[i, :, at] = (grad_inner * (gate_pre * sigmoid)).astype(BF16)

        for n in range(width // TF):
            backward(n)
        save(3, i)
        save(4, i)

        def to_rows(n):
            at = slice(n * TD, (n + 1) * TD)
            back = dot(dgate_ref[i], gate_ref[i, at, :], 1, 1)
            back = back + dot(dup_ref[i], up_ref[i, at, :], 1, 1)
            back_ref[i + shift, :, at] = back.astype(BF16)

        for n in range(MODEL_WIDTH // TD):
            to_rows(n)

    each(n_experts, expert)
    def storing(i):
        source = made_ref.at[i] if emit else (scaled_ref, back_ref, gate_grad_ref)[i].at[0]
        return pltpu.make_async_copy(source, made_hbm[i], out_sem.at[i])

    if not emit:
        for i in range(3):
            storing(i).start()
    else:
        if prior:
            for i in prior_in:
                arrivals[i]().wait()
        table_rows = x_ref.shape[1] - tokens_here
        tall = tokens_here + table_rows
        shape = (table_rows, MODEL_WIDTH)

        def scatter(b):
            row_index = lax.broadcasted_iota(jnp.int32, shape, 0)
            lane_group = lax.broadcasted_iota(jnp.int32, shape, 1) // tokens_here
            slots = pl.ds(pl.multiple_of(b * capacity, capacity), capacity)
            pick = pick_ref[b]

            def spread(n):
                at = slice(n * TD, (n + 1) * TD)
                made = jnp.concatenate([back_ref[0, slots, at], back_ref[1, slots, at]], axis=0)
                made_ref[b, :tokens_here, at] = dot(pick, made, 0, 0).astype(BF16)
                made = jnp.concatenate([scaled_ref[0, slots, at], scaled_ref[1, slots, at]], axis=0)
                made_ref[b, tall:, at] = dot(pick, made, 0, 0).astype(BF16)

            for n in range(MODEL_WIDTH // TD):
                spread(n)
            table = jnp.zeros(shape, F32)
            for e in range(2):
                table_row, group = place(ids[e])
                picked = pick[e * capacity : (e + 1) * capacity].astype(F32)
                line = jnp.sum(picked * gate_grad_ref[e, slots, :1], axis=0, keepdims=True)
                coarse = line.astype(BF16).astype(F32)
                here = lane_group == group
                for first, part in ((0, coarse), (per, line - coarse)):
                    wide = jnp.concatenate([part] * groups, axis=1)
                    table = table + jnp.where(here & (row_index == table_row + first), wide, 0.0)
            made_ref[b, tokens_here:tall, :] = table.astype(BF16)
            for turn in range(n_blocks):
                pl.when(b == turn)(lambda turn=turn: storing(turn).start())

        each(n_blocks, scatter)
    for turn in range(n_experts):
        for which in range(5):
            saving(which, turn).wait()
    for i in range(len(made_hbm)):
        storing(i).wait()


def run_experts(numbers, x_blocks, g_blocks, weights, experts, saved, first, total, capacity, prior=()):
    tokens_here = g_blocks[0][0].shape[0]
    block_rows = x_blocks[0][0].shape[0]
    width = weights[0].shape[2]
    n_blocks, n_here = len(x_blocks), len(experts)
    rows = n_blocks * capacity
    per = lax.axis_size("row") * tokens_here // MODEL_WIDTH
    emit = bool(prior) or n_here == 2
    sources = tuple(len(v) for v in x_blocks)
    plan = (sources, tuple(experts), first, bool(prior), saved is not None)
    hbm = pl.BlockSpec(memory_space=pltpu.HBM)
    if emit:
        made = [jax.ShapeDtypeStruct((tokens_here + block_rows, MODEL_WIDTH), BF16)] * n_blocks
    else:
        made = [jax.ShapeDtypeStruct((rows, MODEL_WIDTH), BF16)] * 2
        made.append(jax.ShapeDtypeStruct((rows, 128), F32))
    kept = [jax.ShapeDtypeStruct((2, total, MODEL_WIDTH), BF16)] * 2
    kept += [jax.ShapeDtypeStruct((2, total, width), BF16)] * 3
    operands = [w for v in (*x_blocks, *g_blocks) for w in v]
    for e in experts:
        operands += weights[3:] if e else weights[:3]
    operands += prior
    handed = 1 + len(operands)
    aliases = {}
    if saved is not None:
        operands += saved
        aliases = {handed + i: len(made) + i for i in range(5)}
    results = pl.pallas_call(
        functools.partial(experts_kernel, tokens_here, capacity, per, plan),
        out_shape=made + kept,
        in_specs=[pl.BlockSpec(memory_space=pltpu.SMEM)] + [hbm] * len(operands),
        out_specs=[hbm] * (len(made) + 5),
        scratch_shapes=[
            pltpu.VMEM((n_blocks, block_rows, MODEL_WIDTH), BF16),
            pltpu.VMEM((n_blocks, tokens_here, MODEL_WIDTH), BF16),
        ]
        + [pltpu.VMEM((n_here, *v.shape[1:]), BF16) for v in weights[:3]]
        + [pltpu.VMEM((n_blocks, *made[0].shape) if emit else (16, 128), BF16)]
        + [pltpu.VMEM((n_here, rows, MODEL_WIDTH), BF16)] * 2
        + [pltpu.VMEM((n_here, rows, width), BF16)] * 3
        + [
            pltpu.VMEM((n_blocks, (2 if emit else 1) * capacity, tokens_here), BF16),
            pltpu.VMEM((n_here, rows, MODEL_WIDTH), BF16),
            pltpu.VMEM((rows, width), F32),
            pltpu.VMEM((rows, width), F32),
            pltpu.VMEM((n_here, rows, 128), F32),
            pltpu.VMEM((2 if emit else 1, rows, MODEL_WIDTH), BF16),
            pltpu.VMEM((2 if emit else 1, rows, MODEL_WIDTH), BF16),
            pltpu.VMEM((2 if emit else 1, rows, 128), F32),
            pltpu.SemaphoreType.DMA((2 * n_blocks + 14,)),
            pltpu.SemaphoreType.DMA((len(made),)),
            pltpu.SemaphoreType.DMA((5, n_here)),
        ],
        input_output_aliases=aliases,
        compiler_params=pltpu.CompilerParams(vmem_limit_bytes=VMEM_ALL),
        cost_estimate=pl.CostEstimate(flops=1000, bytes_accessed=1000, transcendentals=0),
        name="experts",
    )(numbers, *operands)
    return list(results[: len(made)]), list(results[len(made) :])


def swap_halves(values):
    width = values.shape[1]
    half = HEAD_SIZE // 2
    lane = lax.broadcasted_iota(jnp.int32, values.shape, 1)
    return jnp.where(
        lane % HEAD_SIZE < half,
        pltpu.roll(values, width - half, 1),
        pltpu.roll(values, half, 1),
    )


def turn(values, cosine, sine_part):
    times = values.shape[1] // cosine.shape[1]
    wide = [jnp.concatenate([v] * times, axis=1) for v in (cosine, sine_part)]
    return values * wide[0] + swap_halves(values) * wide[1]


def rms_factor(values):
    return lax.rsqrt(jnp.mean(values * values, axis=-1, keepdims=True) + EPSILON)


def block_bias(seg_col_ref, seg_row_ref, first, rows, keys):
    queries = lax.broadcasted_iota(jnp.int32, (rows, keys), 0) + first
    at = lax.broadcasted_iota(jnp.int32, (rows, keys), 1)
    same = seg_col_ref[first : first + rows, :] == seg_row_ref[:, :keys]
    return jnp.where(same & (at <= queries), 0.0, -1e30)


def head_lanes(number):
    return slice(number * HEAD_SIZE, (number + 1) * HEAD_SIZE)


def attend_kernel(n_head, head_ref, *refs):
    token_refs = refs[:n_head]
    seg_col, seg_row, gain, w_q, w_k, w_v, w_o, cos_ref, sin_ref = refs[n_head : n_head + 9]
    normed_ref, q_ref, k_ref, v_ref, mixed_ref, lse_ref, own_ref, other_ref = refs[n_head + 9 : n_head + 17]
    part_ref, bias_ref = refs[n_head + 17 :]
    rows = token_refs[0].shape[0]
    head_at = head_ref[0]
    scale = HEAD_SIZE ** (-0.5)
    for k in range(n_head):
        x = token_refs[k][...].astype(F32)
        at = pl.ds(pl.multiple_of((head_at ^ k) * rows, rows), rows)
        normed_ref[at, :] = (x * rms_factor(x) * gain[...]).astype(BF16)
    normed = normed_ref[...]
    cosine, sine_part = cos_ref[...], sin_ref[...]
    q_ref[...] = (turn(dot(normed, w_q[...], 1, 0), cosine, sine_part).astype(BF16) * scale).astype(BF16)
    k_ref[...] = turn(dot(normed, w_k[...], 1, 0), cosine, sine_part).astype(BF16)
    v_ref[...] = dot(normed, w_v[...], 1, 0).astype(BF16)
    kv = k_ref.shape[1] // HEAD_SIZE
    per_group = q_ref.shape[1] // k_ref.shape[1]
    lane = lax.broadcasted_iota(jnp.int32, (rows, lse_ref.shape[1]), 1)
    wide_q, wide_k = 2 * per_group * HEAD_SIZE, 2 * HEAD_SIZE
    for i in range(n_head):
        first, keys = i * rows, (i + 1) * rows
        bias_ref[:, :keys] = block_bias(seg_col, seg_row, first, rows, keys)
        lse_ref[first:keys, :] = jnp.zeros((rows, lse_ref.shape[1]), F32)

        def pair(jj, first=first, keys=keys):
            q_at = pl.ds(pl.multiple_of(jj * wide_q, wide_q), wide_q)
            k_at = pl.ds(pl.multiple_of(jj * wide_k, wide_k), wide_k)
            query_all, key_all, value_all = q_ref[first:keys, q_at], k_ref[:keys, k_at], v_ref[:keys, k_at]
            made = []
            log_totals = lse_ref[first:keys, :]
            for h in range(2 * per_group):
                j = h // per_group
                key, value = key_all[:, head_lanes(j)], value_all[:, head_lanes(j)]
                scores = dot(query_all[:, head_lanes(h)], key, 1, 1) + bias_ref[:, :keys]
                highest = jnp.max(scores, axis=1, keepdims=True)
                exponent = jnp.exp(scores - highest)
                total = jnp.sum(exponent, axis=1, keepdims=True)
                log_totals = jnp.where(
                    lane == jj * (2 * per_group) + h, highest + jnp.log(total), log_totals
                )
                probs = (exponent * (1.0 / total)).astype(BF16)
                made.append(dot(probs, value, 1, 0).astype(BF16))
            mixed_ref[first:keys, q_at] = jnp.concatenate(made, axis=1)
            lse_ref[first:keys, :] = log_totals

        each(kv // 2, pair)
    part_ref[...] = dot(mixed_ref[...], w_o[...], 1, 0)
    own_ref[...] = part_ref[pl.ds(pl.multiple_of(head_at * rows, rows), rows), :]
    for k in range(1, n_head):
        at = pl.ds(pl.multiple_of((head_at ^ k) * rows, rows), rows)
        other_ref[k - 1] = part_ref[at, :].astype(BF16)


def attend_back_kernel(n_head, head_ref, *refs):
    token_refs, refs = refs[:n_head], refs[n_head:]
    grad_refs = refs[:n_head]
    seg_col, seg_row, w_q, w_k, w_v, w_o, cos_ref, sin_ref = refs[n_head : n_head + 8]
    q_ref, k_ref, v_ref, lse_ref = refs[n_head + 8 : n_head + 12]
    full_ref, proj_ref, own_ref, other_ref, gain_ref = refs[n_head + 12 : n_head + 17]
    gm_ref, dq_ref, dk_ref, dv_ref, part_ref, bias_ref = refs[n_head + 17 :]
    rows = grad_refs[0].shape[0]
    head_at = head_ref[0]
    scale = HEAD_SIZE ** (-0.5)
    for k in range(n_head):
        at = pl.ds(pl.multiple_of((head_at ^ k) * rows, rows), rows)
        full_ref[at, :] = grad_refs[k][...]
    gm_ref[...] = dot(full_ref[...], w_o[...], 1, 1).astype(BF16)
    cosine, sine_part = cos_ref[...], -sin_ref[...]
    kv = k_ref.shape[1] // HEAD_SIZE
    per_group = q_ref.shape[1] // k_ref.shape[1]
    dk_ref[...] = jnp.zeros(dk_ref.shape, F32)
    dv_ref[...] = jnp.zeros(dv_ref.shape, F32)
    lane = lax.broadcasted_iota(jnp.int32, (rows, lse_ref.shape[1]), 1)
    wide_q, wide_k = 2 * per_group * HEAD_SIZE, 2 * HEAD_SIZE
    for i in range(n_head):
        first, keys = i * rows, (i + 1) * rows
        bias_ref[:, :keys] = block_bias(seg_col, seg_row, first, rows, keys)

        def pair(jj, first=first, keys=keys):
            q_at = pl.ds(pl.multiple_of(jj * wide_q, wide_q), wide_q)
            k_at = pl.ds(pl.multiple_of(jj * wide_k, wide_k), wide_k)
            query_all, grad_all = q_ref[first:keys, q_at], gm_ref[first:keys, q_at]
            key_all, value_all = k_ref[:keys, k_at], v_ref[:keys, k_at]
            log_totals = lse_ref[first:keys, :]
            made, dk_all, dv_all = [], [], []
            for j in range(2):
                key, value = key_all[:, head_lanes(j)], value_all[:, head_lanes(j)]
                dk, dv = 0.0, 0.0
                for h in range(j * per_group, (j + 1) * per_group):
                    query, grad = query_all[:, head_lanes(h)], grad_all[:, head_lanes(h)]
                    mine = jnp.where(lane == jj * (2 * per_group) + h, log_totals, 0.0)
                    log_total = jnp.sum(mine, axis=1, keepdims=True)
                    probs = jnp.exp(dot(query, key, 1, 1) + bias_ref[:, :keys] - log_total)
                    grad_probs = dot(grad, value, 1, 1)
                    middle = jnp.sum(probs * grad_probs, axis=1, keepdims=True)
                    ds = (probs * (grad_probs - middle)).astype(BF16)
                    made.append(dot(ds, key, 1, 0) * scale)
                    dk = dk + dot(query, ds, 0, 0)
                    dv = dv + dot(grad, probs.astype(BF16), 0, 0)
                dk_all.append(dk)
                dv_all.append(dv)
            dq_ref[first:keys, q_at] = jnp.concatenate(made, axis=1)
            dk_ref[k_at, :keys] += jnp.concatenate(dk_all, axis=0)
            dv_ref[k_at, :keys] += jnp.concatenate(dv_all, axis=0)

        each(kv // 2, pair)
    width_q, width_k = q_ref.shape[1], k_ref.shape[1]
    proj_ref[:, :width_q] = turn(dq_ref[...], cosine, sine_part).astype(BF16)
    proj_ref[:, width_q : width_q + width_k] = turn(dk_ref[...].T, cosine, sine_part).astype(BF16)
    proj_ref[:, width_q + width_k :] = dv_ref[...].T.astype(BF16)
    part_ref[...] = (
        dot(proj_ref[:, :width_q], w_q[...], 1, 1)
        + dot(proj_ref[:, width_q : width_q + width_k], w_k[...], 1, 1)
        + dot(proj_ref[:, width_q + width_k :], w_v[...], 1, 1)
    )
    gain = jnp.zeros(gain_ref.shape, F32)
    for k in range(n_head):
        part = part_ref[pl.ds(pl.multiple_of((head_at ^ k) * rows, rows), rows), :]
        x = token_refs[k][...].astype(F32)
        gain = gain + jnp.sum(part * (x * rms_factor(x)), axis=0, keepdims=True)
        if k:
            other_ref[k - 1] = part.astype(BF16)
        else:
            own_ref[...] = part
    gain_ref[...] = gain


def weight_grads_kernel(share, core_ref, normed_ref, proj_ref, full_ref, mixed_ref, own_ref, other_ref, all_ref):
    core = core_ref[0]
    width = proj_ref.shape[1]
    all_ref[:, :width] = dot(normed_ref[...], proj_ref[...], 0, 0)
    all_ref[:, width:] = dot(full_ref[...], mixed_ref[...], 0, 0)
    for m in range(own_ref.shape[0] // share):
        at = slice(m * share, (m + 1) * share)
        own = pl.ds(pl.multiple_of((2 * m + core) * share, share), share)
        other = pl.ds(pl.multiple_of((2 * m + 1 - core) * share, share), share)
        own_ref[at, :] = all_ref[own, :]
        other_ref[at, :] = all_ref[other, :].astype(BF16)


def expert_grads_kernel(n_head, axis, heads_first, head_ref, lhs_ref, rhs_ref, *refs):
    head_at = head_ref[0]
    own_ref, rest_ref, away_ref, all_ref = refs
    size = own_ref.shape[axis]

    def part(k):
        at = pl.ds(pl.multiple_of((head_at ^ k) * size, size), size)
        return all_ref[at, :] if axis == 0 else all_ref[:, at]

    def first():
        own_ref[...] = part(0)
        for k in range(1, n_head):
            if heads_first:
                away_ref[k - 1, 0] = part(k).astype(BF16)
            else:
                rest_ref[k - 1] = part(k)

    def second():
        for k in range(n_head):
            if not heads_first:
                away_ref[k] = part(k).astype(BF16)
            elif k:
                away_ref[k - 1, 1] = part(k).astype(BF16)
            else:
                rest_ref[0] = part(0)

    def turn(e):
        all_ref[...] = dot(lhs_ref[e], rhs_ref[e], 0, 0)
        pl.when(e == 0)(first)
        pl.when(e == 1)(second)

    each(2, turn)


def final_kernel(n_head, tokens_ref, grad_hidden_ref, gain, own_ref, *refs):
    total = own_ref[...]
    for part in refs[: n_head - 1]:
        total = total + part[...].astype(F32)
    x = tokens_ref[...].astype(F32)
    factor = rms_factor(x)
    weighted = total * gain[...]
    middle = jnp.mean(weighted * x, axis=-1, keepdims=True)
    refs[-1][...] = grad_hidden_ref[...] + factor * (weighted - x * factor * factor * middle)


def hidden_kernel(n_head, tokens_ref, own_ref, *refs):
    arrived = refs[: n_head - 1]
    gain, router_t, slots_ref, chosen_ref = refs[n_head - 1 : n_head + 3]
    block_ref, hidden_ref, gates_ref = refs[n_head + 3 :]
    rows = tokens_ref.shape[0]
    attention = own_ref[...]
    for part in arrived:
        attention = attention + part[...].astype(F32)
    hidden = tokens_ref[...].astype(F32) + attention
    hidden_ref[...] = hidden
    normed = (hidden * rms_factor(hidden) * gain[...]).astype(BF16)
    block_ref[:rows, :] = normed
    chosen = chosen_ref[...] > 0.0
    logits = jnp.where(chosen, dot(router_t[...], normed, 1, 1), -1e30)
    gates = jnp.where(chosen, jnp.exp(logits - jnp.max(logits, axis=0, keepdims=True)), 0.0)
    gates = gates / jnp.sum(gates, axis=0, keepdims=True)
    gates_ref[...] = gates
    coarse = gates.astype(BF16).astype(F32)
    groups = MODEL_WIDTH // rows
    per = gates.shape[0] // groups
    lines = [
        jnp.concatenate([v[q * per : (q + 1) * per] for q in range(groups)], axis=1)
        for v in (coarse, gates - coarse, slots_ref[...])
    ]
    spare = block_ref.shape[0] - rows - 3 * per
    if spare:
        lines.append(jnp.zeros((spare, MODEL_WIDTH), F32))
    block_ref[rows:, :] = jnp.concatenate(lines, axis=0).astype(BF16)


def grad_hidden_kernel(n_parts, *refs):
    parts = refs[:n_parts]
    hidden_ref, gain, router_t, gates_ref, block_ref, cotangent_ref = refs[n_parts : n_parts + 6]
    grad_ref, low_ref, small_ref = refs[n_parts + 6 :]
    rows = hidden_ref.shape[0]
    tall = block_ref.shape[0]
    total = parts[0][:tall, :].astype(F32)
    for part in parts[1:]:
        total = total + part[:tall, :].astype(F32)
    gates = gates_ref[...]
    groups = MODEL_WIDTH // rows
    per = gates.shape[0] // groups
    lines = total[rows : rows + per] + total[rows + per : rows + 2 * per]
    grad_gates = jnp.concatenate(
        [lines[:, q * rows : (q + 1) * rows] for q in range(groups)], axis=0
    )
    grad_logits = gates * (grad_gates - jnp.sum(gates * grad_gates, axis=0, keepdims=True))
    coarse = grad_logits.astype(BF16)
    fine = (grad_logits - coarse.astype(F32)).astype(BF16)
    normed = block_ref[:rows, :]
    n_experts = gates.shape[0]
    small_ref[:n_experts, :] = dot(coarse, normed, 1, 0) + dot(fine, normed, 1, 0)
    upstream = total[:rows] + dot(coarse, router_t[...], 0, 0) + dot(fine, router_t[...], 0, 0)
    hidden = hidden_ref[...]
    factor = rms_factor(hidden)
    weighted = upstream * gain[...]
    middle = jnp.mean(weighted * hidden, axis=-1, keepdims=True)
    grad = cotangent_ref[...].astype(F32) + factor * (weighted - hidden * factor * factor * middle)
    grad_ref[...] = grad
    low_ref[...] = grad.astype(BF16)
    small_ref[n_experts:, :] = jnp.sum(upstream * hidden * factor, axis=0, keepdims=True)


def call(kernel, name, operands, out_shape, scratch_shapes=(), scalars=0, room=VMEM_BYTES):
    vmem = pl.BlockSpec(memory_space=pltpu.VMEM)
    smem = pl.BlockSpec(memory_space=pltpu.SMEM)
    made = pl.pallas_call(
        kernel,
        out_shape=out_shape,
        in_specs=[smem] * scalars + [vmem] * (len(operands) - scalars),
        out_specs=[vmem] * len(out_shape),
        scratch_shapes=list(scratch_shapes),
        compiler_params=pltpu.CompilerParams(vmem_limit_bytes=room),
        cost_estimate=pl.CostEstimate(flops=1000, bytes_accessed=1000, transcendentals=0),
        name=name,
    )(*operands)
    return list(made)


def local(
    tokens,
    segments,
    routes,
    norm_gain,
    w_query,
    key_weight,
    value_weight,
    w_output,
    moe_gain,
    w_router,
    w_gate,
    w_up,
    w_down,
    cotangent,
):
    local_rows = tokens.shape[0]
    length = segments.shape[0]
    n_experts = w_router.shape[1]
    capacity = local_rows * TOPK * 5 // (4 * n_experts)
    width_query = w_query.shape[1]
    width_key = key_weight.shape[1]
    n_row = lax.axis_size("row")
    n_head = lax.axis_size("head")
    n_outer = n_row // 4
    row_at = lax.axis_index("row")
    head_at = lax.axis_index("head")
    at_end = (row_at // 4 % 3 == 0).astype(jnp.int32)
    numbers = jnp.stack([row_at, head_at & 1, at_end]).astype(jnp.int32)

    routes_t = routes.T
    expert_index = jnp.arange(n_experts, dtype=jnp.int32)[:, None]
    chosen = jnp.any(routes_t[:, None, :] == expert_index[None], axis=0)
    t_index = jnp.arange(local_rows, dtype=jnp.int32)
    before = (t_index[:, None] < t_index[None, :]).astype(BF16)
    rank = dot(chosen.astype(BF16), before, 1, 0)
    slots = jnp.where(chosen & (rank < capacity), rank, -1.0)
    chosen = chosen.astype(F32)
    router_t = w_router.T
    head_number = head_at.astype(jnp.int32).reshape(1)

    line = n_outer == 4
    inner = [(i, i ^ 12) for i in range(4, 12)]
    outward = [(i, i ^ 4) for i in range(4, 12)]
    ends = [*range(4), *range(12, 16)]
    ends_in = [(i, i ^ 8) for i in ends]
    ends_over = [(i, i ^ 12) for i in ends]
    inner_out = [(i, i ^ 8) for i in range(4, 12)]

    def send(value, pairs):
        return lax.ppermute(value, "row", pairs)

    def share_of(weight):
        size = weight.shape[1] // 2
        return lax.dynamic_slice_in_dim(weight[0], (head_at & 1) * size, size, 0)

    def head_all(values):
        return [head_swap(values[k - 1], k) for k in range(1, n_head)]

    def low(value):
        return value.astype(BF16)

    def shape(rows, columns, dtype=BF16):
        return jax.ShapeDtypeStruct((rows, columns), dtype)

    seg_col, seg_row = segments[:, None], segments[None, :]
    gain_row, moe_gain_row = norm_gain[None], moe_gain[None]

    tokens_other = head_all([tokens] * (n_head - 1))
    frequency = ROPE_BASE ** (-2.0 * jnp.arange(HEAD_SIZE // 2, dtype=F32) / HEAD_SIZE)
    angles = jnp.arange(length, dtype=F32)[:, None] * frequency[None, :]
    cosine, sine_part = jnp.cos(angles), jnp.sin(angles)
    cosine = jnp.concatenate([cosine] * 4, axis=1)
    sine_part = jnp.concatenate([-sine_part, sine_part] * 2, axis=1)
    gate_share, down_share = share_of(w_gate), share_of(w_down)
    width = gate_share.shape[1]
    pieces = [down_share[:, k : k + width] for k in range(0, down_share.shape[1], width)]
    gate_here = row_swap(gate_share, 2)
    down_here = row_swap(jnp.concatenate(pieces, axis=0), 2)
    if line:
        g_far = [row_swap(cotangent, 4), send(cotangent, inner)]
    else:
        g_far = [row_swap(cotangent, 4 * o) for o in range(1, n_outer)]
    tokens_other, cosine, sine_part, seg_col, slots, chosen = tie(
        tokens_other, cosine, sine_part, seg_col, slots, chosen
    )
    g_far, w_up_later, _ = tie(g_far, w_up, seg_col)

    g_slabs = [cotangent, *g_far]
    if line:
        g_far += [send(g_far[1], outward), send(g_far[0], inner)]
    head_parts = [
        shape(local_rows, MODEL_WIDTH, F32),
        jax.ShapeDtypeStruct((n_head - 1, local_rows, MODEL_WIDTH), BF16),
    ]
    normed_full, queries, keys, values, mixed_heads, log_totals, part_own, part_other = call(
        functools.partial(attend_kernel, n_head),
        "attend",
        [head_number, tokens, *tokens_other, seg_col, seg_row, gain_row]
        + [w_query, key_weight, value_weight, w_output, cosine, sine_part],
        [shape(length, MODEL_WIDTH), shape(length, width_query)]
        + [shape(length, width_key)] * 2
        + [shape(length, width_query), shape(length, 128, F32), *head_parts],
        [pltpu.VMEM((length, MODEL_WIDTH), F32), pltpu.VMEM((local_rows, length), F32)],
        scalars=1,
        room=VMEM_ALL,
    )
    part_other, part_own, gate_here, down_here, g_far, w_up_later = tie(
        part_other, part_own, gate_here, down_here, g_far, w_up_later
    )

    arrived = head_all(part_other)
    up_here = row_swap(w_up_later, 2)
    g_last = send(g_far[3], outward) if line else cotangent
    arrived, part_own, g_last = tie(arrived, part_own, g_last)
    table_rows = -(-3 * n_experts * local_rows // MODEL_WIDTH // 16) * 16
    x_block, hidden, gates = call(
        functools.partial(hidden_kernel, n_head),
        "hidden",
        [tokens, part_own, *arrived, moe_gain_row, router_t, slots, chosen],
        [
            shape(local_rows + table_rows, MODEL_WIDTH),
            shape(local_rows, MODEL_WIDTH, F32),
            shape(n_experts, local_rows, F32),
        ],
    )
    tall = x_block.shape[0]
    saved = None
    made = []

    def cores(values):
        return [row_swap(v, 1) for v in values]

    def pass_on(chunk):
        made[chunk][1] = row_swap(made[chunk][1], 1)

    def near(which, chunk):
        own, other = (v[:tall] if which else v[tall:] for v in made[chunk])
        return own.astype(F32) + other.astype(F32)

    def experts(x_blocks, g_blocks, which, prior=()):
        nonlocal saved
        first = 2 * len(made) * capacity
        results, saved = run_experts(
            numbers, x_blocks, g_blocks, weights, which, saved, first, total_rows, capacity, prior
        )
        if which == (0,):
            return results
        made.extend(results[i : i + 2] for i in range(0, len(results), 2))

    total_rows = 2 * n_outer * capacity
    gate_there = head_swap(gate_here, 1)
    x_core = row_swap(x_block, 1)
    if line:
        x_far = [row_swap(x_block, 4), send(x_block, inner)]
    else:
        x_far = [row_swap(x_block, 4 * o) for o in range(1, n_outer)]
    x_block, x_core, x_far, up_here, gate_there, down_later, g_slabs, g_far, g_last, cotangent = tie(
        x_block, x_core, x_far, up_here, gate_there, down_here, g_slabs, g_far, g_last, cotangent
    )
    down_there = head_swap(down_later, 1)
    weights = [w_gate, w_up, w_down, gate_here, gate_there, down_here, down_there, up_here]

    if line:
        x_near, x_mid = x_far
        x_near_core = row_swap(x_near, 1)
        g_cores = cores(g_slabs[:2])
        x_near, x_mid, x_near_core, g_cores, g_far = tie(x_near, x_mid, x_near_core, g_cores, g_far)
        x_out, x_deep = send(x_mid, outward), send(x_near, inner)
        x_pairs = [[x_block], [x_core], [x_near], [x_near_core]]
        g_pairs = [[cotangent], [g_cores[0]], [g_slabs[1]], [g_cores[1]]]
        prior = experts(x_pairs, g_pairs, (0,))
        x_out, x_deep, prior, saved, down_there, g_far, x_mid, g_mid, g_last = tie(
            x_out, x_deep, prior, saved, down_there, g_far, x_mid, g_slabs[2], g_last
        )
        weights[6] = down_there
        x_last = send(x_deep, outward)
        x_mid_core, g_mid_core, g_out_core = cores([x_mid, g_mid, g_far[2]])
        experts(x_pairs, g_pairs, (1,), prior)
        x_last, x_mid_core, g_mid_core, g_out_core, made[0], made[1], saved, x_out = tie(
            x_last, x_mid_core, g_mid_core, g_out_core, made[0], made[1], saved, x_out
        )
        x_out_core = row_swap(x_out, 1)
        x_out_core, x_last, x_deep, g_deep, g_last, made[0] = tie(
            x_out_core, x_last, x_deep, g_far[3], g_last, made[0]
        )
        pass_on(1)
        x_deep_core, x_last_core, g_deep_core, g_last_core = cores([x_deep, x_last, g_deep, g_last])
        g_two = [[g_mid, g_far[2]], [g_mid_core, g_out_core]]
        experts([[x_mid, x_out], [x_mid_core, x_out_core]], g_two, (0, 1))
        x_deep_core, x_last_core, g_deep_core, g_last_core, made[0], made[1], made[2], saved = tie(
            x_deep_core, x_last_core, g_deep_core, g_last_core, made[0], made[1], made[2], saved
        )
        pass_on(2)
        made[0], made[1], made[2], x_deep, x_last = tie(made[0], made[1], made[2], x_deep, x_last)
        g_three = [[g_deep, g_last], [g_deep_core, g_last_core]]
        two, sum_one = low(near(1, 2)), low(near(1, 1))
        first_sums = [send(two, ends_in), send(two, inner), row_swap(sum_one, 4)]
        x_deep, x_last, _, _ = tie(x_deep, x_last, two, sum_one)
        experts([[x_deep, x_last], [x_deep_core, x_last_core]], g_three, (0, 1))
    else:
        for o, x in enumerate([x_block, *x_far]):
            experts([[x], [row_swap(x, 1)]], [[g_slabs[o]], [row_swap(g_slabs[o], 1)]], (0, 1))
        for o in range(n_outer):
            pass_on(o)
        one = [row_swap(low(near(1, o)), 4 * o) for o in range(1, n_outer)]

    rows_in, gprod, inner_act, dgate, dup = saved

    def expert_grads(lhs, rhs, axis, heads_first):
        sizes = [lhs.shape[2], rhs.shape[2]]
        part = list(sizes)
        part[axis] //= n_head
        rest = (1, *part) if heads_first else (n_head - 1, *part)
        away = (n_head - 1, 2, *part) if heads_first else (n_head, *part)
        return call(
            functools.partial(expert_grads_kernel, n_head, axis, heads_first),
            "expert_grads",
            [head_number, lhs, rhs],
            [
                jax.ShapeDtypeStruct(tuple(part), F32),
                jax.ShapeDtypeStruct(rest, F32),
                jax.ShapeDtypeStruct(away, BF16),
            ],
            [pltpu.VMEM(tuple(sizes), F32)],
            scalars=1,
        )

    if line:
        made[0], made[3], inner_act, gprod, rows_in, dgate, dup = tie(
            made[0], made[3], inner_act, gprod, rows_in, dgate, dup
        )
    up_parts = expert_grads(rows_in, dup, 0, False)
    down_parts = expert_grads(inner_act, gprod, 1, True)
    up_away, down_away = up_parts[2], down_parts[2]
    if line:
        first_sums, made[0], made[3], up_away, down_away, rows_in, dgate = tie(
            first_sums, made[0], made[3], up_away, down_away, rows_in, dgate
        )
        pass_on(0)
        pass_on(3)
        made[0], made[3], first_sums, up_away, down_away, rows_in, dgate = tie(
            made[0], made[3], first_sums, up_away, down_away, rows_in, dgate
        )
        three = low(near(1, 3))
        last_sums = [send(three, ends_over), send(three, inner_out)]
    up_away = row_swap(up_away, 2)
    down_away = head_all(down_away)
    gate_parts = expert_grads(rows_in, dgate, 0, False)
    gate_away = gate_parts[2]
    if line:
        total = near(1, 0) + sum(v.astype(F32) for v in first_sums)
        made_now, _ = tie(made, three)
        made = list(made_now)
        out_one, out_two, out_three = (low(near(0, o)) for o in range(1, 4))
        one = [total, *last_sums]
    else:
        one = [near(1, 0), *one]
        out_one = out_two = out_three = one[0]
    one, up_away, down_away, gate_away, made_now, out_one, out_two, out_three = tie(
        one, up_away, down_away, gate_away, made, out_one, out_two, out_three
    )
    made = list(made_now)
    grad_sum = one
    grad_hidden, grad_attention, early = call(
        functools.partial(grad_hidden_kernel, len(grad_sum)),
        "grad_hidden",
        [*grad_sum, hidden, moe_gain_row, router_t, gates, x_block, cotangent],
        [
            shape(local_rows, MODEL_WIDTH, F32),
            shape(local_rows, MODEL_WIDTH),
            shape(n_experts + 1, MODEL_WIDTH, F32),
        ],
    )
    made_now, up_away, down_away, gate_away, grad_attention = tie(
        made, up_away, down_away, gate_away, grad_attention
    )
    made = list(made_now)
    grad_arrived = head_all([grad_attention] * (n_head - 1))
    gate_away = row_swap(gate_away, 2)
    out_first = [send(out_two, inner), row_swap(out_one, 4)] if line else [out_two]
    up_rest = [low(v + w.astype(F32)) for v, w in zip(up_parts[1], up_away[1:])]
    down_rest = low(down_parts[1][0] + sum(v[1].astype(F32) for v in down_away))
    grad_arrived, up_rest, down_rest, made_now, out_two, out_three, out_first = tie(
        grad_arrived, up_rest, down_rest, made, out_two, out_three, out_first
    )
    made = list(made_now)
    up_last = head_all(up_rest)
    if line:
        out_first += [send(out_three, ends_over), send(out_three, inner_out)]
    else:
        out_first = grad_attention
    grad_full, grad_proj, grad_own, grad_other, gain_part = call(
        functools.partial(attend_back_kernel, n_head),
        "attend_back",
        [head_number, tokens, *tokens_other, grad_attention, *grad_arrived, seg_col, seg_row]
        + [w_query, key_weight, value_weight, w_output, cosine, sine_part]
        + [queries, keys, values, log_totals],
        [
            shape(length, MODEL_WIDTH),
            shape(length, width_query + 2 * width_key),
            *head_parts,
            shape(1, MODEL_WIDTH, F32),
        ],
        [
            pltpu.VMEM((length, width_query), BF16),
            pltpu.VMEM((length, width_query), F32),
            pltpu.VMEM((width_key, length), F32),
            pltpu.VMEM((width_key, length), F32),
            pltpu.VMEM((length, MODEL_WIDTH), F32),
            pltpu.VMEM((local_rows, length), F32),
        ],
        scalars=1,
        room=VMEM_ALL,
    )
    grad_full, grad_proj, grad_other, gain_part, up_last, gate_away, down_rest, *outs = tie(
        grad_full, grad_proj, grad_other, gain_part, up_last, gate_away, down_rest,
        out_one, out_two,
    )
    out_one, out_two = outs
    share = MODEL_WIDTH // n_row
    width_all = width_query + 2 * width_key
    small = jnp.concatenate([early, gain_part], axis=0)
    weights_own, weights_other = call(
        functools.partial(weight_grads_kernel, share),
        "weight_grads",
        [(row_at % 2).astype(jnp.int32).reshape(1), normed_full, grad_proj, grad_full, mixed_heads],
        [
            shape(MODEL_WIDTH // 2, width_all + width_query, F32),
            shape(MODEL_WIDTH // 2, width_all + width_query),
        ],
        [pltpu.VMEM((MODEL_WIDTH, width_all + width_query), F32)],
        scalars=1,
        room=VMEM_ALL,
    )
    small, weights_own, weights_other, made_now, out_first, out_one, out_two = tie(
        small, weights_own, weights_other, made, out_first, out_one, out_two
    )
    made = list(made_now)
    small_core = row_swap(small, 1)
    weights_core = row_swap(weights_other, 1)
    small, small_core, weights_own, weights_core = tie(small, small_core, weights_own, weights_core)
    small = small + small_core
    small_far = row_swap(small, 2)
    if line:
        out_first = [*out_first, send(out_two, ends_in)]
    else:
        out_first = small
    value = (weights_own + weights_core.astype(F32)).reshape(n_outer, 2, share, -1)
    bit = (row_at // 2) % 2
    other = low(lax.dynamic_index_in_dim(value, 1 - bit, 1, keepdims=False))
    value = lax.dynamic_index_in_dim(value, bit, 1, keepdims=False)
    small, other, value, grad_other, down_rest, gate_away, made_now, out_two = tie(
        small + small_far, other, value, grad_other, down_rest, gate_away, made, out_two
    )
    made = list(made_now)
    other_arrived = row_swap(other, 2)
    offset = 4
    while offset < n_row:
        small = small + row_swap(small, offset)
        offset *= 2
    offset = 1
    while offset < n_head:
        small = small + head_swap(small, offset)
        offset *= 2
    grad_arrived = head_all(grad_other)
    gate_rest = [low(v + w.astype(F32)) for v, w in zip(gate_parts[1], gate_away[1:])]
    mixed_out = hidden + near(0, 0)
    if line:
        mixed_out = mixed_out + sum(v.astype(F32) for v in out_first)
        last = []
    else:
        last = [row_swap(low(near(0, o)), 4 * o) for o in range(1, n_outer)]
    grad_arrived, value, other_arrived, small, gate_rest, last, mixed_out, down_rest = tie(
        grad_arrived, value, other_arrived, small, gate_rest, last, mixed_out, down_rest
    )
    gate_last = head_all(gate_rest)
    value = value + other_arrived.astype(F32)
    at = row_at // 4
    weights_sum = lax.dynamic_index_in_dim(value, at, 0, keepdims=False)
    weights_parts = [
        row_swap(low(lax.dynamic_index_in_dim(value, at ^ o, 0, keepdims=False)), 4 * o)
        for o in range(1, n_outer)
    ]
    down_last = row_swap(down_rest, 2)
    (grad_tokens,) = call(
        functools.partial(final_kernel, n_head),
        "final",
        [tokens, grad_hidden, gain_row, grad_own, *grad_arrived],
        [shape(local_rows, MODEL_WIDTH, F32)],
    )
    for part in last:
        mixed_out = mixed_out + part.astype(F32)
    mixed_out = mixed_out.astype(BF16)

    def add(own, *parts):
        for part in parts:
            own = own + part.astype(F32)
        return own

    down_sum = add(down_parts[0], *(v[0] for v in down_away), down_last)
    up_sum = add(up_parts[0], up_away[0], *up_last)
    gate_sum = add(gate_parts[0], gate_away[0], *gate_last)
    down_sum, up_sum, gate_sum, weights_parts = tie(down_sum, up_sum, gate_sum, weights_parts)
    weights_sum = add(weights_sum, *weights_parts)
    return (
        mixed_out,
        grad_tokens,
        small[n_experts + 1],
        weights_sum[:, :width_query],
        weights_sum[:, width_query : width_query + width_key],
        weights_sum[:, width_query + width_key : width_all],
        weights_sum[:, width_all:].T,
        small[n_experts],
        small[:n_experts].T,
        gate_sum[None],
        up_sum[None],
        down_sum[None],
    )


def solution(mesh):
    in_specs = (
        P(("row", "head"), None),
        P("row"),
        P(("row", "head"), None),
        P(),
        P(None, "head"),
        P(None, "head"),
        P(None, "head"),
        P("head", None),
        P(),
        P(),
        P("row", None, None),
        P("row", None, None),
        P("row", None, None),
        P(("row", "head"), None),
    )
    out_specs = (
        P(("row", "head"), None),
        P(("row", "head"), None),
        P(),
        P("row", "head"),
        P("row", "head"),
        P("row", "head"),
        P("head", "row"),
        P(),
        P(),
        P("row", "head", None),
        P("row", "head", None),
        P("row", None, "head"),
    )
    return jax.shard_map(local, mesh=mesh, in_specs=in_specs, out_specs=out_specs, check_vma=False)
```

```python
import functools

import jax
import jax.numpy as jnp
from jax import lax
from jax.experimental import pallas as pl
from jax.experimental.pallas import tpu as pltpu
from jax.sharding import PartitionSpec as P

MODEL_WIDTH = 1024
HEAD_SIZE = 64
VMEM_BYTES = 36 * 1024 * 1024
VMEM_ALL = 63 * 1024 * 1024
TOPK = 8

EPSILON = 1e-06
ROPE_BASE = 10000.0
F32 = jnp.float32
BF16 = jnp.bfloat16


def row_swap(value, offset):
    size = lax.axis_size("row")
    return lax.ppermute(value, "row", [(i, i ^ offset) for i in range(size)])


def head_swap(value, offset):
    size = lax.axis_size("head")
    return lax.ppermute(value, "head", [(i, i ^ offset) for i in range(size)])


def dot(a, b, ca, cb, **kw):
    return lax.dot_general(a, b, (((ca,), (cb,)), ((), ())), preferred_element_type=F32, **kw)


def tie(*values):
    return lax.optimization_barrier(values)


def each(count, body):
    lax.fori_loop(0, count, lambda i, carry: (body(i), carry)[1], 0)


def experts_kernel(tokens_here, capacity, per, plan, number_ref, *refs):
    sources, experts, rows_before, prior, handed_on = plan
    n_blocks, n_experts = len(sources), len(experts)
    emit = prior or n_experts == 2
    refs = list(refs)

    def pop(number):
        taken, refs[:] = refs[:number], refs[number:]
        return taken

    x_hbm = [pop(k) for k in sources]
    g_hbm = [pop(k) for k in sources]
    w_hbm = {e: pop(5 if e else 3) for e in experts}
    prior_hbm = pop(3) if prior else []
    if handed_on:
        pop(5)
    made_hbm = pop(n_blocks) if emit else pop(3)
    saved_hbm = pop(5)
    x_ref, g_ref, gate_ref, up_ref, down_ref, made_ref = pop(6)
    rows_ref, gprod_ref, inner_ref, dgate_ref, dup_ref = pop(5)
    pick_ref, g_rows_ref, gate_pre_ref, up_pre_ref, slot_ref = pop(5)
    scaled_ref, back_ref, gate_grad_ref, in_sem, out_sem, saved_sem = pop(6)
    ids = (number_ref[0], number_ref[0] ^ 2)
    bit, flag = number_ref[1], number_ref[2]
    arrivals = []

    def load(source, target):
        i = len(arrivals)

        def copy(k=0):
            return pltpu.make_async_copy(source[k](), target(), in_sem.at[i])

        if len(source) == 2:
            for k in range(2):
                pl.when(flag == k)(copy(k).start)
        else:
            copy().start()
        arrivals.append(copy)
        return i

    def whole(ref, *index):
        return lambda: ref.at[index] if index else ref

    def arrive(at, numbers):
        for turn, mine in enumerate(numbers):

            def wait(mine=mine):
                for i in mine:
                    arrivals[i]().wait()

            pl.when(at == turn)(wait)

    width = gate_ref.shape[2]
    depth = down_ref.shape[1] // 2
    rows_half = gate_ref.shape[1] // 2

    def halves(gate, down, index, i):
        def first():
            return gate_ref.at[i, pl.ds(pl.multiple_of(index * rows_half, rows_half), rows_half)]

        def second(k):
            at = pl.ds(pl.multiple_of(index * depth, depth), depth)
            return lambda: down_ref.at[i, at, k * width : (k + 1) * width]

        def part(k):
            return lambda: down.at[k * depth : (k + 1) * depth]

        return (whole(gate), first), [(part(k), second(k)) for k in range(down_ref.shape[2] // width)]

    tokens_in = [
        [
            load([whole(h) for h in x_hbm[b]], whole(x_ref, b)),
            load([whole(h) for h in g_hbm[b]], whole(g_ref, b)),
        ]
        for b in range(n_blocks)
    ]
    gate_in, up_in, down_in = [], [], []
    for i, e in enumerate(experts):
        if e == 0:
            gate_in.append([load([whole(w_hbm[e][0], 0)], whole(gate_ref, i))])
            up_in.append([load([whole(w_hbm[e][1], 0)], whole(up_ref, i))])
            down_in.append([load([whole(w_hbm[e][2], 0)], whole(down_ref, i))])
        else:
            gate_near, gate_far, down_near, down_far, up_h = w_hbm[e]
            gate_here, down_here = halves(gate_near, down_near, bit, i)
            gate_there, down_there = halves(gate_far, down_far, 1 - bit, i)
            gate_in.append([load([a], b) for a, b in (gate_here, gate_there)])
            up_in.append([load([whole(up_h, 0)], whole(up_ref, i))])
            down_in.append([load([a], b) for a, b in down_here + down_there])
    if prior:
        prior_in = [
            load([whole(prior_hbm[0])], whole(scaled_ref, 0)),
            load([whole(prior_hbm[1])], whole(back_ref, 0)),
            load([whole(prior_hbm[2])], whole(gate_grad_ref, 0)),
        ]

    def saving(which, turn):
        buffer = (rows_ref, gprod_ref, inner_ref, dgate_ref, dup_ref)[which]
        return pltpu.make_async_copy(
            buffer.at[turn],
            saved_hbm[which].at[experts[turn], pl.ds(rows_before, n_blocks * capacity)],
            saved_sem.at[which, turn],
        )

    def save(which, i):
        for turn in range(n_experts):
            pl.when(i == turn)(lambda turn=turn: saving(which, turn).start())

    groups = MODEL_WIDTH // tokens_here

    def place(number):
        return number % per, number // per

    def take(table, first, number):
        table_row, group = place(number)
        index = lax.broadcasted_iota(jnp.int32, table.shape, 0)
        line = jnp.sum(jnp.where(index == table_row + first, table, 0.0), axis=0, keepdims=True)
        picked = jnp.zeros((1, tokens_here), F32)
        for q in range(groups):
            part = line[:, q * tokens_here : (q + 1) * tokens_here]
            picked = picked + jnp.where(group == q, part, 0.0)
        return picked

    held = (0, 1) if emit else experts
    first_held = held.index(experts[0]) * capacity
    shift = 1 if prior else 0

    def gather(b):
        arrive(b, tokens_in)
        table = x_ref[b, tokens_here:, :].astype(F32)
        slot_index = lax.broadcasted_iota(jnp.int32, (capacity, tokens_here), 0).astype(F32)
        at = pl.ds(pl.multiple_of(b * capacity, capacity), capacity)
        for h, e in enumerate(held):
            pick = (slot_index == take(table, 2 * per, ids[e])).astype(F32)
            if e in experts:
                gate = take(table, 0, ids[e]) + take(table, per, ids[e])
                slot = jnp.sum(pick * gate, axis=1, keepdims=True)
                slot_ref[experts.index(e), at, :] = jnp.broadcast_to(slot, (capacity, 128))
            pick_ref[b, h * capacity : (h + 1) * capacity, :] = pick.astype(BF16)
        pick = pick_ref[b, first_held : first_held + n_experts * capacity, :]
        rows = dot(pick, x_ref[b, :tokens_here, :], 1, 0).astype(BF16)
        g_rows = dot(pick, g_ref[b], 1, 0).astype(BF16)
        for i in range(n_experts):
            rows_ref[i, at, :] = rows[i * capacity : (i + 1) * capacity]
            g_rows_ref[i, at, :] = g_rows[i * capacity : (i + 1) * capacity]

    each(n_blocks, gather)
    TF, TD = 512, 1024

    def tile_at(n):
        return slice(n * tile, (n + 1) * tile)

    def expert(i):
        save(0, i)
        arrive(i, gate_in)
        arrive(i, up_in)

        def forward(n):
            at = slice(n * TF, (n + 1) * TF)
            gate_pre = dot(rows_ref[i], gate_ref[i, :, at], 1, 0)
            up_pre = dot(rows_ref[i], up_ref[i, :, at], 1, 0)
            gate_pre_ref[:, at] = gate_pre
            up_pre_ref[:, at] = up_pre
            inner_ref[i, :, at] = (gate_pre * jax.nn.sigmoid(gate_pre) * up_pre).astype(BF16)

        for n in range(width // TF):
            forward(n)
        save(2, i)
        arrive(i, down_in)
        gate_grad_ref[i + shift] = jnp.zeros(gate_grad_ref.shape[1:], F32)

        def produce(n):
            at = slice(n * TD, (n + 1) * TD)
            slot = slot_ref[i, :, :1]
            produced = dot(inner_ref[i], down_ref[i, :, at], 1, 0).astype(BF16).astype(F32)
            g_rows = g_rows_ref[i, :, at].astype(F32)
            gate_grad_ref[i + shift] += jnp.sum(g_rows * produced, axis=1, keepdims=True)
            scaled_ref[i + shift, :, at] = (slot * produced).astype(BF16)
            gprod_ref[i, :, at] = (slot * g_rows).astype(BF16)

        for n in range(MODEL_WIDTH // TD):
            produce(n)
        save(1, i)

        def backward(n):
            at = slice(n * TF, (n + 1) * TF)
            grad_inner = dot(gprod_ref[i], down_ref[i, at, :], 1, 1)
            gate_pre, up_pre = gate_pre_ref[:, at], up_pre_ref[:, at]
            sigmoid = jax.nn.sigmoid(gate_pre)
            dgate = grad_inner * up_pre * sigmoid * (1.0 + gate_pre * (1.0 - sigmoid))
            dgate_ref[i, :, at] = dgate.astype(BF16)
            dup_ref[i, :, at] = (grad_inner * (gate_pre * sigmoid)).astype(BF16)

        for n in range(width // TF):
            backward(n)
        save(3, i)
        save(4, i)

        def to_rows(n):
            at = slice(n * TD, (n + 1) * TD)
            back = dot(dgate_ref[i], gate_ref[i, at, :], 1, 1)
            back = back + dot(dup_ref[i], up_ref[i, at, :], 1, 1)
            back_ref[i + shift, :, at] = back.astype(BF16)

        for n in range(MODEL_WIDTH // TD):
            to_rows(n)

    each(n_experts, expert)
    def storing(i):
        source = made_ref.at[i] if emit else (scaled_ref, back_ref, gate_grad_ref)[i].at[0]
        return pltpu.make_async_copy(source, made_hbm[i], out_sem.at[i])

    if not emit:
        for i in range(3):
            storing(i).start()
    else:
        if prior:
            for i in prior_in:
                arrivals[i]().wait()
        table_rows = x_ref.shape[1] - tokens_here
        tall = tokens_here + table_rows
        shape = (table_rows, MODEL_WIDTH)

        def scatter(b):
            row_index = lax.broadcasted_iota(jnp.int32, shape, 0)
            lane_group = lax.broadcasted_iota(jnp.int32, shape, 1) // tokens_here
            slots = pl.ds(pl.multiple_of(b * capacity, capacity), capacity)
            pick = pick_ref[b]

            def spread(n):
                at = slice(n * TD, (n + 1) * TD)
                made = jnp.concatenate([back_ref[0, slots, at], back_ref[1, slots, at]], axis=0)
                made_ref[b, :tokens_here, at] = dot(pick, made, 0, 0).astype(BF16)
                made = jnp.concatenate([scaled_ref[0, slots, at], scaled_ref[1, slots, at]], axis=0)
                made_ref[b, tall:, at] = dot(pick, made, 0, 0).astype(BF16)

            for n in range(MODEL_WIDTH // TD):
                spread(n)
            table = jnp.zeros(shape, F32)
            for e in range(2):
                table_row, group = place(ids[e])
                picked = pick[e * capacity : (e + 1) * capacity].astype(F32)
                line = jnp.sum(picked * gate_grad_ref[e, slots, :1], axis=0, keepdims=True)
                coarse = line.astype(BF16).astype(F32)
                here = lane_group == group
                for first, part in ((0, coarse), (per, line - coarse)):
                    wide = jnp.concatenate([part] * groups, axis=1)
                    table = table + jnp.where(here & (row_index == table_row + first), wide, 0.0)
            made_ref[b, tokens_here:tall, :] = table.astype(BF16)
            for turn in range(n_blocks):
                pl.when(b == turn)(lambda turn=turn: storing(turn).start())

        each(n_blocks, scatter)
    for turn in range(n_experts):
        for which in range(5):
            saving(which, turn).wait()
    for i in range(len(made_hbm)):
        storing(i).wait()


def run_experts(numbers, x_blocks, g_blocks, weights, experts, saved, first, total, capacity, prior=()):
    tokens_here = g_blocks[0][0].shape[0]
    block_rows = x_blocks[0][0].shape[0]
    width = weights[0].shape[2]
    n_blocks, n_here = len(x_blocks), len(experts)
    rows = n_blocks * capacity
    per = lax.axis_size("row") * tokens_here // MODEL_WIDTH
    emit = bool(prior) or n_here == 2
    sources = tuple(len(v) for v in x_blocks)
    plan = (sources, tuple(experts), first, bool(prior), saved is not None)
    hbm = pl.BlockSpec(memory_space=pltpu.HBM)
    if emit:
        made = [jax.ShapeDtypeStruct((tokens_here + block_rows, MODEL_WIDTH), BF16)] * n_blocks
    else:
        made = [jax.ShapeDtypeStruct((rows, MODEL_WIDTH), BF16)] * 2
        made.append(jax.ShapeDtypeStruct((rows, 128), F32))
    kept = [jax.ShapeDtypeStruct((2, total, MODEL_WIDTH), BF16)] * 2
    kept += [jax.ShapeDtypeStruct((2, total, width), BF16)] * 3
    operands = [w for v in (*x_blocks, *g_blocks) for w in v]
    for e in experts:
        operands += weights[3:] if e else weights[:3]
    operands += prior
    handed = 1 + len(operands)
    aliases = {}
    if saved is not None:
        operands += saved
        aliases = {handed + i: len(made) + i for i in range(5)}
    results = pl.pallas_call(
        functools.partial(experts_kernel, tokens_here, capacity, per, plan),
        out_shape=made + kept,
        in_specs=[pl.BlockSpec(memory_space=pltpu.SMEM)] + [hbm] * len(operands),
        out_specs=[hbm] * (len(made) + 5),
        scratch_shapes=[
            pltpu.VMEM((n_blocks, block_rows, MODEL_WIDTH), BF16),
            pltpu.VMEM((n_blocks, tokens_here, MODEL_WIDTH), BF16),
        ]
        + [pltpu.VMEM((n_here, *v.shape[1:]), BF16) for v in weights[:3]]
        + [pltpu.VMEM((n_blocks, *made[0].shape) if emit else (16, 128), BF16)]
        + [pltpu.VMEM((n_here, rows, MODEL_WIDTH), BF16)] * 2
        + [pltpu.VMEM((n_here, rows, width), BF16)] * 3
        + [
            pltpu.VMEM((n_blocks, (2 if emit else 1) * capacity, tokens_here), BF16),
            pltpu.VMEM((n_here, rows, MODEL_WIDTH), BF16),
            pltpu.VMEM((rows, width), F32),
            pltpu.VMEM((rows, width), F32),
            pltpu.VMEM((n_here, rows, 128), F32),
            pltpu.VMEM((2 if emit else 1, rows, MODEL_WIDTH), BF16),
            pltpu.VMEM((2 if emit else 1, rows, MODEL_WIDTH), BF16),
            pltpu.VMEM((2 if emit else 1, rows, 128), F32),
            pltpu.SemaphoreType.DMA((2 * n_blocks + 14,)),
            pltpu.SemaphoreType.DMA((len(made),)),
            pltpu.SemaphoreType.DMA((5, n_here)),
        ],
        input_output_aliases=aliases,
        compiler_params=pltpu.CompilerParams(vmem_limit_bytes=VMEM_ALL),
        cost_estimate=pl.CostEstimate(flops=1000, bytes_accessed=1000, transcendentals=0),
        name="experts",
    )(numbers, *operands)
    return list(results[: len(made)]), list(results[len(made) :])


def swap_halves(values):
    width = values.shape[1]
    half = HEAD_SIZE // 2
    lane = lax.broadcasted_iota(jnp.int32, values.shape, 1)
    return jnp.where(
        lane % HEAD_SIZE < half,
        pltpu.roll(values, width - half, 1),
        pltpu.roll(values, half, 1),
    )


def turn(values, cosine, sine_part):
    times = values.shape[1] // cosine.shape[1]
    wide = [jnp.concatenate([v] * times, axis=1) for v in (cosine, sine_part)]
    return values * wide[0] + swap_halves(values) * wide[1]


def rms_factor(values):
    return lax.rsqrt(jnp.mean(values * values, axis=-1, keepdims=True) + EPSILON)


def block_bias(seg_col_ref, seg_row_ref, first, rows, keys):
    queries = lax.broadcasted_iota(jnp.int32, (rows, keys), 0) + first
    at = lax.broadcasted_iota(jnp.int32, (rows, keys), 1)
    same = seg_col_ref[first : first + rows, :] == seg_row_ref[:, :keys]
    return jnp.where(same & (at <= queries), 0.0, -1e30)


def head_lanes(number):
    return slice(number * HEAD_SIZE, (number + 1) * HEAD_SIZE)


def attend_kernel(n_head, head_ref, *refs):
    token_refs = refs[:n_head]
    seg_col, seg_row, gain, w_q, w_k, w_v, w_o, cos_ref, sin_ref = refs[n_head : n_head + 9]
    normed_ref, q_ref, k_ref, v_ref, mixed_ref, lse_ref, own_ref, other_ref = refs[n_head + 9 : n_head + 17]
    part_ref, bias_ref = refs[n_head + 17 :]
    rows = token_refs[0].shape[0]
    head_at = head_ref[0]
    scale = HEAD_SIZE ** (-0.5)
    for k in range(n_head):
        x = token_refs[k][...].astype(F32)
        at = pl.ds(pl.multiple_of((head_at ^ k) * rows, rows), rows)
        normed_ref[at, :] = (x * rms_factor(x) * gain[...]).astype(BF16)
    normed = normed_ref[...]
    cosine, sine_part = cos_ref[...], sin_ref[...]
    q_ref[...] = (turn(dot(normed, w_q[...], 1, 0), cosine, sine_part).astype(BF16) * scale).astype(BF16)
    k_ref[...] = turn(dot(normed, w_k[...], 1, 0), cosine, sine_part).astype(BF16)
    v_ref[...] = dot(normed, w_v[...], 1, 0).astype(BF16)
    kv = k_ref.shape[1] // HEAD_SIZE
    per_group = q_ref.shape[1] // k_ref.shape[1]
    lane = lax.broadcasted_iota(jnp.int32, (rows, lse_ref.shape[1]), 1)
    wide_q, wide_k = 2 * per_group * HEAD_SIZE, 2 * HEAD_SIZE
    for i in range(n_head):
        first, keys = i * rows, (i + 1) * rows
        bias_ref[:, :keys] = block_bias(seg_col, seg_row, first, rows, keys)
        lse_ref[first:keys, :] = jnp.zeros((rows, lse_ref.shape[1]), F32)

        def pair(jj, first=first, keys=keys):
            q_at = pl.ds(pl.multiple_of(jj * wide_q, wide_q), wide_q)
            k_at = pl.ds(pl.multiple_of(jj * wide_k, wide_k), wide_k)
            query_all, key_all, value_all = q_ref[first:keys, q_at], k_ref[:keys, k_at], v_ref[:keys, k_at]
            made = []
            log_totals = lse_ref[first:keys, :]
            for h in range(2 * per_group):
                j = h // per_group
                key, value = key_all[:, head_lanes(j)], value_all[:, head_lanes(j)]
                scores = dot(query_all[:, head_lanes(h)], key, 1, 1) + bias_ref[:, :keys]
                highest = jnp.max(scores, axis=1, keepdims=True)
                exponent = jnp.exp(scores - highest)
                total = jnp.sum(exponent, axis=1, keepdims=True)
                log_totals = jnp.where(
                    lane == jj * (2 * per_group) + h, highest + jnp.log(total), log_totals
                )
                probs = (exponent * (1.0 / total)).astype(BF16)
                made.append(dot(probs, value, 1, 0).astype(BF16))
            mixed_ref[first:keys, q_at] = jnp.concatenate(made, axis=1)
            lse_ref[first:keys, :] = log_totals

        each(kv // 2, pair)
    part_ref[...] = dot(mixed_ref[...], w_o[...], 1, 0)
    own_ref[...] = part_ref[pl.ds(pl.multiple_of(head_at * rows, rows), rows), :]
    for k in range(1, n_head):
        at = pl.ds(pl.multiple_of((head_at ^ k) * rows, rows), rows)
        other_ref[k - 1] = part_ref[at, :].astype(BF16)


def attend_back_kernel(n_head, head_ref, *refs):
    token_refs, refs = refs[:n_head], refs[n_head:]
    grad_refs = refs[:n_head]
    seg_col, seg_row, w_q, w_k, w_v, w_o, cos_ref, sin_ref = refs[n_head : n_head + 8]
    q_ref, k_ref, v_ref, lse_ref = refs[n_head + 8 : n_head + 12]
    full_ref, proj_ref, own_ref, other_ref, gain_ref = refs[n_head + 12 : n_head + 17]
    gm_ref, dq_ref, dk_ref, dv_ref, part_ref, bias_ref = refs[n_head + 17 :]
    rows = grad_refs[0].shape[0]
    head_at = head_ref[0]
    scale = HEAD_SIZE ** (-0.5)
    for k in range(n_head):
        at = pl.ds(pl.multiple_of((head_at ^ k) * rows, rows), rows)
        full_ref[at, :] = grad_refs[k][...]
    gm_ref[...] = dot(full_ref[...], w_o[...], 1, 1).astype(BF16)
    cosine, sine_part = cos_ref[...], -sin_ref[...]
    kv = k_ref.shape[1] // HEAD_SIZE
    per_group = q_ref.shape[1] // k_ref.shape[1]
    dk_ref[...] = jnp.zeros(dk_ref.shape, F32)
    dv_ref[...] = jnp.zeros(dv_ref.shape, F32)
    lane = lax.broadcasted_iota(jnp.int32, (rows, lse_ref.shape[1]), 1)
    wide_q, wide_k = 2 * per_group * HEAD_SIZE, 2 * HEAD_SIZE
    for i in range(n_head):
        first, keys = i * rows, (i + 1) * rows
        bias_ref[:, :keys] = block_bias(seg_col, seg_row, first, rows, keys)

        def pair(jj, first=first, keys=keys):
            q_at = pl.ds(pl.multiple_of(jj * wide_q, wide_q), wide_q)
            k_at = pl.ds(pl.multiple_of(jj * wide_k, wide_k), wide_k)
            query_all, grad_all = q_ref[first:keys, q_at], gm_ref[first:keys, q_at]
            key_all, value_all = k_ref[:keys, k_at], v_ref[:keys, k_at]
            log_totals = lse_ref[first:keys, :]
            made, dk_all, dv_all = [], [], []
            for j in range(2):
                key, value = key_all[:, head_lanes(j)], value_all[:, head_lanes(j)]
                dk, dv = 0.0, 0.0
                for h in range(j * per_group, (j + 1) * per_group):
                    query, grad = query_all[:, head_lanes(h)], grad_all[:, head_lanes(h)]
                    mine = jnp.where(lane == jj * (2 * per_group) + h, log_totals, 0.0)
                    log_total = jnp.sum(mine, axis=1, keepdims=True)
                    probs = jnp.exp(dot(query, key, 1, 1) + bias_ref[:, :keys] - log_total)
                    grad_probs = dot(grad, value, 1, 1)
                    middle = jnp.sum(probs * grad_probs, axis=1, keepdims=True)
                    ds = (probs * (grad_probs - middle)).astype(BF16)
                    made.append(dot(ds, key, 1, 0) * scale)
                    dk = dk + dot(query, ds, 0, 0)
                    dv = dv + dot(grad, probs.astype(BF16), 0, 0)
                dk_all.append(dk)
                dv_all.append(dv)
            dq_ref[first:keys, q_at] = jnp.concatenate(made, axis=1)
            dk_ref[k_at, :keys] += jnp.concatenate(dk_all, axis=0)
            dv_ref[k_at, :keys] += jnp.concatenate(dv_all, axis=0)

        each(kv // 2, pair)
    width_q, width_k = q_ref.shape[1], k_ref.shape[1]
    proj_ref[:, :width_q] = turn(dq_ref[...], cosine, sine_part).astype(BF16)
    proj_ref[:, width_q : width_q + width_k] = turn(dk_ref[...].T, cosine, sine_part).astype(BF16)
    proj_ref[:, width_q + width_k :] = dv_ref[...].T.astype(BF16)
    part_ref[...] = (
        dot(proj_ref[:, :width_q], w_q[...], 1, 1)
        + dot(proj_ref[:, width_q : width_q + width_k], w_k[...], 1, 1)
        + dot(proj_ref[:, width_q + width_k :], w_v[...], 1, 1)
    )
    gain = jnp.zeros(gain_ref.shape, F32)
    for k in range(n_head):
        part = part_ref[pl.ds(pl.multiple_of((head_at ^ k) * rows, rows), rows), :]
        x = token_refs[k][...].astype(F32)
        gain = gain + jnp.sum(part * (x * rms_factor(x)), axis=0, keepdims=True)
        if k:
            other_ref[k - 1] = part.astype(BF16)
        else:
            own_ref[...] = part
    gain_ref[...] = gain


def weight_grads(share, core, normed_ref, proj_ref, full_ref, mixed_ref, own_ref, other_ref, all_ref):
    width = proj_ref.shape[1]
    all_ref[:, :width] = dot(normed_ref[...], proj_ref[...], 0, 0)
    all_ref[:, width:] = dot(full_ref[...], mixed_ref[...], 0, 0)
    for m in range(own_ref.shape[0] // share):
        at = slice(m * share, (m + 1) * share)
        own = pl.ds(pl.multiple_of((2 * m + core) * share, share), share)
        other = pl.ds(pl.multiple_of((2 * m + 1 - core) * share, share), share)
        own_ref[at, :] = all_ref[own, :]
        other_ref[at, :] = all_ref[other, :].astype(BF16)


def attend_back_all_kernel(n_head, share, head_ref, *refs):
    n_in = 2 * n_head + 12
    normed_ref, mixed_ref = refs[n_in : n_in + 2]
    own_ref, other_ref, gain_ref, weights_own_ref, weights_other_ref = refs[n_in + 2 : n_in + 7]
    full_ref, proj_ref, *work, all_ref = refs[n_in + 7 :]
    attend_back_kernel(
        n_head, head_ref, *refs[:n_in], full_ref, proj_ref, own_ref, other_ref, gain_ref, *work
    )
    weight_grads(
        share, head_ref[1], normed_ref, proj_ref, full_ref, mixed_ref,
        weights_own_ref, weights_other_ref, all_ref,
    )


def expert_grads_kernel(n_head, axis, heads_first, head_ref, lhs_ref, rhs_ref, *refs):
    head_at = head_ref[0]
    own_ref, rest_ref, away_ref, all_ref = refs
    size = own_ref.shape[axis]

    def part(k):
        at = pl.ds(pl.multiple_of((head_at ^ k) * size, size), size)
        return all_ref[at, :] if axis == 0 else all_ref[:, at]

    def first():
        own_ref[...] = part(0)
        for k in range(1, n_head):
            if heads_first:
                away_ref[k - 1, 0] = part(k).astype(BF16)
            else:
                rest_ref[k - 1] = part(k)

    def second():
        for k in range(n_head):
            if not heads_first:
                away_ref[k] = part(k).astype(BF16)
            elif k:
                away_ref[k - 1, 1] = part(k).astype(BF16)
            else:
                rest_ref[0] = part(0)

    def turn(e):
        all_ref[...] = dot(lhs_ref[e], rhs_ref[e], 0, 0)
        pl.when(e == 0)(first)
        pl.when(e == 1)(second)

    each(2, turn)


def final_kernel(n_head, tokens_ref, grad_hidden_ref, gain, own_ref, *refs):
    total = own_ref[...]
    for part in refs[: n_head - 1]:
        total = total + part[...].astype(F32)
    x = tokens_ref[...].astype(F32)
    factor = rms_factor(x)
    weighted = total * gain[...]
    middle = jnp.mean(weighted * x, axis=-1, keepdims=True)
    refs[-1][...] = grad_hidden_ref[...] + factor * (weighted - x * factor * factor * middle)


def hidden_kernel(n_head, tokens_ref, own_ref, *refs):
    arrived = refs[: n_head - 1]
    gain, router_t, slots_ref, chosen_ref = refs[n_head - 1 : n_head + 3]
    block_ref, hidden_ref, gates_ref = refs[n_head + 3 :]
    rows = tokens_ref.shape[0]
    attention = own_ref[...]
    for part in arrived:
        attention = attention + part[...].astype(F32)
    hidden = tokens_ref[...].astype(F32) + attention
    hidden_ref[...] = hidden
    normed = (hidden * rms_factor(hidden) * gain[...]).astype(BF16)
    block_ref[:rows, :] = normed
    chosen = chosen_ref[...] > 0.0
    logits = jnp.where(chosen, dot(router_t[...], normed, 1, 1), -1e30)
    gates = jnp.where(chosen, jnp.exp(logits - jnp.max(logits, axis=0, keepdims=True)), 0.0)
    gates = gates / jnp.sum(gates, axis=0, keepdims=True)
    gates_ref[...] = gates
    coarse = gates.astype(BF16).astype(F32)
    groups = MODEL_WIDTH // rows
    per = gates.shape[0] // groups
    lines = [
        jnp.concatenate([v[q * per : (q + 1) * per] for q in range(groups)], axis=1)
        for v in (coarse, gates - coarse, slots_ref[...])
    ]
    spare = block_ref.shape[0] - rows - 3 * per
    if spare:
        lines.append(jnp.zeros((spare, MODEL_WIDTH), F32))
    block_ref[rows:, :] = jnp.concatenate(lines, axis=0).astype(BF16)


def grad_hidden_kernel(n_parts, *refs):
    parts = refs[:n_parts]
    hidden_ref, gain, router_t, gates_ref, block_ref, cotangent_ref = refs[n_parts : n_parts + 6]
    grad_ref, low_ref, small_ref = refs[n_parts + 6 :]
    rows = hidden_ref.shape[0]
    tall = block_ref.shape[0]
    total = parts[0][:tall, :].astype(F32)
    for part in parts[1:]:
        total = total + part[:tall, :].astype(F32)
    gates = gates_ref[...]
    groups = MODEL_WIDTH // rows
    per = gates.shape[0] // groups
    lines = total[rows : rows + per] + total[rows + per : rows + 2 * per]
    grad_gates = jnp.concatenate(
        [lines[:, q * rows : (q + 1) * rows] for q in range(groups)], axis=0
    )
    grad_logits = gates * (grad_gates - jnp.sum(gates * grad_gates, axis=0, keepdims=True))
    coarse = grad_logits.astype(BF16)
    fine = (grad_logits - coarse.astype(F32)).astype(BF16)
    normed = block_ref[:rows, :]
    n_experts = gates.shape[0]
    small_ref[:n_experts, :] = dot(coarse, normed, 1, 0) + dot(fine, normed, 1, 0)
    upstream = total[:rows] + dot(coarse, router_t[...], 0, 0) + dot(fine, router_t[...], 0, 0)
    hidden = hidden_ref[...]
    factor = rms_factor(hidden)
    weighted = upstream * gain[...]
    middle = jnp.mean(weighted * hidden, axis=-1, keepdims=True)
    grad = cotangent_ref[...].astype(F32) + factor * (weighted - hidden * factor * factor * middle)
    grad_ref[...] = grad
    low_ref[...] = grad.astype(BF16)
    small_ref[n_experts:, :] = jnp.sum(upstream * hidden * factor, axis=0, keepdims=True)


def call(kernel, name, operands, out_shape, scratch_shapes=(), scalars=0, room=VMEM_BYTES):
    vmem = pl.BlockSpec(memory_space=pltpu.VMEM)
    smem = pl.BlockSpec(memory_space=pltpu.SMEM)
    made = pl.pallas_call(
        kernel,
        out_shape=out_shape,
        in_specs=[smem] * scalars + [vmem] * (len(operands) - scalars),
        out_specs=[vmem] * len(out_shape),
        scratch_shapes=list(scratch_shapes),
        compiler_params=pltpu.CompilerParams(vmem_limit_bytes=room),
        cost_estimate=pl.CostEstimate(flops=1000, bytes_accessed=1000, transcendentals=0),
        name=name,
    )(*operands)
    return list(made)


def local(
    tokens,
    segments,
    routes,
    norm_gain,
    w_query,
    key_weight,
    value_weight,
    w_output,
    moe_gain,
    w_router,
    w_gate,
    w_up,
    w_down,
    cotangent,
):
    local_rows = tokens.shape[0]
    length = segments.shape[0]
    n_experts = w_router.shape[1]
    capacity = local_rows * TOPK * 5 // (4 * n_experts)
    width_query = w_query.shape[1]
    width_key = key_weight.shape[1]
    n_row = lax.axis_size("row")
    n_head = lax.axis_size("head")
    n_outer = n_row // 4
    row_at = lax.axis_index("row")
    head_at = lax.axis_index("head")
    at_end = (row_at // 4 % 3 == 0).astype(jnp.int32)
    numbers = jnp.stack([row_at, head_at & 1, at_end]).astype(jnp.int32)

    routes_t = routes.T
    expert_index = jnp.arange(n_experts, dtype=jnp.int32)[:, None]
    chosen = jnp.any(routes_t[:, None, :] == expert_index[None], axis=0)
    t_index = jnp.arange(local_rows, dtype=jnp.int32)
    before = (t_index[:, None] < t_index[None, :]).astype(BF16)
    rank = dot(chosen.astype(BF16), before, 1, 0)
    slots = jnp.where(chosen & (rank < capacity), rank, -1.0)
    chosen = chosen.astype(F32)
    router_t = w_router.T
    head_number = head_at.astype(jnp.int32).reshape(1)

    line = n_outer == 4
    inner = [(i, i ^ 12) for i in range(4, 12)]
    outward = [(i, i ^ 4) for i in range(4, 12)]
    ends = [*range(4), *range(12, 16)]
    ends_in = [(i, i ^ 8) for i in ends]
    ends_over = [(i, i ^ 12) for i in ends]
    inner_out = [(i, i ^ 8) for i in range(4, 12)]

    def send(value, pairs):
        return lax.ppermute(value, "row", pairs)

    def share_of(weight):
        size = weight.shape[1] // 2
        return lax.dynamic_slice_in_dim(weight[0], (head_at & 1) * size, size, 0)

    def head_all(values):
        return [head_swap(values[k - 1], k) for k in range(1, n_head)]

    def low(value):
        return value.astype(BF16)

    def shape(rows, columns, dtype=BF16):
        return jax.ShapeDtypeStruct((rows, columns), dtype)

    seg_col, seg_row = segments[:, None], segments[None, :]
    gain_row, moe_gain_row = norm_gain[None], moe_gain[None]

    tokens_other = head_all([tokens] * (n_head - 1))
    frequency = ROPE_BASE ** (-2.0 * jnp.arange(HEAD_SIZE // 2, dtype=F32) / HEAD_SIZE)
    angles = jnp.arange(length, dtype=F32)[:, None] * frequency[None, :]
    cosine, sine_part = jnp.cos(angles), jnp.sin(angles)
    cosine = jnp.concatenate([cosine] * 4, axis=1)
    sine_part = jnp.concatenate([-sine_part, sine_part] * 2, axis=1)
    gate_share, down_share = share_of(w_gate), share_of(w_down)
    width = gate_share.shape[1]
    pieces = [down_share[:, k : k + width] for k in range(0, down_share.shape[1], width)]
    gate_here = row_swap(gate_share, 2)
    down_here = row_swap(jnp.concatenate(pieces, axis=0), 2)
    if line:
        g_far = [row_swap(cotangent, 4), send(cotangent, inner)]
    else:
        g_far = [row_swap(cotangent, 4 * o) for o in range(1, n_outer)]
    tokens_other, cosine, sine_part, seg_col, slots, chosen = tie(
        tokens_other, cosine, sine_part, seg_col, slots, chosen
    )
    g_far, w_up_later, _ = tie(g_far, w_up, seg_col)

    g_slabs = [cotangent, *g_far]
    if line:
        g_far += [send(g_far[1], outward), send(g_far[0], inner)]
    head_parts = [
        shape(local_rows, MODEL_WIDTH, F32),
        jax.ShapeDtypeStruct((n_head - 1, local_rows, MODEL_WIDTH), BF16),
    ]
    normed_full, queries, keys, values, mixed_heads, log_totals, part_own, part_other = call(
        functools.partial(attend_kernel, n_head),
        "attend",
        [head_number, tokens, *tokens_other, seg_col, seg_row, gain_row]
        + [w_query, key_weight, value_weight, w_output, cosine, sine_part],
        [shape(length, MODEL_WIDTH), shape(length, width_query)]
        + [shape(length, width_key)] * 2
        + [shape(length, width_query), shape(length, 128, F32), *head_parts],
        [pltpu.VMEM((length, MODEL_WIDTH), F32), pltpu.VMEM((local_rows, length), F32)],
        scalars=1,
        room=VMEM_ALL,
    )
    part_other, part_own, gate_here, down_here, g_far, w_up_later = tie(
        part_other, part_own, gate_here, down_here, g_far, w_up_later
    )

    arrived = head_all(part_other)
    up_here = row_swap(w_up_later, 2)
    g_last = send(g_far[3], outward) if line else cotangent
    arrived, part_own, g_last = tie(arrived, part_own, g_last)
    table_rows = -(-3 * n_experts * local_rows // MODEL_WIDTH // 16) * 16
    x_block, hidden, gates = call(
        functools.partial(hidden_kernel, n_head),
        "hidden",
        [tokens, part_own, *arrived, moe_gain_row, router_t, slots, chosen],
        [
            shape(local_rows + table_rows, MODEL_WIDTH),
            shape(local_rows, MODEL_WIDTH, F32),
            shape(n_experts, local_rows, F32),
        ],
    )
    tall = x_block.shape[0]
    saved = None
    made = []

    def cores(values):
        return [row_swap(v, 1) for v in values]

    def pass_on(chunk):
        made[chunk][1] = row_swap(made[chunk][1], 1)

    def near(which, chunk):
        own, other = (v[:tall] if which else v[tall:] for v in made[chunk])
        return own.astype(F32) + other.astype(F32)

    def experts(x_blocks, g_blocks, which, prior=()):
        nonlocal saved
        first = 2 * len(made) * capacity
        results, saved = run_experts(
            numbers, x_blocks, g_blocks, weights, which, saved, first, total_rows, capacity, prior
        )
        if which == (0,):
            return results
        made.extend(results[i : i + 2] for i in range(0, len(results), 2))

    total_rows = 2 * n_outer * capacity
    gate_there = head_swap(gate_here, 1)
    x_core = row_swap(x_block, 1)
    if line:
        x_far = [row_swap(x_block, 4), send(x_block, inner)]
    else:
        x_far = [row_swap(x_block, 4 * o) for o in range(1, n_outer)]
    x_block, x_core, x_far, up_here, gate_there, down_later, g_slabs, g_far, g_last, cotangent = tie(
        x_block, x_core, x_far, up_here, gate_there, down_here, g_slabs, g_far, g_last, cotangent
    )
    down_there = head_swap(down_later, 1)
    weights = [w_gate, w_up, w_down, gate_here, gate_there, down_here, down_there, up_here]

    if line:
        x_near, x_mid = x_far
        x_near_core = row_swap(x_near, 1)
        g_cores = cores(g_slabs[:2])
        x_near, x_mid, x_near_core, g_cores, g_far = tie(x_near, x_mid, x_near_core, g_cores, g_far)
        x_out, x_deep = send(x_mid, outward), send(x_near, inner)
        x_pairs = [[x_block], [x_core], [x_near], [x_near_core]]
        g_pairs = [[cotangent], [g_cores[0]], [g_slabs[1]], [g_cores[1]]]
        prior = experts(x_pairs, g_pairs, (0,))
        x_out, x_deep, prior, saved, down_there, g_far, x_mid, g_mid, g_last = tie(
            x_out, x_deep, prior, saved, down_there, g_far, x_mid, g_slabs[2], g_last
        )
        weights[6] = down_there
        x_last = send(x_deep, outward)
        x_mid_core, g_mid_core, g_out_core = cores([x_mid, g_mid, g_far[2]])
        experts(x_pairs, g_pairs, (1,), prior)
        x_last, x_mid_core, g_mid_core, g_out_core, made[0], made[1], saved, x_out = tie(
            x_last, x_mid_core, g_mid_core, g_out_core, made[0], made[1], saved, x_out
        )
        x_out_core = row_swap(x_out, 1)
        x_out_core, x_last, x_deep, g_deep, g_last, made[0] = tie(
            x_out_core, x_last, x_deep, g_far[3], g_last, made[0]
        )
        pass_on(1)
        x_deep_core, x_last_core, g_deep_core, g_last_core = cores([x_deep, x_last, g_deep, g_last])
        g_two = [[g_mid, g_far[2]], [g_mid_core, g_out_core]]
        experts([[x_mid, x_out], [x_mid_core, x_out_core]], g_two, (0, 1))
        x_deep_core, x_last_core, g_deep_core, g_last_core, made[0], made[1], made[2], saved = tie(
            x_deep_core, x_last_core, g_deep_core, g_last_core, made[0], made[1], made[2], saved
        )
        pass_on(2)
        made[0], made[1], made[2], x_deep, x_last = tie(made[0], made[1], made[2], x_deep, x_last)
        g_three = [[g_deep, g_last], [g_deep_core, g_last_core]]
        two, sum_one = low(near(1, 2)), low(near(1, 1))
        first_sums = [send(two, ends_in), send(two, inner), row_swap(sum_one, 4)]
        x_deep, x_last, _, _ = tie(x_deep, x_last, two, sum_one)
        experts([[x_deep, x_last], [x_deep_core, x_last_core]], g_three, (0, 1))
    else:
        for o, x in enumerate([x_block, *x_far]):
            experts([[x], [row_swap(x, 1)]], [[g_slabs[o]], [row_swap(g_slabs[o], 1)]], (0, 1))
        for o in range(n_outer):
            pass_on(o)
        one = [row_swap(low(near(1, o)), 4 * o) for o in range(1, n_outer)]

    rows_in, gprod, inner_act, dgate, dup = saved

    def expert_grads(lhs, rhs, axis, heads_first):
        sizes = [lhs.shape[2], rhs.shape[2]]
        part = list(sizes)
        part[axis] //= n_head
        rest = (1, *part) if heads_first else (n_head - 1, *part)
        away = (n_head - 1, 2, *part) if heads_first else (n_head, *part)
        return call(
            functools.partial(expert_grads_kernel, n_head, axis, heads_first),
            "expert_grads",
            [head_number, lhs, rhs],
            [
                jax.ShapeDtypeStruct(tuple(part), F32),
                jax.ShapeDtypeStruct(rest, F32),
                jax.ShapeDtypeStruct(away, BF16),
            ],
            [pltpu.VMEM(tuple(sizes), F32)],
            scalars=1,
        )

    if line:
        made[0], made[3], inner_act, gprod, rows_in, dgate, dup = tie(
            made[0], made[3], inner_act, gprod, rows_in, dgate, dup
        )
    up_parts = expert_grads(rows_in, dup, 0, False)
    down_parts = expert_grads(inner_act, gprod, 1, True)
    up_away, down_away = up_parts[2], down_parts[2]
    if line:
        first_sums, made[0], made[3], up_away, down_away, rows_in, dgate = tie(
            first_sums, made[0], made[3], up_away, down_away, rows_in, dgate
        )
        pass_on(0)
        pass_on(3)
        made[0], made[3], first_sums, up_away, down_away, rows_in, dgate = tie(
            made[0], made[3], first_sums, up_away, down_away, rows_in, dgate
        )
        three = low(near(1, 3))
        last_sums = [send(three, ends_over), send(three, inner_out)]
    up_away = row_swap(up_away, 2)
    down_away = head_all(down_away)
    gate_parts = expert_grads(rows_in, dgate, 0, False)
    gate_away = gate_parts[2]
    if line:
        total = near(1, 0) + sum(v.astype(F32) for v in first_sums)
        made_now, _ = tie(made, three)
        made = list(made_now)
        out_one, out_two, out_three = (low(near(0, o)) for o in range(1, 4))
        one = [total, *last_sums]
    else:
        one = [near(1, 0), *one]
        out_one = out_two = out_three = one[0]
    one, up_away, down_away, gate_away, made_now, out_one, out_two, out_three = tie(
        one, up_away, down_away, gate_away, made, out_one, out_two, out_three
    )
    made = list(made_now)
    grad_sum = one
    grad_hidden, grad_attention, early = call(
        functools.partial(grad_hidden_kernel, len(grad_sum)),
        "grad_hidden",
        [*grad_sum, hidden, moe_gain_row, router_t, gates, x_block, cotangent],
        [
            shape(local_rows, MODEL_WIDTH, F32),
            shape(local_rows, MODEL_WIDTH),
            shape(n_experts + 1, MODEL_WIDTH, F32),
        ],
    )
    made_now, up_away, down_away, gate_away, grad_attention = tie(
        made, up_away, down_away, gate_away, grad_attention
    )
    made = list(made_now)
    grad_arrived = head_all([grad_attention] * (n_head - 1))
    gate_away = row_swap(gate_away, 2)
    out_first = [send(out_two, ends_in)] if line else [out_two]
    up_rest = [low(v + w.astype(F32)) for v, w in zip(up_parts[1], up_away[1:])]
    down_rest = low(down_parts[1][0] + sum(v[1].astype(F32) for v in down_away))
    grad_arrived, up_rest, down_rest, made_now, out_two, out_three, out_first = tie(
        grad_arrived, up_rest, down_rest, made, out_two, out_three, out_first
    )
    made = list(made_now)
    up_last = head_all(up_rest)
    if line:
        out_first += [send(out_three, ends_over), send(out_three, inner_out)]
    else:
        out_first = grad_attention
    share = MODEL_WIDTH // n_row
    width_all = width_query + 2 * width_key
    grad_own, grad_other, gain_part, weights_own, weights_other = call(
        functools.partial(attend_back_all_kernel, n_head, share),
        "attend_back",
        [jnp.stack([head_at, row_at % 2]).astype(jnp.int32), tokens, *tokens_other, grad_attention]
        + [*grad_arrived, seg_col, seg_row, w_query, key_weight, value_weight, w_output]
        + [cosine, sine_part, queries, keys, values, log_totals, normed_full, mixed_heads],
        [
            *head_parts,
            shape(1, MODEL_WIDTH, F32),
            shape(MODEL_WIDTH // 2, width_all + width_query, F32),
            shape(MODEL_WIDTH // 2, width_all + width_query),
        ],
        [
            pltpu.VMEM((length, MODEL_WIDTH), BF16),
            pltpu.VMEM((length, width_all), BF16),
            pltpu.VMEM((length, width_query), BF16),
            pltpu.VMEM((length, width_query), F32),
            pltpu.VMEM((width_key, length), F32),
            pltpu.VMEM((width_key, length), F32),
            pltpu.VMEM((length, MODEL_WIDTH), F32),
            pltpu.VMEM((local_rows, length), F32),
            pltpu.VMEM((MODEL_WIDTH, width_all + width_query), F32),
        ],
        scalars=1,
        room=VMEM_ALL,
    )
    grad_other, gain_part, weights_own, weights_other, up_last, gate_away, down_rest, *outs = tie(
        grad_other, gain_part, weights_own, weights_other, up_last, gate_away, down_rest,
        out_one, out_two,
    )
    out_one, out_two = outs
    small = jnp.concatenate([early, gain_part], axis=0)
    small, weights_own, weights_other, made_now, out_first, out_one, out_two = tie(
        small, weights_own, weights_other, made, out_first, out_one, out_two
    )
    made = list(made_now)
    small_core = row_swap(small, 1)
    weights_core = row_swap(weights_other, 1)
    small, small_core, weights_own, weights_core = tie(small, small_core, weights_own, weights_core)
    small = small + small_core
    small_far = row_swap(small, 2)
    if line:
        out_first = [*out_first, send(out_two, inner), row_swap(out_one, 4)]
    else:
        out_first = small
    value = (weights_own + weights_core.astype(F32)).reshape(n_outer, 2, share, -1)
    bit = (row_at // 2) % 2
    other = low(lax.dynamic_index_in_dim(value, 1 - bit, 1, keepdims=False))
    value = lax.dynamic_index_in_dim(value, bit, 1, keepdims=False)
    small, other, value, grad_other, down_rest, gate_away, made_now, out_two = tie(
        small + small_far, other, value, grad_other, down_rest, gate_away, made, out_two
    )
    made = list(made_now)
    other_arrived = row_swap(other, 2)
    offset = 4
    while offset < n_row:
        small = small + row_swap(small, offset)
        offset *= 2
    offset = 1
    while offset < n_head:
        small = small + head_swap(small, offset)
        offset *= 2
    grad_arrived = head_all(grad_other)
    gate_rest = [low(v + w.astype(F32)) for v, w in zip(gate_parts[1], gate_away[1:])]
    mixed_out = hidden + near(0, 0)
    if line:
        mixed_out = mixed_out + sum(v.astype(F32) for v in out_first)
        last = []
    else:
        last = [row_swap(low(near(0, o)), 4 * o) for o in range(1, n_outer)]
    grad_arrived, value, other_arrived, small, gate_rest, last, mixed_out, down_rest = tie(
        grad_arrived, value, other_arrived, small, gate_rest, last, mixed_out, down_rest
    )
    gate_last = head_all(gate_rest)
    value = value + other_arrived.astype(F32)
    at = row_at // 4
    weights_sum = lax.dynamic_index_in_dim(value, at, 0, keepdims=False)
    weights_parts = [
        row_swap(low(lax.dynamic_index_in_dim(value, at ^ o, 0, keepdims=False)), 4 * o)
        for o in range(1, n_outer)
    ]
    down_last = row_swap(down_rest, 2)
    (grad_tokens,) = call(
        functools.partial(final_kernel, n_head),
        "final",
        [tokens, grad_hidden, gain_row, grad_own, *grad_arrived],
        [shape(local_rows, MODEL_WIDTH, F32)],
    )
    for part in last:
        mixed_out = mixed_out + part.astype(F32)
    mixed_out = mixed_out.astype(BF16)

    def add(own, *parts):
        for part in parts:
            own = own + part.astype(F32)
        return own

    down_sum = add(down_parts[0], *(v[0] for v in down_away), down_last)
    up_sum = add(up_parts[0], up_away[0], *up_last)
    gate_sum = add(gate_parts[0], gate_away[0], *gate_last)
    down_sum, up_sum, gate_sum, weights_parts = tie(down_sum, up_sum, gate_sum, weights_parts)
    weights_sum = add(weights_sum, *weights_parts)
    return (
        mixed_out,
        grad_tokens,
        small[n_experts + 1],
        weights_sum[:, :width_query],
        weights_sum[:, width_query : width_query + width_key],
        weights_sum[:, width_query + width_key : width_all],
        weights_sum[:, width_all:].T,
        small[n_experts],
        small[:n_experts].T,
        gate_sum[None],
        up_sum[None],
        down_sum[None],
    )


def solution(mesh):
    in_specs = (
        P(("row", "head"), None),
        P("row"),
        P(("row", "head"), None),
        P(),
        P(None, "head"),
        P(None, "head"),
        P(None, "head"),
        P("head", None),
        P(),
        P(),
        P("row", None, None),
        P("row", None, None),
        P("row", None, None),
        P(("row", "head"), None),
    )
    out_specs = (
        P(("row", "head"), None),
        P(("row", "head"), None),
        P(),
        P("row", "head"),
        P("row", "head"),
        P("row", "head"),
        P("head", "row"),
        P(),
        P(),
        P("row", "head", None),
        P("row", "head", None),
        P("row", None, "head"),
    )
    return jax.shard_map(local, mesh=mesh, in_specs=in_specs, out_specs=out_specs, check_vma=False)
```

```python
import functools

import jax
import jax.numpy as jnp
from jax import lax
from jax.experimental import pallas as pl
from jax.experimental.pallas import tpu as pltpu
from jax.sharding import PartitionSpec as P

MODEL_WIDTH = 1024
HEAD_SIZE = 64
VMEM_BYTES = 36 * 1024 * 1024
VMEM_ALL = 63 * 1024 * 1024
TOPK = 8

EPSILON = 1e-06
ROPE_BASE = 10000.0
F32 = jnp.float32
BF16 = jnp.bfloat16


def row_swap(value, offset):
    size = lax.axis_size("row")
    return lax.ppermute(value, "row", [(i, i ^ offset) for i in range(size)])


def head_swap(value, offset):
    size = lax.axis_size("head")
    return lax.ppermute(value, "head", [(i, i ^ offset) for i in range(size)])


def dot(a, b, ca, cb, **kw):
    return lax.dot_general(a, b, (((ca,), (cb,)), ((), ())), preferred_element_type=F32, **kw)


def tie(*values):
    return lax.optimization_barrier(values)


def each(count, body):
    lax.fori_loop(0, count, lambda i, carry: (body(i), carry)[1], 0)


def experts_kernel(tokens_here, capacity, per, plan, number_ref, *refs):
    sources, experts, rows_before, prior, handed_on = plan
    n_blocks, n_experts = len(sources), len(experts)
    emit = prior or n_experts == 2
    refs = list(refs)

    def pop(number):
        taken, refs[:] = refs[:number], refs[number:]
        return taken

    x_hbm = [pop(k) for k in sources]
    g_hbm = [pop(k) for k in sources]
    w_hbm = {e: pop(5 if e else 3) for e in experts}
    prior_hbm = pop(3) if prior else []
    if handed_on:
        pop(5)
    made_hbm = pop(n_blocks) if emit else pop(3)
    saved_hbm = pop(5)
    x_ref, g_ref, gate_ref, up_ref, down_ref, made_ref = pop(6)
    rows_ref, gprod_ref, inner_ref, dgate_ref, dup_ref = pop(5)
    pick_ref, g_rows_ref, gate_pre_ref, up_pre_ref, slot_ref = pop(5)
    scaled_ref, back_ref, gate_grad_ref, in_sem, out_sem, saved_sem = pop(6)
    ids = (number_ref[0], number_ref[0] ^ 2)
    bit, flag = number_ref[1], number_ref[2]
    arrivals = []

    def load(source, target):
        i = len(arrivals)

        def copy(k=0):
            return pltpu.make_async_copy(source[k](), target(), in_sem.at[i])

        if len(source) == 2:
            for k in range(2):
                pl.when(flag == k)(copy(k).start)
        else:
            copy().start()
        arrivals.append(copy)
        return i

    def whole(ref, *index):
        return lambda: ref.at[index] if index else ref

    def arrive(at, numbers):
        for turn, mine in enumerate(numbers):

            def wait(mine=mine):
                for i in mine:
                    arrivals[i]().wait()

            pl.when(at == turn)(wait)

    width = gate_ref.shape[2]
    depth = down_ref.shape[1] // 2
    rows_half = gate_ref.shape[1] // 2

    def halves(gate, down, index, i):
        def first():
            return gate_ref.at[i, pl.ds(pl.multiple_of(index * rows_half, rows_half), rows_half)]

        def second(k):
            at = pl.ds(pl.multiple_of(index * depth, depth), depth)
            return lambda: down_ref.at[i, at, k * width : (k + 1) * width]

        def part(k):
            return lambda: down.at[k * depth : (k + 1) * depth]

        return (whole(gate), first), [(part(k), second(k)) for k in range(down_ref.shape[2] // width)]

    tokens_in = [
        [
            load([whole(h) for h in x_hbm[b]], whole(x_ref, b)),
            load([whole(h) for h in g_hbm[b]], whole(g_ref, b)),
        ]
        for b in range(n_blocks)
    ]
    gate_in, up_in, down_in = [], [], []
    for i, e in enumerate(experts):
        if e == 0:
            gate_in.append([load([whole(w_hbm[e][0], 0)], whole(gate_ref, i))])
            up_in.append([load([whole(w_hbm[e][1], 0)], whole(up_ref, i))])
            down_in.append([load([whole(w_hbm[e][2], 0)], whole(down_ref, i))])
        else:
            gate_near, gate_far, down_near, down_far, up_h = w_hbm[e]
            gate_here, down_here = halves(gate_near, down_near, bit, i)
            gate_there, down_there = halves(gate_far, down_far, 1 - bit, i)
            gate_in.append([load([a], b) for a, b in (gate_here, gate_there)])
            up_in.append([load([whole(up_h, 0)], whole(up_ref, i))])
            down_in.append([load([a], b) for a, b in down_here + down_there])
    if prior:
        prior_in = [
            load([whole(prior_hbm[0])], whole(scaled_ref, 0)),
            load([whole(prior_hbm[1])], whole(back_ref, 0)),
            load([whole(prior_hbm[2])], whole(gate_grad_ref, 0)),
        ]

    def saving(which, turn):
        buffer = (rows_ref, gprod_ref, inner_ref, dgate_ref, dup_ref)[which]
        return pltpu.make_async_copy(
            buffer.at[turn],
            saved_hbm[which].at[experts[turn], pl.ds(rows_before, n_blocks * capacity)],
            saved_sem.at[which, turn],
        )

    def save(which, i):
        for turn in range(n_experts):
            pl.when(i == turn)(lambda turn=turn: saving(which, turn).start())

    groups = MODEL_WIDTH // tokens_here

    def place(number):
        return number % per, number // per

    def take(table, first, number):
        table_row, group = place(number)
        index = lax.broadcasted_iota(jnp.int32, table.shape, 0)
        line = jnp.sum(jnp.where(index == table_row + first, table, 0.0), axis=0, keepdims=True)
        picked = jnp.zeros((1, tokens_here), F32)
        for q in range(groups):
            part = line[:, q * tokens_here : (q + 1) * tokens_here]
            picked = picked + jnp.where(group == q, part, 0.0)
        return picked

    held = (0, 1) if emit else experts
    first_held = held.index(experts[0]) * capacity
    shift = 1 if prior else 0

    def gather(b):
        arrive(b, tokens_in)
        table = x_ref[b, tokens_here:, :].astype(F32)
        slot_index = lax.broadcasted_iota(jnp.int32, (capacity, tokens_here), 0).astype(F32)
        at = pl.ds(pl.multiple_of(b * capacity, capacity), capacity)
        for h, e in enumerate(held):
            pick = (slot_index == take(table, 2 * per, ids[e])).astype(F32)
            if e in experts:
                gate = take(table, 0, ids[e]) + take(table, per, ids[e])
                slot = jnp.sum(pick * gate, axis=1, keepdims=True)
                slot_ref[experts.index(e), at, :] = jnp.broadcast_to(slot, (capacity, 128))
            pick_ref[b, h * capacity : (h + 1) * capacity, :] = pick.astype(BF16)
        pick = pick_ref[b, first_held : first_held + n_experts * capacity, :]
        rows = dot(pick, x_ref[b, :tokens_here, :], 1, 0).astype(BF16)
        g_rows = dot(pick, g_ref[b], 1, 0).astype(BF16)
        for i in range(n_experts):
            rows_ref[i, at, :] = rows[i * capacity : (i + 1) * capacity]
            g_rows_ref[i, at, :] = g_rows[i * capacity : (i + 1) * capacity]

    each(n_blocks, gather)
    TF, TD = 512, 1024

    def tile_at(n):
        return slice(n * tile, (n + 1) * tile)

    def expert(i):
        save(0, i)
        arrive(i, gate_in)
        arrive(i, up_in)

        def forward(n):
            at = slice(n * TF, (n + 1) * TF)
            gate_pre = dot(rows_ref[i], gate_ref[i, :, at], 1, 0)
            up_pre = dot(rows_ref[i], up_ref[i, :, at], 1, 0)
            gate_pre_ref[:, at] = gate_pre
            up_pre_ref[:, at] = up_pre
            inner_ref[i, :, at] = (gate_pre * jax.nn.sigmoid(gate_pre) * up_pre).astype(BF16)

        for n in range(width // TF):
            forward(n)
        save(2, i)
        arrive(i, down_in)
        gate_grad_ref[i + shift] = jnp.zeros(gate_grad_ref.shape[1:], F32)

        def produce(n):
            at = slice(n * TD, (n + 1) * TD)
            slot = slot_ref[i, :, :1]
            produced = dot(inner_ref[i], down_ref[i, :, at], 1, 0).astype(BF16).astype(F32)
            g_rows = g_rows_ref[i, :, at].astype(F32)
            gate_grad_ref[i + shift] += jnp.sum(g_rows * produced, axis=1, keepdims=True)
            scaled_ref[i + shift, :, at] = (slot * produced).astype(BF16)
            gprod_ref[i, :, at] = (slot * g_rows).astype(BF16)

        for n in range(MODEL_WIDTH // TD):
            produce(n)
        save(1, i)

        def backward(n):
            at = slice(n * TF, (n + 1) * TF)
            grad_inner = dot(gprod_ref[i], down_ref[i, at, :], 1, 1)
            gate_pre, up_pre = gate_pre_ref[:, at], up_pre_ref[:, at]
            sigmoid = jax.nn.sigmoid(gate_pre)
            dgate = grad_inner * up_pre * sigmoid * (1.0 + gate_pre * (1.0 - sigmoid))
            dgate_ref[i, :, at] = dgate.astype(BF16)
            dup_ref[i, :, at] = (grad_inner * (gate_pre * sigmoid)).astype(BF16)

        for n in range(width // TF):
            backward(n)
        save(3, i)
        save(4, i)

        def to_rows(n):
            at = slice(n * TD, (n + 1) * TD)
            back = dot(dgate_ref[i], gate_ref[i, at, :], 1, 1)
            back = back + dot(dup_ref[i], up_ref[i, at, :], 1, 1)
            back_ref[i + shift, :, at] = back.astype(BF16)

        for n in range(MODEL_WIDTH // TD):
            to_rows(n)

    each(n_experts, expert)
    def storing(i):
        source = made_ref.at[i] if emit else (scaled_ref, back_ref, gate_grad_ref)[i].at[0]
        return pltpu.make_async_copy(source, made_hbm[i], out_sem.at[i])

    if not emit:
        for i in range(3):
            storing(i).start()
    else:
        if prior:
            for i in prior_in:
                arrivals[i]().wait()
        table_rows = x_ref.shape[1] - tokens_here
        tall = tokens_here + table_rows
        shape = (table_rows, MODEL_WIDTH)

        def scatter(b):
            row_index = lax.broadcasted_iota(jnp.int32, shape, 0)
            lane_group = lax.broadcasted_iota(jnp.int32, shape, 1) // tokens_here
            slots = pl.ds(pl.multiple_of(b * capacity, capacity), capacity)
            pick = pick_ref[b]

            def spread(n):
                at = slice(n * TD, (n + 1) * TD)
                made = jnp.concatenate([back_ref[0, slots, at], back_ref[1, slots, at]], axis=0)
                made_ref[b, :tokens_here, at] = dot(pick, made, 0, 0).astype(BF16)
                made = jnp.concatenate([scaled_ref[0, slots, at], scaled_ref[1, slots, at]], axis=0)
                made_ref[b, tall:, at] = dot(pick, made, 0, 0).astype(BF16)

            for n in range(MODEL_WIDTH // TD):
                spread(n)
            table = jnp.zeros(shape, F32)
            for e in range(2):
                table_row, group = place(ids[e])
                picked = pick[e * capacity : (e + 1) * capacity].astype(F32)
                line = jnp.sum(picked * gate_grad_ref[e, slots, :1], axis=0, keepdims=True)
                coarse = line.astype(BF16).astype(F32)
                here = lane_group == group
                for first, part in ((0, coarse), (per, line - coarse)):
                    wide = jnp.concatenate([part] * groups, axis=1)
                    table = table + jnp.where(here & (row_index == table_row + first), wide, 0.0)
            made_ref[b, tokens_here:tall, :] = table.astype(BF16)
            for turn in range(n_blocks):
                pl.when(b == turn)(lambda turn=turn: storing(turn).start())

        each(n_blocks, scatter)
    for turn in range(n_experts):
        for which in range(5):
            saving(which, turn).wait()
    for i in range(len(made_hbm)):
        storing(i).wait()


def run_experts(numbers, x_blocks, g_blocks, weights, experts, saved, first, total, capacity, prior=()):
    tokens_here = g_blocks[0][0].shape[0]
    block_rows = x_blocks[0][0].shape[0]
    width = weights[0].shape[2]
    n_blocks, n_here = len(x_blocks), len(experts)
    rows = n_blocks * capacity
    per = lax.axis_size("row") * tokens_here // MODEL_WIDTH
    emit = bool(prior) or n_here == 2
    sources = tuple(len(v) for v in x_blocks)
    plan = (sources, tuple(experts), first, bool(prior), saved is not None)
    hbm = pl.BlockSpec(memory_space=pltpu.HBM)
    if emit:
        made = [jax.ShapeDtypeStruct((tokens_here + block_rows, MODEL_WIDTH), BF16)] * n_blocks
    else:
        made = [jax.ShapeDtypeStruct((rows, MODEL_WIDTH), BF16)] * 2
        made.append(jax.ShapeDtypeStruct((rows, 128), F32))
    kept = [jax.ShapeDtypeStruct((2, total, MODEL_WIDTH), BF16)] * 2
    kept += [jax.ShapeDtypeStruct((2, total, width), BF16)] * 3
    operands = [w for v in (*x_blocks, *g_blocks) for w in v]
    for e in experts:
        operands += weights[3:] if e else weights[:3]
    operands += prior
    handed = 1 + len(operands)
    aliases = {}
    if saved is not None:
        operands += saved
        aliases = {handed + i: len(made) + i for i in range(5)}
    results = pl.pallas_call(
        functools.partial(experts_kernel, tokens_here, capacity, per, plan),
        out_shape=made + kept,
        in_specs=[pl.BlockSpec(memory_space=pltpu.SMEM)] + [hbm] * len(operands),
        out_specs=[hbm] * (len(made) + 5),
        scratch_shapes=[
            pltpu.VMEM((n_blocks, block_rows, MODEL_WIDTH), BF16),
            pltpu.VMEM((n_blocks, tokens_here, MODEL_WIDTH), BF16),
        ]
        + [pltpu.VMEM((n_here, *v.shape[1:]), BF16) for v in weights[:3]]
        + [pltpu.VMEM((n_blocks, *made[0].shape) if emit else (16, 128), BF16)]
        + [pltpu.VMEM((n_here, rows, MODEL_WIDTH), BF16)] * 2
        + [pltpu.VMEM((n_here, rows, width), BF16)] * 3
        + [
            pltpu.VMEM((n_blocks, (2 if emit else 1) * capacity, tokens_here), BF16),
            pltpu.VMEM((n_here, rows, MODEL_WIDTH), BF16),
            pltpu.VMEM((rows, width), F32),
            pltpu.VMEM((rows, width), F32),
            pltpu.VMEM((n_here, rows, 128), F32),
            pltpu.VMEM((2 if emit else 1, rows, MODEL_WIDTH), BF16),
            pltpu.VMEM((2 if emit else 1, rows, MODEL_WIDTH), BF16),
            pltpu.VMEM((2 if emit else 1, rows, 128), F32),
            pltpu.SemaphoreType.DMA((2 * n_blocks + 14,)),
            pltpu.SemaphoreType.DMA((len(made),)),
            pltpu.SemaphoreType.DMA((5, n_here)),
        ],
        input_output_aliases=aliases,
        compiler_params=pltpu.CompilerParams(vmem_limit_bytes=VMEM_ALL),
        cost_estimate=pl.CostEstimate(flops=1000, bytes_accessed=1000, transcendentals=0),
        name="experts",
    )(numbers, *operands)
    return list(results[: len(made)]), list(results[len(made) :])


def swap_halves(values):
    width = values.shape[1]
    half = HEAD_SIZE // 2
    lane = lax.broadcasted_iota(jnp.int32, values.shape, 1)
    return jnp.where(
        lane % HEAD_SIZE < half,
        pltpu.roll(values, width - half, 1),
        pltpu.roll(values, half, 1),
    )


def turn(values, cosine, sine_part):
    times = values.shape[1] // cosine.shape[1]
    wide = [jnp.concatenate([v] * times, axis=1) for v in (cosine, sine_part)]
    return values * wide[0] + swap_halves(values) * wide[1]


def rms_factor(values):
    return lax.rsqrt(jnp.mean(values * values, axis=-1, keepdims=True) + EPSILON)


def block_bias(seg_col_ref, seg_row_ref, first, rows, keys):
    queries = lax.broadcasted_iota(jnp.int32, (rows, keys), 0) + first
    at = lax.broadcasted_iota(jnp.int32, (rows, keys), 1)
    same = seg_col_ref[first : first + rows, :] == seg_row_ref[:, :keys]
    return jnp.where(same & (at <= queries), 0.0, -1e30)


def head_lanes(number):
    return slice(number * HEAD_SIZE, (number + 1) * HEAD_SIZE)


def attend_kernel(n_head, head_ref, *refs):
    token_refs = refs[:n_head]
    seg_col, seg_row, gain, w_q, w_k, w_v, w_o, cos_ref, sin_ref = refs[n_head : n_head + 9]
    normed_ref, q_ref, k_ref, v_ref, mixed_ref, lse_ref, own_ref, other_ref = refs[n_head + 9 : n_head + 17]
    part_ref, bias_ref = refs[n_head + 17 :]
    rows = token_refs[0].shape[0]
    head_at = head_ref[0]
    scale = HEAD_SIZE ** (-0.5)
    for k in range(n_head):
        x = token_refs[k][...].astype(F32)
        at = pl.ds(pl.multiple_of((head_at ^ k) * rows, rows), rows)
        normed_ref[at, :] = (x * rms_factor(x) * gain[...]).astype(BF16)
    normed = normed_ref[...]
    cosine, sine_part = cos_ref[...], sin_ref[...]
    q_ref[...] = (turn(dot(normed, w_q[...], 1, 0), cosine, sine_part).astype(BF16) * scale).astype(BF16)
    k_ref[...] = turn(dot(normed, w_k[...], 1, 0), cosine, sine_part).astype(BF16)
    v_ref[...] = dot(normed, w_v[...], 1, 0).astype(BF16)
    kv = k_ref.shape[1] // HEAD_SIZE
    per_group = q_ref.shape[1] // k_ref.shape[1]
    lane = lax.broadcasted_iota(jnp.int32, (rows, lse_ref.shape[1]), 1)
    wide_q, wide_k = 2 * per_group * HEAD_SIZE, 2 * HEAD_SIZE
    for i in range(n_head):
        first, keys = i * rows, (i + 1) * rows
        bias_ref[:, :keys] = block_bias(seg_col, seg_row, first, rows, keys)
        lse_ref[first:keys, :] = jnp.zeros((rows, lse_ref.shape[1]), F32)

        def pair(jj, first=first, keys=keys):
            q_at = pl.ds(pl.multiple_of(jj * wide_q, wide_q), wide_q)
            k_at = pl.ds(pl.multiple_of(jj * wide_k, wide_k), wide_k)
            query_all, key_all, value_all = q_ref[first:keys, q_at], k_ref[:keys, k_at], v_ref[:keys, k_at]
            made = []
            log_totals = lse_ref[first:keys, :]
            for h in range(2 * per_group):
                j = h // per_group
                key, value = key_all[:, head_lanes(j)], value_all[:, head_lanes(j)]
                scores = dot(query_all[:, head_lanes(h)], key, 1, 1) + bias_ref[:, :keys]
                highest = jnp.max(scores, axis=1, keepdims=True)
                exponent = jnp.exp(scores - highest)
                total = jnp.sum(exponent, axis=1, keepdims=True)
                log_totals = jnp.where(
                    lane == jj * (2 * per_group) + h, highest + jnp.log(total), log_totals
                )
                probs = (exponent * (1.0 / total)).astype(BF16)
                made.append(dot(probs, value, 1, 0).astype(BF16))
            mixed_ref[first:keys, q_at] = jnp.concatenate(made, axis=1)
            lse_ref[first:keys, :] = log_totals

        each(kv // 2, pair)
    part_ref[...] = dot(mixed_ref[...], w_o[...], 1, 0)
    own_ref[...] = part_ref[pl.ds(pl.multiple_of(head_at * rows, rows), rows), :]
    for k in range(1, n_head):
        at = pl.ds(pl.multiple_of((head_at ^ k) * rows, rows), rows)
        other_ref[k - 1] = part_ref[at, :].astype(BF16)


def attend_back_kernel(n_head, head_ref, *refs):
    token_refs, refs = refs[:n_head], refs[n_head:]
    grad_refs = refs[:n_head]
    seg_col, seg_row, w_q, w_k, w_v, w_o, cos_ref, sin_ref = refs[n_head : n_head + 8]
    q_ref, k_ref, v_ref, lse_ref = refs[n_head + 8 : n_head + 12]
    full_ref, proj_ref, own_ref, other_ref, gain_ref = refs[n_head + 12 : n_head + 17]
    gm_ref, dq_ref, dk_ref, dv_ref, part_ref, bias_ref = refs[n_head + 17 :]
    rows = grad_refs[0].shape[0]
    head_at = head_ref[0]
    scale = HEAD_SIZE ** (-0.5)
    for k in range(n_head):
        at = pl.ds(pl.multiple_of((head_at ^ k) * rows, rows), rows)
        full_ref[at, :] = grad_refs[k][...]
    gm_ref[...] = dot(full_ref[...], w_o[...], 1, 1).astype(BF16)
    cosine, sine_part = cos_ref[...], -sin_ref[...]
    kv = k_ref.shape[1] // HEAD_SIZE
    per_group = q_ref.shape[1] // k_ref.shape[1]
    dk_ref[...] = jnp.zeros(dk_ref.shape, F32)
    dv_ref[...] = jnp.zeros(dv_ref.shape, F32)
    lane = lax.broadcasted_iota(jnp.int32, (rows, lse_ref.shape[1]), 1)
    wide_q, wide_k = 2 * per_group * HEAD_SIZE, 2 * HEAD_SIZE
    for i in range(n_head):
        first, keys = i * rows, (i + 1) * rows
        bias_ref[:, :keys] = block_bias(seg_col, seg_row, first, rows, keys)

        def pair(jj, first=first, keys=keys):
            q_at = pl.ds(pl.multiple_of(jj * wide_q, wide_q), wide_q)
            k_at = pl.ds(pl.multiple_of(jj * wide_k, wide_k), wide_k)
            query_all, grad_all = q_ref[first:keys, q_at], gm_ref[first:keys, q_at]
            key_all, value_all = k_ref[:keys, k_at], v_ref[:keys, k_at]
            log_totals = lse_ref[first:keys, :]
            made, dk_all, dv_all = [], [], []
            for j in range(2):
                key, value = key_all[:, head_lanes(j)], value_all[:, head_lanes(j)]
                dk, dv = 0.0, 0.0
                for h in range(j * per_group, (j + 1) * per_group):
                    query, grad = query_all[:, head_lanes(h)], grad_all[:, head_lanes(h)]
                    mine = jnp.where(lane == jj * (2 * per_group) + h, log_totals, 0.0)
                    log_total = jnp.sum(mine, axis=1, keepdims=True)
                    probs = jnp.exp(dot(query, key, 1, 1) + bias_ref[:, :keys] - log_total)
                    grad_probs = dot(grad, value, 1, 1)
                    middle = jnp.sum(probs * grad_probs, axis=1, keepdims=True)
                    ds = (probs * (grad_probs - middle)).astype(BF16)
                    made.append(dot(ds, key, 1, 0) * scale)
                    dk = dk + dot(query, ds, 0, 0)
                    dv = dv + dot(grad, probs.astype(BF16), 0, 0)
                dk_all.append(dk)
                dv_all.append(dv)
            dq_ref[first:keys, q_at] = jnp.concatenate(made, axis=1)
            dk_ref[k_at, :keys] += jnp.concatenate(dk_all, axis=0)
            dv_ref[k_at, :keys] += jnp.concatenate(dv_all, axis=0)

        each(kv // 2, pair)
    width_q, width_k = q_ref.shape[1], k_ref.shape[1]
    proj_ref[:, :width_q] = turn(dq_ref[...], cosine, sine_part).astype(BF16)
    proj_ref[:, width_q : width_q + width_k] = turn(dk_ref[...].T, cosine, sine_part).astype(BF16)
    proj_ref[:, width_q + width_k :] = dv_ref[...].T.astype(BF16)
    part_ref[...] = (
        dot(proj_ref[:, :width_q], w_q[...], 1, 1)
        + dot(proj_ref[:, width_q : width_q + width_k], w_k[...], 1, 1)
        + dot(proj_ref[:, width_q + width_k :], w_v[...], 1, 1)
    )
    gain = jnp.zeros(gain_ref.shape, F32)
    for k in range(n_head):
        part = part_ref[pl.ds(pl.multiple_of((head_at ^ k) * rows, rows), rows), :]
        x = token_refs[k][...].astype(F32)
        gain = gain + jnp.sum(part * (x * rms_factor(x)), axis=0, keepdims=True)
        if k:
            other_ref[k - 1] = part.astype(BF16)
        else:
            own_ref[...] = part
    gain_ref[...] = gain


def weight_grads(share, core, normed_ref, proj_ref, full_ref, mixed_ref, own_ref, other_ref, all_ref):
    width = proj_ref.shape[1]
    all_ref[:, :width] = dot(normed_ref[...], proj_ref[...], 0, 0)
    all_ref[:, width:] = dot(full_ref[...], mixed_ref[...], 0, 0)
    for m in range(own_ref.shape[0] // share):
        at = slice(m * share, (m + 1) * share)
        own = pl.ds(pl.multiple_of((2 * m + core) * share, share), share)
        other = pl.ds(pl.multiple_of((2 * m + 1 - core) * share, share), share)
        own_ref[at, :] = all_ref[own, :]
        other_ref[at, :] = all_ref[other, :].astype(BF16)


def attend_back_all_kernel(n_head, share, head_ref, *refs):
    n_in = 2 * n_head + 12
    normed_ref, mixed_ref = refs[n_in : n_in + 2]
    own_ref, other_ref, gain_ref, weights_own_ref, weights_other_ref = refs[n_in + 2 : n_in + 7]
    full_ref, proj_ref, *work, all_ref = refs[n_in + 7 :]
    attend_back_kernel(
        n_head, head_ref, *refs[:n_in], full_ref, proj_ref, own_ref, other_ref, gain_ref, *work
    )
    weight_grads(
        share, head_ref[1], normed_ref, proj_ref, full_ref, mixed_ref,
        weights_own_ref, weights_other_ref, all_ref,
    )


def expert_grads_kernel(n_head, axis, heads_first, head_ref, lhs_ref, rhs_ref, *refs):
    head_at = head_ref[0]
    own_ref, rest_ref, away_ref, all_ref = refs
    size = own_ref.shape[axis]

    def part(k):
        at = pl.ds(pl.multiple_of((head_at ^ k) * size, size), size)
        return all_ref[at, :] if axis == 0 else all_ref[:, at]

    def first():
        own_ref[...] = part(0)
        for k in range(1, n_head):
            if heads_first:
                away_ref[k - 1, 0] = part(k).astype(BF16)
            else:
                rest_ref[k - 1] = part(k)

    def second():
        for k in range(n_head):
            if not heads_first:
                away_ref[k] = part(k).astype(BF16)
            elif k:
                away_ref[k - 1, 1] = part(k).astype(BF16)
            else:
                rest_ref[0] = part(0)

    def turn(e):
        all_ref[...] = dot(lhs_ref[e], rhs_ref[e], 0, 0)
        pl.when(e == 0)(first)
        pl.when(e == 1)(second)

    each(2, turn)


def final_kernel(n_head, tokens_ref, grad_hidden_ref, gain, own_ref, *refs):
    total = own_ref[...]
    for part in refs[: n_head - 1]:
        total = total + part[...].astype(F32)
    x = tokens_ref[...].astype(F32)
    factor = rms_factor(x)
    weighted = total * gain[...]
    middle = jnp.mean(weighted * x, axis=-1, keepdims=True)
    refs[-1][...] = grad_hidden_ref[...] + factor * (weighted - x * factor * factor * middle)


def hidden_kernel(n_head, tokens_ref, own_ref, *refs):
    arrived = refs[: n_head - 1]
    gain, router_t, slots_ref, chosen_ref = refs[n_head - 1 : n_head + 3]
    block_ref, hidden_ref, gates_ref = refs[n_head + 3 :]
    rows = tokens_ref.shape[0]
    attention = own_ref[...]
    for part in arrived:
        attention = attention + part[...].astype(F32)
    hidden = tokens_ref[...].astype(F32) + attention
    hidden_ref[...] = hidden
    normed = (hidden * rms_factor(hidden) * gain[...]).astype(BF16)
    block_ref[:rows, :] = normed
    chosen = chosen_ref[...] > 0.0
    logits = jnp.where(chosen, dot(router_t[...], normed, 1, 1), -1e30)
    gates = jnp.where(chosen, jnp.exp(logits - jnp.max(logits, axis=0, keepdims=True)), 0.0)
    gates = gates / jnp.sum(gates, axis=0, keepdims=True)
    gates_ref[...] = gates
    coarse = gates.astype(BF16).astype(F32)
    groups = MODEL_WIDTH // rows
    per = gates.shape[0] // groups
    lines = [
        jnp.concatenate([v[q * per : (q + 1) * per] for q in range(groups)], axis=1)
        for v in (coarse, gates - coarse, slots_ref[...])
    ]
    spare = block_ref.shape[0] - rows - 3 * per
    if spare:
        lines.append(jnp.zeros((spare, MODEL_WIDTH), F32))
    block_ref[rows:, :] = jnp.concatenate(lines, axis=0).astype(BF16)


def grad_hidden_kernel(n_parts, *refs):
    parts = refs[:n_parts]
    hidden_ref, gain, router_t, gates_ref, block_ref, cotangent_ref = refs[n_parts : n_parts + 6]
    grad_ref, low_ref, small_ref = refs[n_parts + 6 :]
    rows = hidden_ref.shape[0]
    tall = block_ref.shape[0]
    total = parts[0][:tall, :].astype(F32)
    for part in parts[1:]:
        total = total + part[:tall, :].astype(F32)
    gates = gates_ref[...]
    groups = MODEL_WIDTH // rows
    per = gates.shape[0] // groups
    lines = total[rows : rows + per] + total[rows + per : rows + 2 * per]
    grad_gates = jnp.concatenate(
        [lines[:, q * rows : (q + 1) * rows] for q in range(groups)], axis=0
    )
    grad_logits = gates * (grad_gates - jnp.sum(gates * grad_gates, axis=0, keepdims=True))
    coarse = grad_logits.astype(BF16)
    fine = (grad_logits - coarse.astype(F32)).astype(BF16)
    normed = block_ref[:rows, :]
    n_experts = gates.shape[0]
    small_ref[:n_experts, :] = dot(coarse, normed, 1, 0) + dot(fine, normed, 1, 0)
    upstream = total[:rows] + dot(coarse, router_t[...], 0, 0) + dot(fine, router_t[...], 0, 0)
    hidden = hidden_ref[...]
    factor = rms_factor(hidden)
    weighted = upstream * gain[...]
    middle = jnp.mean(weighted * hidden, axis=-1, keepdims=True)
    grad = cotangent_ref[...].astype(F32) + factor * (weighted - hidden * factor * factor * middle)
    grad_ref[...] = grad
    low_ref[...] = grad.astype(BF16)
    small_ref[n_experts:, :] = jnp.sum(upstream * hidden * factor, axis=0, keepdims=True)


def call(kernel, name, operands, out_shape, scratch_shapes=(), scalars=0, room=VMEM_BYTES):
    vmem = pl.BlockSpec(memory_space=pltpu.VMEM)
    smem = pl.BlockSpec(memory_space=pltpu.SMEM)
    made = pl.pallas_call(
        kernel,
        out_shape=out_shape,
        in_specs=[smem] * scalars + [vmem] * (len(operands) - scalars),
        out_specs=[vmem] * len(out_shape),
        scratch_shapes=list(scratch_shapes),
        compiler_params=pltpu.CompilerParams(vmem_limit_bytes=room),
        cost_estimate=pl.CostEstimate(flops=1000, bytes_accessed=1000, transcendentals=0),
        name=name,
    )(*operands)
    return list(made)


def local(
    tokens,
    segments,
    routes,
    norm_gain,
    w_query,
    key_weight,
    value_weight,
    w_output,
    moe_gain,
    w_router,
    w_gate,
    w_up,
    w_down,
    cotangent,
):
    local_rows = tokens.shape[0]
    length = segments.shape[0]
    n_experts = w_router.shape[1]
    capacity = local_rows * TOPK * 5 // (4 * n_experts)
    width_query = w_query.shape[1]
    width_key = key_weight.shape[1]
    n_row = lax.axis_size("row")
    n_head = lax.axis_size("head")
    n_outer = n_row // 4
    row_at = lax.axis_index("row")
    head_at = lax.axis_index("head")
    at_end = (row_at // 4 % 3 == 0).astype(jnp.int32)
    numbers = jnp.stack([row_at, head_at & 1, at_end]).astype(jnp.int32)

    routes_t = routes.T
    expert_index = jnp.arange(n_experts, dtype=jnp.int32)[:, None]
    chosen = jnp.any(routes_t[:, None, :] == expert_index[None], axis=0)
    t_index = jnp.arange(local_rows, dtype=jnp.int32)
    before = (t_index[:, None] < t_index[None, :]).astype(BF16)
    rank = dot(chosen.astype(BF16), before, 1, 0)
    slots = jnp.where(chosen & (rank < capacity), rank, -1.0)
    chosen = chosen.astype(F32)
    router_t = w_router.T
    head_number = head_at.astype(jnp.int32).reshape(1)

    line = n_outer == 4
    inner = [(i, i ^ 12) for i in range(4, 12)]
    outward = [(i, i ^ 4) for i in range(4, 12)]
    ends = [*range(4), *range(12, 16)]
    ends_in = [(i, i ^ 8) for i in ends]
    ends_over = [(i, i ^ 12) for i in ends]
    inner_out = [(i, i ^ 8) for i in range(4, 12)]

    def send(value, pairs):
        return lax.ppermute(value, "row", pairs)

    def share_of(weight):
        size = weight.shape[1] // 2
        return lax.dynamic_slice_in_dim(weight[0], (head_at & 1) * size, size, 0)

    def head_all(values):
        return [head_swap(values[k - 1], k) for k in range(1, n_head)]

    def low(value):
        return value.astype(BF16)

    def shape(rows, columns, dtype=BF16):
        return jax.ShapeDtypeStruct((rows, columns), dtype)

    seg_col, seg_row = segments[:, None], segments[None, :]
    gain_row, moe_gain_row = norm_gain[None], moe_gain[None]

    tokens_other = head_all([tokens] * (n_head - 1))
    frequency = ROPE_BASE ** (-2.0 * jnp.arange(HEAD_SIZE // 2, dtype=F32) / HEAD_SIZE)
    angles = jnp.arange(length, dtype=F32)[:, None] * frequency[None, :]
    cosine, sine_part = jnp.cos(angles), jnp.sin(angles)
    cosine = jnp.concatenate([cosine] * 4, axis=1)
    sine_part = jnp.concatenate([-sine_part, sine_part] * 2, axis=1)
    gate_share, down_share = share_of(w_gate), share_of(w_down)
    width = gate_share.shape[1]
    pieces = [down_share[:, k : k + width] for k in range(0, down_share.shape[1], width)]
    gate_here = row_swap(gate_share, 2)
    down_here = row_swap(jnp.concatenate(pieces, axis=0), 2)
    if line:
        g_far = [row_swap(cotangent, 4), send(cotangent, inner)]
    else:
        g_far = [row_swap(cotangent, 4 * o) for o in range(1, n_outer)]
    tokens_other, cosine, sine_part, seg_col, slots, chosen = tie(
        tokens_other, cosine, sine_part, seg_col, slots, chosen
    )
    g_far, w_up_later, _ = tie(g_far, w_up, seg_col)

    g_slabs = [cotangent, *g_far]
    if line:
        g_far += [send(g_far[1], outward), send(g_far[0], inner)]
    head_parts = [
        shape(local_rows, MODEL_WIDTH, F32),
        jax.ShapeDtypeStruct((n_head - 1, local_rows, MODEL_WIDTH), BF16),
    ]
    normed_full, queries, keys, values, mixed_heads, log_totals, part_own, part_other = call(
        functools.partial(attend_kernel, n_head),
        "attend",
        [head_number, tokens, *tokens_other, seg_col, seg_row, gain_row]
        + [w_query, key_weight, value_weight, w_output, cosine, sine_part],
        [shape(length, MODEL_WIDTH), shape(length, width_query)]
        + [shape(length, width_key)] * 2
        + [shape(length, width_query), shape(length, 128, F32), *head_parts],
        [pltpu.VMEM((length, MODEL_WIDTH), F32), pltpu.VMEM((local_rows, length), F32)],
        scalars=1,
        room=VMEM_ALL,
    )
    part_other, part_own, gate_here, down_here, g_far, w_up_later = tie(
        part_other, part_own, gate_here, down_here, g_far, w_up_later
    )

    arrived = head_all(part_other)
    up_here = row_swap(w_up_later, 2)
    g_last = send(g_far[3], outward) if line else cotangent
    arrived, part_own, g_last = tie(arrived, part_own, g_last)
    table_rows = -(-3 * n_experts * local_rows // MODEL_WIDTH // 16) * 16
    x_block, hidden, gates = call(
        functools.partial(hidden_kernel, n_head),
        "hidden",
        [tokens, part_own, *arrived, moe_gain_row, router_t, slots, chosen],
        [
            shape(local_rows + table_rows, MODEL_WIDTH),
            shape(local_rows, MODEL_WIDTH, F32),
            shape(n_experts, local_rows, F32),
        ],
    )
    tall = x_block.shape[0]
    saved = None
    made = []

    def cores(values):
        return [row_swap(v, 1) for v in values]

    def pass_on(chunk):
        made[chunk][1] = row_swap(made[chunk][1], 1)

    def near(which, chunk):
        own, other = (v[:tall] if which else v[tall:] for v in made[chunk])
        return own.astype(F32) + other.astype(F32)

    def experts(x_blocks, g_blocks, which, prior=()):
        nonlocal saved
        first = 2 * len(made) * capacity
        results, saved = run_experts(
            numbers, x_blocks, g_blocks, weights, which, saved, first, total_rows, capacity, prior
        )
        if which == (0,):
            return results
        made.extend(results[i : i + 2] for i in range(0, len(results), 2))

    total_rows = 2 * n_outer * capacity
    gate_there = head_swap(gate_here, 1)
    x_core = row_swap(x_block, 1)
    if line:
        x_far = [row_swap(x_block, 4), send(x_block, inner)]
    else:
        x_far = [row_swap(x_block, 4 * o) for o in range(1, n_outer)]
    x_block, x_core, x_far, up_here, gate_there, down_later, g_slabs, g_far, g_last, cotangent = tie(
        x_block, x_core, x_far, up_here, gate_there, down_here, g_slabs, g_far, g_last, cotangent
    )
    down_there = head_swap(down_later, 1)
    weights = [w_gate, w_up, w_down, gate_here, gate_there, down_here, down_there, up_here]

    if line:
        x_near, x_mid = x_far
        x_near_core = row_swap(x_near, 1)
        g_cores = cores(g_slabs[:2])
        x_near, x_mid, x_near_core, g_cores, g_far = tie(x_near, x_mid, x_near_core, g_cores, g_far)
        x_out, x_deep = send(x_mid, outward), send(x_near, inner)
        x_pairs = [[x_block], [x_core], [x_near], [x_near_core]]
        g_pairs = [[cotangent], [g_cores[0]], [g_slabs[1]], [g_cores[1]]]
        prior = experts(x_pairs, g_pairs, (0,))
        x_out, x_deep, prior, saved, down_there, g_far, x_mid, g_mid, g_last = tie(
            x_out, x_deep, prior, saved, down_there, g_far, x_mid, g_slabs[2], g_last
        )
        weights[6] = down_there
        x_last = send(x_deep, outward)
        x_mid_core, g_mid_core, g_out_core = cores([x_mid, g_mid, g_far[2]])
        experts(x_pairs, g_pairs, (1,), prior)
        x_last, x_mid_core, g_mid_core, g_out_core, made[0], made[1], saved, x_out = tie(
            x_last, x_mid_core, g_mid_core, g_out_core, made[0], made[1], saved, x_out
        )
        x_out_core = row_swap(x_out, 1)
        x_out_core, x_last, x_deep, g_deep, g_last, made[0] = tie(
            x_out_core, x_last, x_deep, g_far[3], g_last, made[0]
        )
        pass_on(1)
        x_deep_core, x_last_core, g_deep_core, g_last_core = cores([x_deep, x_last, g_deep, g_last])
        g_two = [[g_mid, g_far[2]], [g_mid_core, g_out_core]]
        experts([[x_mid, x_out], [x_mid_core, x_out_core]], g_two, (0, 1))
        x_deep_core, x_last_core, g_deep_core, g_last_core, made[0], made[1], made[2], saved = tie(
            x_deep_core, x_last_core, g_deep_core, g_last_core, made[0], made[1], made[2], saved
        )
        pass_on(2)
        made[0], made[1], made[2], x_deep, x_last = tie(made[0], made[1], made[2], x_deep, x_last)
        g_three = [[g_deep, g_last], [g_deep_core, g_last_core]]
        two, sum_one = low(near(1, 2)), low(near(1, 1))
        first_sums = [send(two, ends_in), send(two, inner), row_swap(sum_one, 4)]
        x_deep, x_last, _, _ = tie(x_deep, x_last, two, sum_one)
        experts([[x_deep, x_last], [x_deep_core, x_last_core]], g_three, (0, 1))
    else:
        for o, x in enumerate([x_block, *x_far]):
            experts([[x], [row_swap(x, 1)]], [[g_slabs[o]], [row_swap(g_slabs[o], 1)]], (0, 1))
        for o in range(n_outer):
            pass_on(o)
        one = [row_swap(low(near(1, o)), 4 * o) for o in range(1, n_outer)]

    rows_in, gprod, inner_act, dgate, dup = saved

    def expert_grads(lhs, rhs, axis, heads_first):
        sizes = [lhs.shape[2], rhs.shape[2]]
        part = list(sizes)
        part[axis] //= n_head
        rest = (1, *part) if heads_first else (n_head - 1, *part)
        away = (n_head - 1, 2, *part) if heads_first else (n_head, *part)
        return call(
            functools.partial(expert_grads_kernel, n_head, axis, heads_first),
            "expert_grads",
            [head_number, lhs, rhs],
            [
                jax.ShapeDtypeStruct(tuple(part), F32),
                jax.ShapeDtypeStruct(rest, F32),
                jax.ShapeDtypeStruct(away, BF16),
            ],
            [pltpu.VMEM(tuple(sizes), F32)],
            scalars=1,
        )

    if line:
        made[0], made[3], inner_act, gprod, rows_in, dgate, dup = tie(
            made[0], made[3], inner_act, gprod, rows_in, dgate, dup
        )
    up_parts = expert_grads(rows_in, dup, 0, False)
    down_parts = expert_grads(inner_act, gprod, 1, True)
    up_away, down_away = up_parts[2], down_parts[2]
    if line:
        first_sums, made[0], made[3], up_away, down_away, rows_in, dgate = tie(
            first_sums, made[0], made[3], up_away, down_away, rows_in, dgate
        )
        pass_on(0)
        pass_on(3)
        made[0], made[3], first_sums, up_away, down_away, rows_in, dgate = tie(
            made[0], made[3], first_sums, up_away, down_away, rows_in, dgate
        )
        three = low(near(1, 3))
        last_sums = [send(three, ends_over), send(three, inner_out)]
    up_away = row_swap(up_away, 2)
    down_away = head_all(down_away)
    gate_parts = expert_grads(rows_in, dgate, 0, False)
    gate_away = gate_parts[2]
    if line:
        total = near(1, 0) + sum(v.astype(F32) for v in first_sums)
        made_now, _ = tie(made, three)
        made = list(made_now)
        out_one, out_two, out_three = (low(near(0, o)) for o in range(1, 4))
        one = [total, *last_sums]
    else:
        one = [near(1, 0), *one]
        out_one = out_two = out_three = one[0]
    one, up_away, down_away, gate_away, made_now, out_one, out_two, out_three = tie(
        one, up_away, down_away, gate_away, made, out_one, out_two, out_three
    )
    made = list(made_now)
    grad_sum = one
    grad_hidden, grad_attention, early = call(
        functools.partial(grad_hidden_kernel, len(grad_sum)),
        "grad_hidden",
        [*grad_sum, hidden, moe_gain_row, router_t, gates, x_block, cotangent],
        [
            shape(local_rows, MODEL_WIDTH, F32),
            shape(local_rows, MODEL_WIDTH),
            shape(n_experts + 1, MODEL_WIDTH, F32),
        ],
    )
    made_now, up_away, down_away, gate_away, grad_attention = tie(
        made, up_away, down_away, gate_away, grad_attention
    )
    made = list(made_now)
    grad_arrived = head_all([grad_attention] * (n_head - 1))
    gate_away = row_swap(gate_away, 2)
    out_first = [send(out_two, ends_in)] if line else [out_two]
    up_rest = [low(v + w.astype(F32)) for v, w in zip(up_parts[1], up_away[1:])]
    down_rest = low(down_parts[1][0] + sum(v[1].astype(F32) for v in down_away))
    grad_arrived, up_rest, down_rest, made_now, out_two, out_three, out_first = tie(
        grad_arrived, up_rest, down_rest, made, out_two, out_three, out_first
    )
    made = list(made_now)
    up_last = head_all(up_rest)
    if line:
        out_first += [send(out_three, ends_over), send(out_three, inner_out)]
    else:
        out_first = grad_attention
    share = MODEL_WIDTH // n_row
    width_all = width_query + 2 * width_key
    grad_own, grad_other, gain_part, weights_own, weights_other = call(
        functools.partial(attend_back_all_kernel, n_head, share),
        "attend_back",
        [jnp.stack([head_at, row_at % 2]).astype(jnp.int32), tokens, *tokens_other, grad_attention]
        + [*grad_arrived, seg_col, seg_row, w_query, key_weight, value_weight, w_output]
        + [cosine, sine_part, queries, keys, values, log_totals, normed_full, mixed_heads],
        [
            *head_parts,
            shape(1, MODEL_WIDTH, F32),
            shape(MODEL_WIDTH // 2, width_all + width_query, F32),
            shape(MODEL_WIDTH // 2, width_all + width_query),
        ],
        [
            pltpu.VMEM((length, MODEL_WIDTH), BF16),
            pltpu.VMEM((length, width_all), BF16),
            pltpu.VMEM((length, width_query), BF16),
            pltpu.VMEM((length, width_query), F32),
            pltpu.VMEM((width_key, length), F32),
            pltpu.VMEM((width_key, length), F32),
            pltpu.VMEM((length, MODEL_WIDTH), F32),
            pltpu.VMEM((local_rows, length), F32),
            pltpu.VMEM((MODEL_WIDTH, width_all + width_query), F32),
        ],
        scalars=1,
        room=VMEM_ALL,
    )
    grad_other, gain_part, weights_own, weights_other, up_last, gate_away, down_rest, *outs = tie(
        grad_other, gain_part, weights_own, weights_other, up_last, gate_away, down_rest,
        out_one, out_two,
    )
    out_one, out_two = outs
    small = jnp.concatenate([early, gain_part], axis=0)
    small, weights_own, weights_other, made_now, out_first, out_one, out_two = tie(
        small, weights_own, weights_other, made, out_first, out_one, out_two
    )
    made = list(made_now)
    small_core = row_swap(small, 1)
    weights_core = row_swap(weights_other, 1)
    small, small_core, weights_own, weights_core = tie(small, small_core, weights_own, weights_core)
    small = small + small_core
    small_far = row_swap(small, 2)
    if line:
        out_first = [*out_first, send(out_two, inner), row_swap(out_one, 4)]
    else:
        out_first = small
    value = (weights_own + weights_core.astype(F32)).reshape(n_outer, 2, share, -1)
    bit = (row_at // 2) % 2
    other = low(lax.dynamic_index_in_dim(value, 1 - bit, 1, keepdims=False))
    value = lax.dynamic_index_in_dim(value, bit, 1, keepdims=False)
    small, other, value, grad_other, down_rest, gate_away, made_now, out_two = tie(
        small + small_far, other, value, grad_other, down_rest, gate_away, made, out_two
    )
    made = list(made_now)
    other_arrived = row_swap(other, 2)
    offset = 4
    while offset < n_row:
        small = small + row_swap(small, offset)
        offset *= 2
    offset = 1
    while offset < n_head:
        small = small + head_swap(small, offset)
        offset *= 2
    grad_arrived = head_all(grad_other)
    gate_rest = [low(v + w.astype(F32)) for v, w in zip(gate_parts[1], gate_away[1:])]
    mixed_out = hidden + near(0, 0)
    if line:
        mixed_out = mixed_out + sum(v.astype(F32) for v in out_first)
        last = []
    else:
        last = [row_swap(low(near(0, o)), 4 * o) for o in range(1, n_outer)]
    grad_arrived, value, other_arrived, small, gate_rest, last, mixed_out, down_rest = tie(
        grad_arrived, value, other_arrived, small, gate_rest, last, mixed_out, down_rest
    )
    gate_last = head_all(gate_rest)
    value = value + other_arrived.astype(F32)
    at = row_at // 4
    weights_sum = lax.dynamic_index_in_dim(value, at, 0, keepdims=False)
    weights_parts = [
        row_swap(low(lax.dynamic_index_in_dim(value, at ^ o, 0, keepdims=False)), 4 * o)
        for o in range(1, n_outer)
    ]
    down_last = row_swap(down_rest, 2)
    (grad_tokens,) = call(
        functools.partial(final_kernel, n_head),
        "final",
        [tokens, grad_hidden, gain_row, grad_own, *grad_arrived],
        [shape(local_rows, MODEL_WIDTH, F32)],
    )
    for part in last:
        mixed_out = mixed_out + part.astype(F32)
    mixed_out = mixed_out.astype(BF16)

    def add(own, *parts):
        for part in parts:
            own = own + part.astype(F32)
        return own

    down_sum = add(down_parts[0], *(v[0] for v in down_away), down_last)
    up_sum = add(up_parts[0], up_away[0], *up_last)
    gate_sum = add(gate_parts[0], gate_away[0], *gate_last)
    up_sum, gate_sum, weights_parts = tie(up_sum, gate_sum, weights_parts)
    weights_sum = add(weights_sum, *weights_parts)
    return (
        mixed_out,
        grad_tokens,
        small[n_experts + 1],
        weights_sum[:, :width_query],
        weights_sum[:, width_query : width_query + width_key],
        weights_sum[:, width_query + width_key : width_all],
        weights_sum[:, width_all:].T,
        small[n_experts],
        small[:n_experts].T,
        gate_sum[None],
        up_sum[None],
        down_sum[None],
    )


def solution(mesh):
    in_specs = (
        P(("row", "head"), None),
        P("row"),
        P(("row", "head"), None),
        P(),
        P(None, "head"),
        P(None, "head"),
        P(None, "head"),
        P("head", None),
        P(),
        P(),
        P("row", None, None),
        P("row", None, None),
        P("row", None, None),
        P(("row", "head"), None),
    )
    out_specs = (
        P(("row", "head"), None),
        P(("row", "head"), None),
        P(),
        P("row", "head"),
        P("row", "head"),
        P("row", "head"),
        P("head", "row"),
        P(),
        P(),
        P("row", "head", None),
        P("row", "head", None),
        P("row", None, "head"),
    )
    return jax.shard_map(local, mesh=mesh, in_specs=in_specs, out_specs=out_specs, check_vma=False)
```
